128 devices in a mesh: gx: 32 (over y_lo, x, z), gy: 4 (over y_hi, core).
Axes of the slice: x: 4, y: 4 (y_hi: 2, y_lo: 2; y = y_hi * 2 + y_lo), z: 4, core: 2. Of those that a mesh axis runs over, the one named last changes fastest.
Arguments:
- state: float32 [32, 4, 96, 8, 128], P('gx', 'gy'), may hold values from -4 to 4, as said below
- leaving: int32 [32, 4, 24], P('gx', 'gy'), may hold values from 0 to 95, as said below
- pairs: int32 [32, 4, 2, 576], P('gx', 'gy'), may hold values from 0 to 863, as said below
- counts: int32 [32, 4, 2], P('gx', 'gy'), may hold values from 0 to 576, as said below
- wall_flags: int32 [32, 4, 96, 128], P('gx', 'gy'), may hold values 0 or 1
- cell_index: int32 [32, 4, 96, 128], P('gx', 'gy'), may hold values from 0 to 255
- fluid_temp: float32 [32, 4, 256], P('gx', 'gy'), may hold values from -5 to 5
Outputs:
- moved_state: float32 [32, 4, 96, 8, 128], P('gx', 'gy')
- rates: float32 [32, 4, 96, 4, 128], P('gx', 'gy')
- fluid_terms: float32 [32, 4, 2, 256], P('gx', 'gy')
The draws below stay inside these ranges and needn't reach their ends.
Inputs may be any that keep to these rules, and one draw needn't show every extreme that they name: `leaving`: the 24 slots of one column are distinct. pairs[a, b, 0, k] names an own block; pairs[a, b, 1, k] names a neighbourhood block other than the own block itself. The first counts[a, b, 0] pairs have their partner in the own column (384 to 479), the other listed ones outside it. Slots at or beyond counts[a, b, 1] hold valid indices and are ignored. counts[a, b, 0] <= counts[a, b, 1]; some column lists all 576 pairs. `state`: radii lie in 0.3 to 0.7.
All inputs are finite; a program needn't handle non-finite values. No bound on the sum of `wall_flags` on one device may be relied on, other than what follows from the above.
Results may differ from the reference program's by a relative error of at most 0.0003.
Values sent between devices are 32-bit elements; how exact they have to be, the bound alone decides.
A program may use at most 64 MiB of HBM per device.

```python
import math
import jax
import jax.numpy as jnp
from jax import lax

BS = 128
NB = 96
CELLS = 256
PAIRS = 576
MIG = 24
N_GX = 32
N_GY = 4


def pair_counts(key):
    total = jax.random.randint(jax.random.fold_in(key, 11), (N_GX, N_GY), PAIRS // 4, PAIRS + 1)
    chosen = jax.random.randint(jax.random.fold_in(key, 12), (), 0, N_GX * N_GY)
    places = jnp.arange(N_GX * N_GY).reshape(N_GX, N_GY)
    total = jnp.where(places == chosen, PAIRS, total)
    share = jax.random.randint(jax.random.fold_in(key, 13), (N_GX, N_GY), 1, 4)
    local = total * share // 4
    return (local.astype(jnp.int32), total.astype(jnp.int32))


def draw_counts(key, part):
    local, total = pair_counts(key)
    return jnp.stack([local, total], axis=-1)


def draw_pairs(key, part):
    local, total = pair_counts(key)
    key = jax.random.fold_in(key, 2)
    shape = (N_GX, N_GY, PAIRS)
    own = jax.random.randint(jax.random.fold_in(key, 21), shape, 0, NB)
    step_on = jax.random.randint(jax.random.fold_in(key, 22), shape, 1, NB)
    near = 4 * NB + (own + step_on) % NB
    raw_region = jax.random.randint(jax.random.fold_in(key, 23), shape, 0, 8)
    region = raw_region + (raw_region >= 4).astype(jnp.int32)
    far = region * NB + jax.random.randint(jax.random.fold_in(key, 24), shape, 0, NB)
    place = jnp.arange(PAIRS)[None, None, :]
    partner = jnp.where(place < local[:, :, None], near, far)
    return jnp.stack([own, partner], axis=2).astype(jnp.int32)


def draw_leaving(key, part):
    key = jax.random.fold_in(key, 3)
    keys = jax.random.split(key, N_GX * N_GY)
    chosen = jax.vmap(lambda single: jax.random.permutation(single, NB)[:MIG])(keys)
    return chosen.reshape(N_GX, N_GY, MIG).astype(jnp.int32)


def draw_state(key, part):
    key = jax.random.fold_in(key, 4)
    shape = (N_GX, N_GY, NB, 1, BS)
    pos = 0.5 * jnp.clip(jax.random.normal(jax.random.fold_in(key, 41), (N_GX, N_GY, NB, 3, BS), jnp.float32), -4.0, 4.0)
    vel = jnp.clip(jax.random.normal(jax.random.fold_in(key, 42), (N_GX, N_GY, NB, 3, BS), jnp.float32), -4.0, 4.0)
    temper = jnp.clip(jax.random.normal(jax.random.fold_in(key, 43), shape, jnp.float32), -4.0, 4.0)
    radius = jax.random.uniform(jax.random.fold_in(key, 44), shape, jnp.float32, 0.3, 0.7)
    return jnp.concatenate([pos, vel, temper, radius], axis=3)


def plant(values, stream_key, low, high):
    extent = values.shape
    spot = [jax.random.randint(jax.random.fold_in(stream_key, axis), (), 0, extent[axis]) for axis in range(len(extent))]
    values = values.at[tuple(spot)].set(low)
    longest = extent.index(max(extent))
    spot[longest] = (spot[longest] + 1) % extent[longest]
    return values.at[tuple(spot)].set(high)


def levels(own_key, dims, pieces, smallest, largest):
    level, own = 1.0, jax.random.fold_in(own_key, 6)
    for axis_at, blocks in pieces:
        steps = jnp.exp(jax.random.uniform(jax.random.fold_in(own, axis_at), (blocks,), jnp.float32, smallest / len(pieces), largest / len(pieces)))
        level = level * jnp.repeat(steps, dims[axis_at] // blocks).reshape([-1 if axis == axis_at else 1 for axis in range(len(dims))])
    return level


def normal_values(own_key, shape, width, most, pieces=(), held_as=jnp.bfloat16):
    gain = levels(own_key, shape, pieces, -0.22, 0.18) if pieces else 1.0
    drawn = jax.random.normal(own_key, shape, jnp.float32) * width * gain
    return jnp.minimum(jnp.maximum(drawn, -most), most).astype(held_as)


def setup_inputs(seed: int = 0) -> dict:
    splits = jax.random.split(jax.random.key(seed), 8)
    state = draw_state(jax.random.fold_in(splits[7], 71), 0)
    leaving = draw_leaving(jax.random.fold_in(splits[7], 71), 0)
    pairs = draw_pairs(jax.random.fold_in(splits[7], 71), 0)
    counts = draw_counts(jax.random.fold_in(splits[7], 71), 0)
    wall_flags = plant((jax.random.randint(splits[4], (N_GX, N_GY, NB, BS), 0, 4) < 1).astype(jnp.int32), jax.random.fold_in(splits[4], 1), 0, 1)
    cell_index = plant(jax.random.randint(splits[5], (N_GX, N_GY, NB, BS), 0, CELLS), jax.random.fold_in(splits[5], 1), 0, CELLS - 1).astype(jnp.int32)
    fluid_temp = normal_values(splits[6], (N_GX, N_GY, CELLS), 1.0, 5.0, ((0, 32), (1, 4)), jnp.float32)
    return {"state": state, "leaving": leaving, "pairs": pairs, "counts": counts, "wall_flags": wall_flags, "cell_index": cell_index, "fluid_temp": fluid_temp}


pair_group = 16
soften = 0.01
stiffness = 0.2
damping = 0.05
conductance = 0.05
film_gain = 0.5
wall_gain = 2.0
wall_temp = 1.0
gravity = 1.0
cell_volume = 32.0

def pair_terms(blk_first, blk_second):
    pos_a = blk_first[:, 0:3]
    pos_b = blk_second[:, 0:3]
    delta = pos_a[:, :, :, None] - pos_b[:, :, None, :]
    dist = jnp.sqrt(lax.optimization_barrier(jnp.sum(delta * delta, axis=1)) + soften)
    vrel = blk_first[:, 3:6][:, :, :, None] - blk_second[:, 3:6][:, :, None, :]
    normal_speed = lax.optimization_barrier(jnp.sum(vrel * delta, axis=1)) / dist
    rad_a = blk_first[:, 7][:, :, None]
    rad_b = blk_second[:, 7][:, None, :]
    intersection = jnp.maximum(rad_a + rad_b - dist, 0.0)
    root = jnp.sqrt(intersection)
    weight = (stiffness * intersection * root - damping * root * normal_speed) / dist
    pushed = weight[:, None] * delta
    conduct = conductance * jnp.sqrt(rad_a * rad_b / (rad_a + rad_b) * intersection) * (blk_second[:, 6][:, None, :] - blk_first[:, 6][:, :, None])
    side_first = jnp.concatenate([lax.optimization_barrier(jnp.sum(pushed, axis=3)), lax.optimization_barrier(jnp.sum(conduct, axis=2))[:, None]], axis=1)
    side_second = -jnp.concatenate([lax.optimization_barrier(jnp.sum(pushed, axis=2)), lax.optimization_barrier(jnp.sum(conduct, axis=1))[:, None]], axis=1)
    return (side_first, side_second)

def finish(mine, own, flags, cells, table):
    radius = mine[:, 7]
    temper = mine[:, 6]
    volume = 4.0 / 3.0 * math.pi * radius * radius * radius
    fluid_at = jnp.take(table, cells, axis=0)
    to_fluid = film_gain * radius * radius * (temper - fluid_at)
    to_wall = wall_gain * flags.astype(jnp.float32) * (wall_temp - temper) * radius
    accel = own[:, 0:3] / volume[:, None]
    accel = accel.at[:, 2].add(-gravity)
    heating = (own[:, 3] + to_wall - to_fluid) / volume
    rates = jnp.concatenate([accel, heating[:, None]], axis=1)
    solid = jax.ops.segment_sum(volume.reshape(-1), cells.reshape(-1), table.shape[0]) / cell_volume
    heat = jax.ops.segment_sum(to_fluid.reshape(-1), cells.reshape(-1), table.shape[0])
    return (rates, jnp.stack([solid, heat]))

def reference(state, leaving, pairs, counts, wall_flags, cell_index, fluid_temp):
    gxn, gyn, blocks = (state.shape[0], state.shape[1], state.shape[2])
    flat = state.reshape(gxn * gyn, blocks, 8, BS)
    slots = leaving.reshape(gxn * gyn, -1)
    departing = jax.vmap(lambda src, sl: jnp.take(src, sl, axis=0))(flat, slots)
    departing = jnp.roll(departing.reshape((gxn, gyn) + departing.shape[1:]), 1, axis=0)
    departing = departing.reshape((gxn * gyn,) + departing.shape[2:])
    moved = jax.vmap(lambda src, sl, arr: src.at[sl].set(arr))(flat, slots, departing)
    grid = moved.reshape(gxn, gyn, blocks, 8, BS)
    center = 4 * blocks

    def column(index):
        row_a = index // gyn
        row_b = index % gyn
        regions = [grid[(row_a + off_a) % gxn, (row_b + off_b) % gyn] for off_a in (-1, 0, 1) for off_b in (-1, 0, 1)]
        haloed = jnp.concatenate(regions, axis=0)
        first = pairs[row_a, row_b, 0]
        second = pairs[row_a, row_b, 1]
        total = counts[row_a, row_b, 1]
        groups = first.shape[0] // pair_group

        def turn(acc, step):
            start = (step * pair_group).astype(jnp.int32)
            live = (start + jnp.arange(pair_group).astype(jnp.int32) < total).astype(jnp.float32)
            own_idx = lax.dynamic_slice_in_dim(first, start, pair_group) + center
            far_idx = lax.dynamic_slice_in_dim(second, start, pair_group)
            side_first, side_second = pair_terms(jnp.take(haloed, own_idx, axis=0), jnp.take(haloed, far_idx, axis=0))
            acc = acc.at[own_idx].add(side_first * live[:, None, None])
            acc = acc.at[far_idx].add(side_second * live[:, None, None])
            return (acc, None)
        acc, _ = lax.scan(turn, jnp.zeros((9 * blocks, 4, BS), jnp.float32), jnp.arange(groups).astype(jnp.int32))
        return acc
    accs = lax.map(column, jnp.arange(gxn * gyn).astype(jnp.int32)).reshape(gxn, gyn, 3, 3, blocks, 4, BS)
    own = jnp.zeros((gxn, gyn, blocks, 4, BS), jnp.float32)
    for reg_a in range(3):
        for reg_b in range(3):
            own = own + jnp.roll(accs[:, :, reg_a, reg_b], (reg_a - 1, reg_b - 1), axis=(0, 1))

    def finish_column(mine, contact, flags, cells, table):
        return finish(mine, contact, flags, cells, table)
    rates, fluid = jax.vmap(finish_column)(grid.reshape(gxn * gyn, blocks, 8, BS), own.reshape(gxn * gyn, blocks, 4, BS), wall_flags.reshape(gxn * gyn, blocks, BS), cell_index.reshape(gxn * gyn, blocks, BS), fluid_temp.reshape(gxn * gyn, -1))
    return (grid, rates.reshape(gxn, gyn, blocks, 4, BS), fluid.reshape(gxn, gyn, 2, -1))
```

```python
import functools
import math

import jax
import jax.numpy as jnp
from jax import lax
from jax.experimental import pallas as pl
from jax.experimental.pallas import tpu as pltpu
from jax.sharding import PartitionSpec as P

soften = 0.01
stiffness = 0.2
damping = 0.05
conductance = 0.05
film_gain = 0.5
wall_gain = 2.0
wall_temp = 1.0
gravity = 1.0
cell_volume = 32.0

f32 = jnp.float32
bf16 = jnp.bfloat16
i32 = jnp.int32

tiny = 1e-30
group = 12
lag_a = 2
lag_b = 2
ring = lag_a + lag_b
MESH = pl.DeviceIdType.MESH


def iota(shape, dim):
    return lax.broadcasted_iota(i32, shape, dim)


def split2(value):
    hi = value.astype(bf16).astype(f32)
    return hi, (value - hi).astype(bf16).astype(f32)


def split3(value):
    hi = value.astype(bf16).astype(f32)
    rest = value - hi
    mid = rest.astype(bf16).astype(f32)
    return hi, mid, rest - mid


def dot_tt(left, right):
    return lax.dot_general(left, right, (((1,), (1,)), ((), ())), preferred_element_type=f32)


def neighbours():
    a = lax.axis_index("gx")
    b = lax.axis_index("gy")
    na = lax.axis_size("gx")
    nb = lax.axis_size("gy")
    return (
        {"gx": lax.rem(a + 1, na)},
        {"gx": lax.rem(a + na - 1, na)},
        {"gy": lax.rem(b + 1, nb)},
        {"gy": lax.rem(b + nb - 1, nb)},
    )


def greet(everyone):
    barrier = pltpu.get_barrier_semaphore()
    for device in everyone:
        pl.semaphore_signal(barrier, inc=1, device_id=device, device_id_type=MESH)
    pl.semaphore_wait(barrier, len(everyone))


def sort_pairs(lanes, pad, total):
    own = pad[0:1, :]
    code = pad[1:2, :]
    region = jnp.zeros_like(code)
    for step in range(1, 9):
        region = region + (code >= 96 * step).astype(i32)
    far = code - 96 * region
    live = iota((1, lanes), 1) < total

    def among(*names):
        hit = region == names[0]
        for name in names[1:]:
            hit = hit | (region == name)
        return hit

    kind = jnp.where(among(1, 4, 5), 0, jnp.where(among(0, 3), 1, jnp.where(among(2), 2, 3)))
    kind = jnp.where(live, kind, 4)
    u_far = among(0, 1, 2, 3)
    u = jnp.where(u_far, far, own) + jnp.where(among(4, 5, 3), 0, 96)
    v_slot = jnp.where(u_far, own, far)
    v_side = jnp.where(among(4, 1, 7), 0, jnp.where(among(5, 3, 0, 8), 1, 2))
    ranks = iota((8, lanes), 0)
    marks = (ranks == kind).astype(f32)
    before = (iota((lanes, lanes), 0) < iota((lanes, lanes), 1)).astype(bf16)
    seen = jnp.dot(marks.astype(bf16), before, preferred_element_type=f32)
    starts = jnp.sum((kind < ranks).astype(f32), axis=1, keepdims=True)
    place = jnp.sum(marks * (seen + starts), axis=0, keepdims=True)
    target = (iota((lanes, lanes), 0).astype(f32) == place).astype(bf16)
    rows = iota((8, lanes), 0)
    values = jnp.where(
        rows == 0, u, jnp.where(rows == 1, v_slot, jnp.where(rows == 2, v_side, 0))
    )
    moved = dot_tt(values.astype(bf16), target)
    packed = moved[0:1] + 256.0 * (moved[1:2] + 96.0 * moved[2:3])
    diag = iota((8, 128), 0) == iota((8, 128), 1)
    begin = jnp.sum(jnp.where(diag, starts, 0.0), axis=0, keepdims=True)
    return packed.astype(i32), begin.astype(i32)


def halo_kernel(
    leaving_ref,
    counts_ref,
    pairs_ref,
    state_ref,
    cols_ref,
    lists_ref,
    cat,
    dep,
    moved,
    pad,
    slot_vec,
    slot_smem,
    dep_send,
    dep_recv,
    list_send,
    list_recv,
    col_send,
    col_recv,
    local_sem,
):
    blocks = state_ref.shape[0]
    count = leaving_ref.shape[0]
    ahead, behind, up, down = neighbours()
    for m in range(count):
        dep[m] = state_ref[leaving_ref[m]]
    greet((ahead, behind, up, down))
    depart = pltpu.make_async_remote_copy(
        src_ref=dep,
        dst_ref=cat.at[0:count],
        send_sem=dep_send,
        recv_sem=dep_recv,
        device_id=ahead,
        device_id_type=MESH,
    )
    depart.start()
    place = iota((8, 128), 1)
    slot = place + count
    for m in range(count):
        slot = jnp.where(place == leaving_ref[m], m, slot)
    slot_vec[...] = slot
    to_smem = pltpu.make_async_copy(slot_vec, slot_smem, local_sem)
    to_smem.start()
    cat[count : count + blocks] = state_ref[...]
    lanes = pad.shape[1]
    pad[...] = jnp.zeros_like(pad)
    pad[0:2, 0 : pairs_ref.shape[1]] = pairs_ref[...]
    packed, begin = sort_pairs(lanes, pad, counts_ref[1])
    lists_ref[0] = jnp.zeros((8, 128), i32)
    for row in range(lanes // 128):
        lists_ref[0, row : row + 1, :] = packed[:, 128 * row : 128 * row + 128]
    lists_ref[0, 6:7, :] = begin
    copies = []
    for at, device in ((1, down), (2, up), (3, ahead)):
        copy = pltpu.make_async_remote_copy(
            src_ref=lists_ref.at[0],
            dst_ref=lists_ref.at[at],
            send_sem=list_send.at[at - 1],
            recv_sem=list_recv.at[at - 1],
            device_id=device,
            device_id_type=MESH,
        )
        copy.start()
        copies.append(copy)
    to_smem.wait()
    depart.wait()

    def place_block(j, carry):
        moved[j] = cat[slot_smem[0, j]]
        return carry

    lax.fori_loop(0, blocks, place_block, 0)
    keep = pltpu.make_async_copy(moved, cols_ref.at[0], local_sem)
    keep.start()
    for at, device in ((1, ahead), (2, down), (3, up)):
        copy = pltpu.make_async_remote_copy(
            src_ref=moved,
            dst_ref=cols_ref.at[at],
            send_sem=col_send.at[at - 1],
            recv_sem=col_recv.at[at - 1],
            device_id=device,
            device_id_type=MESH,
        )
        copy.start()
        copies.append(copy)
    keep.wait()
    for copy in copies:
        copy.wait()


def build_tables(cols_ref, U, V, L, RB, extra):
    rows = iota((8, 128), 0)
    eye = (iota((128, 128), 0) == iota((128, 128), 1)).astype(bf16)
    c6 = jnp.where(rows == 6, 1.0, 0.0)
    c7 = jnp.where(rows == 7, 0.25, 0.0)
    ca = jnp.where(rows < 3, -2.0, 0.0)
    cb = jnp.where(rows < 6, -0.25, 0.0)
    ones = jnp.where(rows >= 6, 1.0, 0.0)

    def dense(g, carry):
        at = pl.ds(g * 8, 8)
        x = [cols_ref[at, c, :] for c in range(3)]
        v = [cols_ref[at, c, :] for c in range(3, 6)]
        root = jnp.sqrt(cols_ref[at, 7, :])
        extra[at, 3, :] = jnp.ones((8, 128), f32)
        extra[at, 4, :] = root * cols_ref[at, 6, :]
        extra[at, 5, :] = root
        extra[at, 6, :] = x[0] * x[0] + x[1] * x[1] + x[2] * x[2] + 0.5 * soften
        extra[at, 7, :] = x[0] * v[0] + x[1] * v[1] + x[2] * v[2]
        return carry

    lax.fori_loop(0, cols_ref.shape[0] // 8, dense, 0, unroll=2)

    def one(i, want_u, v_at):
        S = cols_ref[i]
        E = extra[i]
        hi, mid = split2(jnp.where(rows < 3, S, jnp.where(rows < 6, E, 0.0)))
        L[i] = jnp.concatenate([hi, mid], axis=0).astype(bf16)
        full = jnp.where(rows < 6, S, E)
        hi, mid, lo = split3(full)
        if want_u:
            natural = jnp.concatenate(
                [hi, jnp.where(rows < 6, hi, lo), mid, ones, ones, ones], axis=0
            ).astype(bf16)
            U[i] = dot_tt(eye, natural).astype(bf16)
        if v_at is not None:
            def swap(value):
                return jnp.where(
                    rows < 3, pltpu.roll(value, 5, 0), pltpu.roll(value, 3, 0)
                )

            a0 = hi * ca + c6
            a1 = mid * ca + c6
            b0 = swap(hi) * cb + c7
            b1 = swap(mid) * cb + c7
            A = jnp.concatenate([a0, a1, a0, hi * c6, mid * c6, lo * c6], axis=0)
            B = jnp.concatenate([b0, b1, b0, hi * c7, mid * c7, lo * c7], axis=0)
            V[v_at, :, 0:128] = A.astype(bf16)
            V[v_at, :, 128:256] = B.astype(bf16)

    def sweep(low, high, want_u, shift):
        step = 4

        def body(t, carry):
            for q in range(step):
                i = low + t * step + q
                one(i, want_u, None if shift is None else i + shift)
            return carry

        lax.fori_loop(0, (high - low) // step, body, 0)

    sweep(0, 96, True, 0)
    sweep(96, 192, True, None)
    sweep(192, 384, False, -96)

    for col in range(2):
        radius = cols_ref[96 * col : 96 * col + 96, 7, :]
        turned = jnp.concatenate([radius, jnp.zeros((32, 128), f32)], axis=0).T

        def spread(g, carry, turned=turned, col=col):
            here = pltpu.roll(turned, lax.rem(128 - 8 * g, 128), 1)
            for c in range(8):
                RB[96 * col + 8 * g + c] = jnp.broadcast_to(here[:, c : c + 1], (128, 128))
            return carry

        lax.fori_loop(0, 12, spread, 0)


def pair_kernel(lists_ref, cols_ref, moved_ref, own_ref, sides_ref, U, V, L, RB, extra, acc, *rings):
    AB = rings[0:ring]
    M = rings[ring : 2 * ring]
    moved_ref[...] = cols_ref[0:96]
    build_tables(cols_ref, U, V, L, RB, extra)
    trash = acc.shape[0] - 1
    acc[...] = jnp.zeros_like(acc)

    ends = []
    shifts = []
    so_far = 0
    for at in range(4):
        low = lists_ref[at * 1024 + 6 * 128 + at]
        high = lists_ref[at * 1024 + 6 * 128 + at + 1]
        shifts.append(at * 1024 + low - so_far)
        so_far = so_far + (high - low)
        ends.append(so_far)
    n = ends[3]
    last = jnp.maximum(n - 1, 0)

    def entry(k):
        k = jnp.minimum(k, last)
        shift = jnp.where(
            k < ends[0],
            shifts[0],
            jnp.where(k < ends[1], shifts[1], jnp.where(k < ends[2], shifts[2], shifts[3])),
        )
        code = lists_ref[k + shift]
        return code & 255, lax.shift_right_logical(code, 8)

    def spot(v):
        return jnp.where(v < 96, v, v + 96)

    def distances(k, at):
        u, v = entry(k)
        AB[at][...] = jnp.dot(U[u], V[v], preferred_element_type=f32)

    def weights(k, at):
        u, v = entry(k)
        rt = cols_ref[spot(v), 7:8, :]
        for r in range(0, 128, 16):
            A = AB[at][r : r + 16, 0:128]
            B = AB[at][r : r + 16, 128:256]
            R = RB[u, r : r + 16, :] + rt
            inv = lax.rsqrt(A)
            gap = R - A * inv
            inter = jnp.maximum(gap, 0.0)
            root = inter * lax.rsqrt(jnp.maximum(gap, tiny))
            W = (root * inv) * (inter - B * inv)
            G = root * lax.rsqrt(R)
            wh = W.astype(bf16)
            gh = G.astype(bf16)
            M[at][r : r + 16, 0:128] = wh
            M[at][r : r + 16, 128:256] = gh
            M[at][128 + r : 144 + r, 0:128] = (W - wh.astype(f32)).astype(bf16)
            M[at][128 + r : 144 + r, 128:256] = (G - gh.astype(f32)).astype(bf16)

    rows = iota((8, 128), 0)

    def folded(out):
        both = out[0:8] + out[8:16]
        return jnp.where(rows < 4, both[:, 0:128], both[:, 128:256])

    def sums(k, at):
        u, v = entry(k)
        w = spot(v)
        first = jnp.concatenate([L[u], L[u]], axis=1)
        second = jnp.concatenate([L[w], L[w]], axis=1)
        m = M[at]
        crossed = jnp.concatenate(
            [
                jnp.concatenate([m[0:128, 0:128], m[128:256, 0:128]], axis=1),
                jnp.concatenate([m[0:128, 128:256], m[128:256, 128:256]], axis=1),
            ],
            axis=0,
        )
        to_second = folded(jnp.dot(first, m[...], preferred_element_type=f32))
        to_first = folded(dot_tt(second, crossed))
        live = k < n
        u = jnp.where(live, u, trash)
        w = jnp.where(live, w, trash)
        acc[u] += to_first
        acc[w] += to_second

    for q in range(ring):
        distances(q, q)
    for q in range(lag_b):
        weights(q, q)

    def turn(t, carry):
        for q in range(group):
            k = t * group + q
            sums(k, q % ring)
            weights(k + lag_b, (q + lag_b) % ring)
            distances(k + ring, q % ring)
        return carry

    lax.fori_loop(0, lax.div(n + group - 1, group), turn, 0)

    def result(i):
        S = cols_ref[i]
        got = acc[i]
        hi, mid = split2(S)
        force = stiffness * ((hi + mid) * got[3:4] - got)
        heat = conductance * jnp.sqrt(S[7:8]) * (got[4:5] - S[6:7] * got[5:6])
        return jnp.where(rows < 3, force, jnp.where(rows == 3, heat, 0.0))

    def close(t, carry):
        for q in range(4):
            i = t * 4 + q
            own_ref[i] = result(i)
        return carry

    lax.fori_loop(0, 24, close, 0)

    def close_far(t, carry):
        for q in range(4):
            i = t * 4 + q
            lower = result(96 + 2 * i)
            upper = result(97 + 2 * i)
            sides_ref[i] = jnp.where(rows < 4, lower, pltpu.roll(upper, 4, 0))
        return carry

    lax.fori_loop(0, 36, close_far, 0)


def finish_kernel(
    moved_ref,
    own_ref,
    sides_ref,
    flags_ref,
    cells_ref,
    table_ref,
    rates_ref,
    fluid_ref,
    got,
    heat_in,
    to_fluid,
    sums,
    send,
    recv,
):
    ahead, behind, up, down = neighbours()
    greet((ahead, behind, up, down))
    copies = []
    for at, device in ((0, behind), (1, up), (2, down)):
        copy = pltpu.make_async_remote_copy(
            src_ref=sides_ref.at[at],
            dst_ref=got.at[at],
            send_sem=send.at[at],
            recv_sem=recv.at[at],
            device_id=device,
            device_id_type=MESH,
        )
        copy.start()
        copies.append(copy)

    table = jnp.concatenate(split3(table_ref[...]), axis=0).astype(bf16)
    sums[...] = jnp.zeros_like(sums)
    sub = iota((16, 128), 0)

    def cells_of(g, carry):
        at = pl.ds(g * 8, 8)
        temper = moved_ref[at, 6, :]
        radius = moved_ref[at, 7, :]
        volume = 4.0 / 3.0 * math.pi * radius * radius * radius
        cell = cells_ref[at, :]
        high = lax.shift_right_logical(cell, 4)
        low = cell & 15
        fluid = []
        hots = []
        for c in range(8):
            hot_high = (sub == high[c : c + 1]).astype(f32)
            hot_low = (sub == low[c : c + 1]).astype(f32)
            parts = jnp.dot(table, hot_low.astype(bf16), preferred_element_type=f32)
            value = parts[0:16] + parts[16:32] + parts[32:48]
            fluid.append(jnp.sum(value * hot_high, axis=0, keepdims=True))
            hots.append((hot_high, hot_low))
        flow = film_gain * radius * radius * (temper - jnp.concatenate(fluid, axis=0))
        to_fluid[at, :] = flow
        pieces = split3(volume) + split3(flow)
        total = sums[...]
        for c in range(8):
            hot_high, hot_low = hots[c]
            spread = jnp.concatenate([hot_low * piece[c : c + 1] for piece in pieces], axis=0)
            total = total + dot_tt(hot_high.astype(bf16), spread.astype(bf16))
        sums[...] = total
        wall = wall_gain * flags_ref[at, :].astype(f32) * (wall_temp - temper) * radius
        heat_in[at, :] = wall - flow
        return carry

    lax.fori_loop(0, 12, cells_of, 0)
    total = sums[...]
    fluid_ref[0] = (total[:, 0:16] + total[:, 16:32] + total[:, 32:48]) / cell_volume
    fluid_ref[1] = total[:, 48:64] + total[:, 64:80] + total[:, 80:96]
    for copy in copies:
        copy.wait()

    def combine(g, carry):
        at = pl.ds(g * 8, 8)
        radius = moved_ref[at, 7, :]
        volume = 4.0 / 3.0 * math.pi * radius * radius * radius
        inverse = 1.0 / volume
        half = pl.ds(g * 4, 4)
        for c in range(4):
            near = own_ref[at, c, :]
            even = got[0, half, c, :] + got[1, half, c, :] + got[2, half, c, :]
            odd = got[0, half, c + 4, :] + got[1, half, c + 4, :] + got[2, half, c + 4, :]
            far = jnp.stack([even, odd], axis=1).reshape(8, 128)
            value = near + far
            if c == 3:
                value = value + heat_in[at, :]
            value = value * inverse
            if c == 2:
                value = value - gravity
            rates_ref[at, c, :] = value
        return carry

    lax.fori_loop(0, 12, combine, 0)


def vmem():
    return pl.BlockSpec(memory_space=pltpu.VMEM)


def smem():
    return pl.BlockSpec(memory_space=pltpu.SMEM)


def shards(state, leaving, pairs, counts, wall_flags, cell_index, fluid_temp):
    mine = state[0, 0]
    blocks = mine.shape[0]
    count = leaving.shape[2]
    lanes = -(-pairs.shape[3] // 128) * 128
    cols, lists = pl.pallas_call(
        halo_kernel,
        out_shape=(
            jax.ShapeDtypeStruct((4, blocks, 8, 128), f32),
            jax.ShapeDtypeStruct((4, 8, 128), i32),
        ),
        in_specs=[smem(), smem(), vmem(), vmem()],
        out_specs=(pl.BlockSpec(memory_space=pl.ANY), vmem()),
        scratch_shapes=[
            pltpu.VMEM((count + blocks, 8, 128), f32),
            pltpu.VMEM((count, 8, 128), f32),
            pltpu.VMEM((blocks, 8, 128), f32),
            pltpu.VMEM((8, lanes), i32),
            pltpu.VMEM((8, 128), i32),
            pltpu.SMEM((8, 128), i32),
            pltpu.SemaphoreType.DMA,
            pltpu.SemaphoreType.DMA,
            pltpu.SemaphoreType.DMA((3,)),
            pltpu.SemaphoreType.DMA((3,)),
            pltpu.SemaphoreType.DMA((3,)),
            pltpu.SemaphoreType.DMA((3,)),
            pltpu.SemaphoreType.DMA,
        ],
        compiler_params=pltpu.CompilerParams(
            collective_id=0, has_side_effects=True, vmem_limit_bytes=16 * 2**20
        ),
        name="halo",
    )(leaving[0, 0], counts[0, 0], pairs[0, 0], mine)

    moved, own, sides = pl.pallas_call(
        pair_kernel,
        out_shape=(
            jax.ShapeDtypeStruct((blocks, 8, 128), f32),
            jax.ShapeDtypeStruct((blocks, 8, 128), f32),
            jax.ShapeDtypeStruct((3 * blocks // 2, 8, 128), f32),
        ),
        in_specs=[smem(), vmem()],
        out_specs=(vmem(), vmem(), vmem()),
        scratch_shapes=[
            pltpu.VMEM((2 * blocks, 128, 48), bf16),
            pltpu.VMEM((3 * blocks, 48, 256), bf16),
            pltpu.VMEM((4 * blocks, 16, 128), bf16),
            pltpu.VMEM((2 * blocks, 128, 128), f32),
            pltpu.VMEM((4 * blocks, 8, 128), f32),
            pltpu.VMEM((4 * blocks + 1, 8, 128), f32),
        ]
        + [pltpu.VMEM((128, 256), f32)] * ring
        + [pltpu.VMEM((256, 256), bf16)] * ring,
        compiler_params=pltpu.CompilerParams(vmem_limit_bytes=52 * 2**20),
        name="contact",
    )(lists.reshape(4096), cols.reshape(4 * blocks, 8, 128))

    rates, fluid = pl.pallas_call(
        finish_kernel,
        out_shape=(
            jax.ShapeDtypeStruct((blocks, 4, 128), f32),
            jax.ShapeDtypeStruct((2, 16, 16), f32),
        ),
        in_specs=[vmem()] * 6,
        out_specs=(vmem(), vmem()),
        scratch_shapes=[
            pltpu.VMEM((3, blocks // 2, 8, 128), f32),
            pltpu.VMEM((blocks, 128), f32),
            pltpu.VMEM((blocks, 128), f32),
            pltpu.VMEM((16, 96), f32),
            pltpu.SemaphoreType.DMA((3,)),
            pltpu.SemaphoreType.DMA((3,)),
        ],
        compiler_params=pltpu.CompilerParams(
            collective_id=1, has_side_effects=True, vmem_limit_bytes=16 * 2**20
        ),
        name="finish",
    )(
        moved,
        own,
        sides.reshape(3, blocks // 2, 8, 128),
        wall_flags[0, 0],
        cell_index[0, 0],
        fluid_temp.reshape(16, 16),
    )
    return moved[None, None], rates[None, None], fluid.reshape(1, 1, 2, 256)


def solution(mesh):
    in_specs = (
        P("gx", "gy", None, None, None),
        P("gx", "gy", None),
        P("gx", "gy", None, None),
        P("gx", "gy", None),
        P("gx", "gy", None, None),
        P("gx", "gy", None, None),
        P("gx", "gy", None),
    )
    out_specs = (
        P("gx", "gy", None, None, None),
        P("gx", "gy", None, None, None),
        P("gx", "gy", None, None),
    )
    return jax.shard_map(shards, mesh=mesh, in_specs=in_specs, out_specs=out_specs, check_vma=False)
```

```python
import functools
import math

import jax
import jax.numpy as jnp
from jax import lax
from jax.experimental import pallas as pl
from jax.experimental.pallas import tpu as pltpu
from jax.sharding import PartitionSpec as P

soften = 0.01
stiffness = 0.2
damping = 0.05
conductance = 0.05
film_gain = 0.5
wall_gain = 2.0
wall_temp = 1.0
gravity = 1.0
cell_volume = 32.0

f32 = jnp.float32
bf16 = jnp.bfloat16
i32 = jnp.int32

tiny = 1e-30
group = 12
lag_a = 2
lag_b = 2
ring = lag_a + lag_b
MESH = pl.DeviceIdType.MESH


def iota(shape, dim):
    return lax.broadcasted_iota(i32, shape, dim)


def split2(value):
    hi = value.astype(bf16).astype(f32)
    return hi, (value - hi).astype(bf16).astype(f32)


def split3(value):
    hi = value.astype(bf16).astype(f32)
    rest = value - hi
    mid = rest.astype(bf16).astype(f32)
    return hi, mid, rest - mid


def dot_tt(left, right):
    return lax.dot_general(left, right, (((1,), (1,)), ((), ())), preferred_element_type=f32)


def neighbours():
    a = lax.axis_index("gx")
    b = lax.axis_index("gy")
    na = lax.axis_size("gx")
    nb = lax.axis_size("gy")
    return (
        {"gx": lax.rem(a + 1, na)},
        {"gx": lax.rem(a + na - 1, na)},
        {"gy": lax.rem(b + 1, nb)},
        {"gy": lax.rem(b + nb - 1, nb)},
    )


def greet(everyone):
    barrier = pltpu.get_barrier_semaphore()
    for device in everyone:
        pl.semaphore_signal(barrier, inc=1, device_id=device, device_id_type=MESH)
    pl.semaphore_wait(barrier, len(everyone))


def sort_pairs(lanes, pad, total):
    own = pad[0:1, :]
    code = pad[1:2, :]
    region = jnp.zeros_like(code)
    for step in range(1, 9):
        region = region + (code >= 96 * step).astype(i32)
    far = code - 96 * region
    live = iota((1, lanes), 1) < total

    def among(*names):
        hit = region == names[0]
        for name in names[1:]:
            hit = hit | (region == name)
        return hit

    kind = jnp.where(
        among(4),
        0,
        jnp.where(among(1, 5), 1, jnp.where(among(0, 3), 2, jnp.where(among(2), 3, 4))),
    )
    kind = jnp.where(live, kind, 5)
    u_far = among(0, 1, 2, 3)
    u = jnp.where(u_far, far, own) + jnp.where(among(4, 5, 3), 0, 96)
    v_slot = jnp.where(u_far, own, far)
    v_side = jnp.where(among(4, 1, 7), 0, jnp.where(among(5, 3, 0, 8), 1, 2))
    ranks = iota((8, lanes), 0)
    marks = (ranks == kind).astype(f32)
    before = (iota((lanes, lanes), 0) < iota((lanes, lanes), 1)).astype(bf16)
    seen = jnp.dot(marks.astype(bf16), before, preferred_element_type=f32)
    starts = jnp.sum((kind < ranks).astype(f32), axis=1, keepdims=True)
    place = jnp.sum(marks * (seen + starts), axis=0, keepdims=True)
    target = (iota((lanes, lanes), 0).astype(f32) == place).astype(bf16)
    rows = iota((8, lanes), 0)
    values = jnp.where(
        rows == 0, u, jnp.where(rows == 1, v_slot, jnp.where(rows == 2, v_side, 0))
    )
    moved = dot_tt(values.astype(bf16), target)
    packed = moved[0:1] + 256.0 * (moved[1:2] + 96.0 * moved[2:3])
    diag = iota((8, 128), 0) == iota((8, 128), 1)
    begin = jnp.sum(jnp.where(diag, starts, 0.0), axis=0, keepdims=True)
    return packed.astype(i32), begin.astype(i32)


def halo_kernel(
    leaving_hbm,
    counts_hbm,
    pairs_hbm,
    state_hbm,
    cols_ref,
    lists_ref,
    leaving_ref,
    counts_ref,
    pairs_ref,
    cat,
    dep,
    moved,
    pad,
    slot_vec,
    slot_smem,
    dep_send,
    dep_recv,
    list_send,
    list_recv,
    col_send,
    col_recv,
    local_sem,
    in_sem,
):
    blocks = state_hbm.shape[0]
    count = leaving_hbm.shape[0]
    ahead, behind, up, down = neighbours()
    state_ref = cat.at[count : count + blocks]
    inputs = [
        pltpu.make_async_copy(source, target, in_sem.at[at])
        for at, (source, target) in enumerate(
            (
                (leaving_hbm, leaving_ref),
                (state_hbm, state_ref),
                (pairs_hbm, pairs_ref),
                (counts_hbm, counts_ref),
            )
        )
    ]
    for copy in inputs:
        copy.start()
    inputs[0].wait()
    inputs[1].wait()
    for m in range(count):
        dep[m] = state_ref[leaving_ref[m]]
    greet((ahead, behind, up, down))
    depart = pltpu.make_async_remote_copy(
        src_ref=dep,
        dst_ref=cat.at[0:count],
        send_sem=dep_send,
        recv_sem=dep_recv,
        device_id=ahead,
        device_id_type=MESH,
    )
    depart.start()
    place = iota((8, 128), 1)
    slot = place + count
    for m in range(count):
        slot = jnp.where(place == leaving_ref[m], m, slot)
    slot_vec[...] = slot
    to_smem = pltpu.make_async_copy(slot_vec, slot_smem, local_sem)
    to_smem.start()
    inputs[2].wait()
    inputs[3].wait()
    lanes = pad.shape[1]
    pad[...] = jnp.zeros_like(pad)
    pad[0:2, 0 : pairs_ref.shape[1]] = pairs_ref[...]
    packed, begin = sort_pairs(lanes, pad, counts_ref[1])
    lists_ref[0] = jnp.zeros((8, 128), i32)
    for row in range(lanes // 128):
        lists_ref[0, row : row + 1, :] = packed[:, 128 * row : 128 * row + 128]
    lists_ref[0, 6:7, :] = begin
    copies = []
    for at, device in ((1, down), (2, up), (3, ahead)):
        copy = pltpu.make_async_remote_copy(
            src_ref=lists_ref.at[0],
            dst_ref=lists_ref.at[at],
            send_sem=list_send.at[at - 1],
            recv_sem=list_recv.at[at - 1],
            device_id=device,
            device_id_type=MESH,
        )
        copy.start()
        copies.append(copy)
    to_smem.wait()
    depart.wait()

    def place_block(j, carry):
        moved[j] = cat[slot_smem[0, j]]
        return carry

    lax.fori_loop(0, blocks, place_block, 0)
    keep = pltpu.make_async_copy(moved, cols_ref.at[0], local_sem)
    keep.start()
    for at, device in ((1, ahead), (2, down), (3, up)):
        copy = pltpu.make_async_remote_copy(
            src_ref=moved,
            dst_ref=cols_ref.at[at],
            send_sem=col_send.at[at - 1],
            recv_sem=col_recv.at[at - 1],
            device_id=device,
            device_id_type=MESH,
        )
        copy.start()
        copies.append(copy)
    keep.wait()
    for copy in copies:
        copy.wait()


def build_tables(cols_ref, U, V, L, RB, extra, start, step):
    rows = iota((8, 128), 0)
    eye = (iota((128, 128), 0) == iota((128, 128), 1)).astype(bf16)
    c6 = jnp.where(rows == 6, 1.0, 0.0)
    c7 = jnp.where(rows == 7, 0.25, 0.0)
    ca = jnp.where(rows < 3, -2.0, 0.0)
    cb = jnp.where(rows < 6, -0.25, 0.0)
    ones = jnp.where(rows >= 6, 1.0, 0.0)
    zeros = jnp.zeros((8, 128), f32)

    def dense(base):
        at = pl.ds(base, 8)
        x = [cols_ref[at, c, :] for c in range(3)]
        v = [cols_ref[at, c, :] for c in range(3, 6)]
        root = jnp.sqrt(cols_ref[at, 7, :])
        extra[at, 3, :] = jnp.ones((8, 128), f32)
        extra[at, 4, :] = root * cols_ref[at, 6, :]
        extra[at, 5, :] = root
        extra[at, 6, :] = x[0] * x[0] + x[1] * x[1] + x[2] * x[2] + 0.5 * soften
        extra[at, 7, :] = x[0] * v[0] + x[1] * v[1] + x[2] * v[2]

    def swap(value):
        return jnp.where(rows < 3, pltpu.roll(value, 5, 0), pltpu.roll(value, 3, 0))

    def eight(base, shift, want_u):
        naturals = []
        for q in range(8):
            i = base + q
            S = cols_ref[i]
            E = extra[i]
            hi, mid = split2(jnp.where(rows < 3, S, jnp.where(rows < 6, E, 0.0)))
            L[i] = jnp.concatenate([hi, mid], axis=0).astype(bf16)
            hi, mid, lo = split3(jnp.where(rows < 6, S, E))
            if want_u:
                naturals.append(
                    jnp.concatenate(
                        [hi, jnp.where(rows < 6, hi, lo), mid, ones, ones, ones, zeros, zeros],
                        axis=0,
                    ).astype(bf16)
                )
            a0 = hi * ca + c6
            a1 = mid * ca + c6
            b0 = swap(hi) * cb + c7
            b1 = swap(mid) * cb + c7
            A = jnp.concatenate([a0, a1, a0, hi * c6, mid * c6, lo * c6], axis=0)
            B = jnp.concatenate([b0, b1, b0, hi * c7, mid * c7, lo * c7], axis=0)
            V[i + shift, :, 0:128] = A.astype(bf16)
            V[i + shift, :, 128:256] = B.astype(bf16)
        if want_u:
            for half in range(2):
                four = jnp.concatenate(naturals[4 * half : 4 * half + 4], axis=0)
                turned = dot_tt(eye, four)
                for q in range(4):
                    U[base + 4 * half + q] = turned[:, 64 * q : 64 * q + 48].astype(bf16)
            radius = cols_ref[pl.ds(base, 8), 7, :].T
            for q in range(8):
                RB[base + q] = jnp.broadcast_to(radius[:, q : q + 1], (128, 128))

    def body(t, carry):
        for col in range(4):
            dense(96 * col + 8 * t)
        eight(8 * t, 0, True)
        eight(96 + 8 * t, 192, True)
        eight(192 + 8 * t, -96, False)
        eight(288 + 8 * t, -96, False)
        return step(step(carry))

    return lax.fori_loop(0, cols_ref.shape[0] // 32, body, start)


def shares(counts_ref):
    total = counts_ref[1:2, :].astype(f32)
    local = counts_ref[0:1, :].astype(f32)
    device = iota((128, 128), 0)
    lanes = iota((128, 128), 1)
    pick = (lax.shift_right_logical(device, 2) == (lanes & 31)).astype(bf16)
    mine = (iota((8, 128), 1) & 3) == (iota((8, 128), 0) & 3)

    def laid(value):
        hi, mid = split2(jnp.where(mine, value, 0.0))
        return jnp.dot(hi.astype(bf16), pick, preferred_element_type=f32) + jnp.dot(
            mid.astype(bf16), pick, preferred_element_type=f32
        )

    local = laid(local)
    far = (laid(total) - local) * 0.125
    load = (
        local
        + 2.0 * far
        + 2.0 * pltpu.roll(far, 7, 0)
        + pltpu.roll(far, 1, 0)
        + 3.0 * pltpu.roll(far, 1, 1)
    )

    def step(given):
        now = load - given + pltpu.roll(given, 1, 1)
        change = 0.48 * (now - pltpu.roll(now, 127, 1))
        return jnp.minimum(jnp.maximum(given + change, 0.0), local)

    a = lax.axis_index("gx")
    b = lax.axis_index("gy")
    count = lax.axis_size("gx")

    def mask(shift):
        column = lax.rem(a + shift + count, count)
        return (iota((8, 128), 1) == column) & (iota((8, 128), 0) == b)

    return jnp.zeros((8, 128), f32), step, mask


def pair_kernel(lists_ref, cols_ref, counts_ref, moved_ref, own_ref, sides_ref, U, V, L, RB, extra, acc, *rings):
    AB = rings[0:ring]
    M = rings[ring : 2 * ring]
    moved_ref[...] = cols_ref[0:96]
    given, kept, mask = shares(counts_ref)
    given = build_tables(cols_ref, U, V, L, RB, extra, given, kept)
    s_out = jnp.sum(jnp.where(mask(0), given, 0.0)).astype(i32)
    s_in = jnp.sum(jnp.where(mask(-1), given, 0.0)).astype(i32)
    trash = acc.shape[0] - 1
    acc[...] = jnp.zeros_like(acc)

    def begin(at, name):
        return lists_ref[at * 1024 + 6 * 128 + name]

    s_out = jnp.minimum(s_out, begin(0, 1))
    s_in = jnp.minimum(s_in, begin(3, 1))
    ends = []
    shifts = []
    so_far = 0
    for at, low, high in (
        (0, s_out, begin(0, 1)),
        (0, begin(0, 1), begin(0, 2)),
        (1, begin(1, 2), begin(1, 3)),
        (2, begin(2, 3), begin(2, 4)),
        (3, begin(3, 4), begin(3, 5)),
        (3, 0, s_in),
    ):
        shifts.append(at * 1024 + low - so_far)
        so_far = so_far + (high - low)
        ends.append(so_far)
    n = so_far
    last = jnp.maximum(n - 1, 0)

    def entry(k):
        k = jnp.minimum(k, last)
        shift = shifts[5]
        for at in range(4, -1, -1):
            shift = jnp.where(k < ends[at], shifts[at], shift)
        code = lists_ref[k + shift]
        code = code + jnp.where(k < ends[4], 0, 96 + 256 * 288)
        return code & 255, lax.shift_right_logical(code, 8)

    def spot(v):
        return jnp.where(v < 96, v, jnp.where(v < 288, v + 96, v - 192))

    def distances(k, at):
        u, v = entry(k)
        AB[at][...] = jnp.dot(U[u], V[v], preferred_element_type=f32)

    def weights(k, at):
        u, v = entry(k)
        rt = cols_ref[spot(v), 7:8, :]
        for r in range(0, 128, 16):
            A = AB[at][r : r + 16, 0:128]
            B = AB[at][r : r + 16, 128:256]
            R = RB[u, r : r + 16, :] + rt
            inv = lax.rsqrt(A)
            gap = R - A * inv
            inter = jnp.maximum(gap, 0.0)
            root = inter * lax.rsqrt(jnp.maximum(gap, tiny))
            W = (root * inv) * (inter - B * inv)
            G = root * lax.rsqrt(R)
            wh = W.astype(bf16)
            gh = G.astype(bf16)
            M[at][r : r + 16, 0:128] = wh
            M[at][r : r + 16, 128:256] = gh
            M[at][128 + r : 144 + r, 0:128] = (W - wh.astype(f32)).astype(bf16)
            M[at][128 + r : 144 + r, 128:256] = (G - gh.astype(f32)).astype(bf16)

    rows = iota((8, 128), 0)

    def folded(out):
        both = out[0:8] + out[8:16]
        return jnp.where(rows < 4, both[:, 0:128], both[:, 128:256])

    def sums(k, at):
        u, v = entry(k)
        w = spot(v)
        first = jnp.concatenate([L[u], L[u]], axis=1)
        second = jnp.concatenate([L[w], L[w]], axis=1)
        m = M[at]
        crossed = jnp.concatenate(
            [
                jnp.concatenate([m[0:128, 0:128], m[128:256, 0:128]], axis=1),
                jnp.concatenate([m[0:128, 128:256], m[128:256, 128:256]], axis=1),
            ],
            axis=0,
        )
        to_second = folded(jnp.dot(first, m[...], preferred_element_type=f32))
        to_first = folded(dot_tt(second, crossed))
        live = k < n
        u = jnp.where(live, u, trash)
        w = jnp.where(live, w, trash)
        acc[u] += to_first
        acc[w] += to_second

    for q in range(ring):
        distances(q, q)
    for q in range(lag_b):
        weights(q, q)

    def turn(t, carry):
        for q in range(group):
            k = t * group + q
            sums(k, q % ring)
            weights(k + lag_b, (q + lag_b) % ring)
            distances(k + ring, q % ring)
        return carry

    lax.fori_loop(0, lax.div(n + group - 1, group), turn, 0)

    def result(i):
        S = cols_ref[i]
        got = acc[i]
        hi, mid = split2(S)
        force = stiffness * ((hi + mid) * got[3:4] - got)
        heat = conductance * jnp.sqrt(S[7:8]) * (got[4:5] - S[6:7] * got[5:6])
        return jnp.where(rows < 3, force, jnp.where(rows == 3, heat, 0.0))

    def close(t, carry):
        for q in range(4):
            i = t * 4 + q
            own_ref[i] = result(i)
        return carry

    lax.fori_loop(0, 24, close, 0)

    def close_far(t, carry):
        for q in range(4):
            i = t * 4 + q
            lower = result(96 + 2 * i)
            upper = result(97 + 2 * i)
            sides_ref[i] = jnp.where(rows < 4, lower, pltpu.roll(upper, 4, 0))
        return carry

    lax.fori_loop(0, 36, close_far, 0)


def finish_kernel(
    moved_ref,
    own_ref,
    sides_ref,
    flags_ref,
    cells_ref,
    table_ref,
    rates_ref,
    fluid_ref,
    got,
    heat_in,
    to_fluid,
    sums,
    send,
    recv,
):
    ahead, behind, up, down = neighbours()
    greet((ahead, behind, up, down))
    copies = []
    for at, device in ((0, behind), (1, up), (2, down)):
        copy = pltpu.make_async_remote_copy(
            src_ref=sides_ref.at[at],
            dst_ref=got.at[at],
            send_sem=send.at[at],
            recv_sem=recv.at[at],
            device_id=device,
            device_id_type=MESH,
        )
        copy.start()
        copies.append(copy)

    square = jnp.concatenate([table_ref[:, 16 * a : 16 * a + 16] for a in range(16)], axis=0)
    table = jnp.concatenate(split3(square), axis=0).astype(bf16)
    sums[...] = jnp.zeros_like(sums)
    sub = iota((16, 128), 0)

    def cells_of(g, carry):
        at = pl.ds(g * 8, 8)
        temper = moved_ref[at, 6, :]
        radius = moved_ref[at, 7, :]
        volume = 4.0 / 3.0 * math.pi * radius * radius * radius
        cell = cells_ref[at, :]
        high = lax.shift_right_logical(cell, 4)
        low = cell & 15
        fluid = []
        hots = []
        for c in range(8):
            hot_high = (sub == high[c : c + 1]).astype(f32)
            hot_low = (sub == low[c : c + 1]).astype(f32)
            parts = jnp.dot(table, hot_low.astype(bf16), preferred_element_type=f32)
            value = parts[0:16] + parts[16:32] + parts[32:48]
            fluid.append(jnp.sum(value * hot_high, axis=0, keepdims=True))
            hots.append((hot_high, hot_low))
        flow = film_gain * radius * radius * (temper - jnp.concatenate(fluid, axis=0))
        to_fluid[at, :] = flow
        pieces = split3(volume) + split3(flow)
        total = sums[...]
        for c in range(8):
            hot_high, hot_low = hots[c]
            spread = jnp.concatenate([hot_low * piece[c : c + 1] for piece in pieces], axis=0)
            total = total + dot_tt(hot_high.astype(bf16), spread.astype(bf16))
        sums[...] = total
        wall = wall_gain * flags_ref[at, :].astype(f32) * (wall_temp - temper) * radius
        heat_in[at, :] = wall - flow
        return carry

    lax.fori_loop(0, 12, cells_of, 0)
    total = sums[...]
    solid = (total[:, 0:16] + total[:, 16:32] + total[:, 32:48]) / cell_volume
    heat = total[:, 48:64] + total[:, 64:80] + total[:, 80:96]
    for a in range(16):
        fluid_ref[0:1, 16 * a : 16 * a + 16] = solid[a : a + 1]
        fluid_ref[1:2, 16 * a : 16 * a + 16] = heat[a : a + 1]
    for copy in copies:
        copy.wait()

    def combine(g, carry):
        at = pl.ds(g * 8, 8)
        radius = moved_ref[at, 7, :]
        volume = 4.0 / 3.0 * math.pi * radius * radius * radius
        inverse = 1.0 / volume
        half = pl.ds(g * 4, 4)
        for c in range(4):
            near = own_ref[at, c, :]
            even = got[0, half, c, :] + got[1, half, c, :] + got[2, half, c, :]
            odd = got[0, half, c + 4, :] + got[1, half, c + 4, :] + got[2, half, c + 4, :]
            far = jnp.stack([even, odd], axis=1).reshape(8, 128)
            value = near + far
            if c == 3:
                value = value + heat_in[at, :]
            value = value * inverse
            if c == 2:
                value = value - gravity
            rates_ref[at, c, :] = value
        return carry

    lax.fori_loop(0, 12, combine, 0)


def vmem():
    return pl.BlockSpec(memory_space=pltpu.VMEM)


def smem():
    return pl.BlockSpec(memory_space=pltpu.SMEM)


def shards(state, leaving, pairs, counts, wall_flags, cell_index, fluid_temp):
    mine = state[0, 0]
    blocks = mine.shape[0]
    count = leaving.shape[2]
    lanes = -(-pairs.shape[3] // 128) * 128
    every = lax.all_gather(counts.reshape(2, 1), ("gx", "gy"), axis=1, tiled=True)
    cols, lists = pl.pallas_call(
        halo_kernel,
        out_shape=(
            jax.ShapeDtypeStruct((4, blocks, 8, 128), f32),
            jax.ShapeDtypeStruct((4, 8, 128), i32),
        ),
        in_specs=[pl.BlockSpec(memory_space=pl.ANY)] * 4,
        out_specs=(pl.BlockSpec(memory_space=pl.ANY), vmem()),
        scratch_shapes=[
            pltpu.SMEM(leaving.shape[2:], i32),
            pltpu.SMEM(counts.shape[2:], i32),
            pltpu.VMEM(pairs.shape[2:], i32),
            pltpu.VMEM((count + blocks, 8, 128), f32),
            pltpu.VMEM((count, 8, 128), f32),
            pltpu.VMEM((blocks, 8, 128), f32),
            pltpu.VMEM((8, lanes), i32),
            pltpu.VMEM((8, 128), i32),
            pltpu.SMEM((8, 128), i32),
            pltpu.SemaphoreType.DMA,
            pltpu.SemaphoreType.DMA,
            pltpu.SemaphoreType.DMA((3,)),
            pltpu.SemaphoreType.DMA((3,)),
            pltpu.SemaphoreType.DMA((3,)),
            pltpu.SemaphoreType.DMA((3,)),
            pltpu.SemaphoreType.DMA,
            pltpu.SemaphoreType.DMA((4,)),
        ],
        compiler_params=pltpu.CompilerParams(
            collective_id=0, has_side_effects=True, vmem_limit_bytes=16 * 2**20
        ),
        name="halo",
    )(leaving[0, 0], counts[0, 0], pairs[0, 0], mine)

    moved, own, sides = pl.pallas_call(
        pair_kernel,
        out_shape=(
            jax.ShapeDtypeStruct((blocks, 8, 128), f32),
            jax.ShapeDtypeStruct((blocks, 8, 128), f32),
            jax.ShapeDtypeStruct((3 * blocks // 2, 8, 128), f32),
        ),
        in_specs=[smem(), vmem(), vmem()],
        out_specs=(vmem(), vmem(), vmem()),
        scratch_shapes=[
            pltpu.VMEM((2 * blocks, 128, 48), bf16),
            pltpu.VMEM((4 * blocks, 48, 256), bf16),
            pltpu.VMEM((4 * blocks, 16, 128), bf16),
            pltpu.VMEM((2 * blocks, 128, 128), f32),
            pltpu.VMEM((4 * blocks, 8, 128), f32),
            pltpu.VMEM((4 * blocks + 1, 8, 128), f32),
        ]
        + [pltpu.VMEM((128, 256), f32)] * ring
        + [pltpu.VMEM((256, 256), bf16)] * ring,
        compiler_params=pltpu.CompilerParams(vmem_limit_bytes=52 * 2**20),
        name="contact",
    )(lists.reshape(4096), cols.reshape(4 * blocks, 8, 128), every)

    rates, fluid = pl.pallas_call(
        finish_kernel,
        out_shape=(
            jax.ShapeDtypeStruct((blocks, 4, 128), f32),
            jax.ShapeDtypeStruct((2, 256), f32),
        ),
        in_specs=[vmem()] * 6,
        out_specs=(vmem(), vmem()),
        scratch_shapes=[
            pltpu.VMEM((3, blocks // 2, 8, 128), f32),
            pltpu.VMEM((blocks, 128), f32),
            pltpu.VMEM((blocks, 128), f32),
            pltpu.VMEM((16, 96), f32),
            pltpu.SemaphoreType.DMA((3,)),
            pltpu.SemaphoreType.DMA((3,)),
        ],
        compiler_params=pltpu.CompilerParams(
            collective_id=1, has_side_effects=True, vmem_limit_bytes=16 * 2**20
        ),
        name="finish",
    )(
        moved,
        own,
        sides.reshape(3, blocks // 2, 8, 128),
        wall_flags[0, 0],
        cell_index[0, 0],
        fluid_temp.reshape(1, 256),
    )
    return moved[None, None], rates[None, None], fluid.reshape(1, 1, 2, 256)


def solution(mesh):
    in_specs = (
        P("gx", "gy", None, None, None),
        P("gx", "gy", None),
        P("gx", "gy", None, None),
        P("gx", "gy", None),
        P("gx", "gy", None, None),
        P("gx", "gy", None, None),
        P("gx", "gy", None),
    )
    out_specs = (
        P("gx", "gy", None, None, None),
        P("gx", "gy", None, None, None),
        P("gx", "gy", None, None),
    )
    return jax.shard_map(shards, mesh=mesh, in_specs=in_specs, out_specs=out_specs, check_vma=False)
```

```python
import functools
import math

import jax
import jax.numpy as jnp
from jax import lax
from jax.experimental import pallas as pl
from jax.experimental.pallas import tpu as pltpu
from jax.sharding import PartitionSpec as P

soften = 0.01
stiffness = 0.2
damping = 0.05
conductance = 0.05
film_gain = 0.5
wall_gain = 2.0
wall_temp = 1.0
gravity = 1.0
cell_volume = 32.0

f32 = jnp.float32
bf16 = jnp.bfloat16
i32 = jnp.int32

tiny = 1e-30
group = 16
lag_a = 2
lag_b = 2
ring = lag_a + lag_b
reach = 4
vmem_grant = 56 * 2**20
MESH = pl.DeviceIdType.MESH


def iota(shape, dim):
    return lax.broadcasted_iota(i32, shape, dim)


def split2(value):
    hi = value.astype(bf16).astype(f32)
    return hi, (value - hi).astype(bf16).astype(f32)


def split3(value):
    hi = value.astype(bf16).astype(f32)
    rest = value - hi
    mid = rest.astype(bf16).astype(f32)
    return hi, mid, rest - mid


def dot_tt(left, right):
    return lax.dot_general(left, right, (((1,), (1,)), ((), ())), preferred_element_type=f32)


def neighbours():
    a = lax.axis_index("gx")
    b = lax.axis_index("gy")
    na = lax.axis_size("gx")
    nb = lax.axis_size("gy")
    return (
        {"gx": lax.rem(a + 1, na)},
        {"gx": lax.rem(a + na - 1, na)},
        {"gy": lax.rem(b + 1, nb)},
        {"gy": lax.rem(b + nb - 1, nb)},
    )


def greet(everyone):
    barrier = pltpu.get_barrier_semaphore()
    for device in everyone:
        pl.semaphore_signal(barrier, inc=1, device_id=device, device_id_type=MESH)
    pl.semaphore_wait(barrier, len(everyone))


def sort_pairs(lanes, pad, total):
    own = pad[0:1, :]
    code = pad[1:2, :]
    region = jnp.zeros_like(code)
    for step in range(1, 9):
        region = region + (code >= 96 * step).astype(i32)
    far = code - 96 * region
    live = iota((1, lanes), 1) < total

    def among(*names):
        hit = region == names[0]
        for name in names[1:]:
            hit = hit | (region == name)
        return hit

    kind = jnp.where(
        among(4),
        0,
        jnp.where(among(1, 5), 1, jnp.where(among(0, 3), 2, jnp.where(among(2), 3, 4))),
    )
    kind = jnp.where(live, kind, 5)
    u_far = among(0, 1, 2, 3)
    u = jnp.where(u_far, far, own) + jnp.where(among(4, 5, 3), 0, 96)
    v_slot = jnp.where(u_far, own, far)
    v_side = jnp.where(among(4, 1, 7), 0, jnp.where(among(5, 3, 0, 8), 1, 2))
    ranks = iota((8, lanes), 0)
    marks = (ranks == kind).astype(f32)
    before = (iota((lanes, lanes), 0) < iota((lanes, lanes), 1)).astype(bf16)
    seen = jnp.dot(marks.astype(bf16), before, preferred_element_type=f32)
    starts = jnp.sum((kind < ranks).astype(f32), axis=1, keepdims=True)
    place = jnp.sum(marks * (seen + starts), axis=0, keepdims=True)
    target = (iota((lanes, lanes), 0).astype(f32) == place).astype(bf16)
    rows = iota((8, lanes), 0)
    values = jnp.where(
        rows == 0, u, jnp.where(rows == 1, v_slot, jnp.where(rows == 2, v_side, 0))
    )
    moved = dot_tt(values.astype(bf16), target)
    packed = moved[0:1] + 256.0 * (moved[1:2] + 96.0 * moved[2:3])
    diag = iota((8, 128), 0) == iota((8, 128), 1)
    begin = jnp.sum(jnp.where(diag, starts, 0.0), axis=0, keepdims=True)
    return packed.astype(i32), begin.astype(i32)


def halo_kernel(
    leaving_hbm,
    counts_hbm,
    pairs_hbm,
    state_hbm,
    cols_ref,
    lists_ref,
    wide_ref,
    leaving_ref,
    counts_ref,
    pairs_ref,
    cat,
    dep,
    moved,
    pad,
    slot_vec,
    slot_smem,
    dep_send,
    dep_recv,
    list_send,
    list_recv,
    col_send,
    col_recv,
    local_sem,
    in_sem,
    near,
    near_send,
    near_recv,
    wide_send,
    wide_recv,
):
    blocks = state_hbm.shape[0]
    count = leaving_hbm.shape[0]
    ahead, behind, up, down = neighbours()
    state_ref = cat.at[count : count + blocks]
    inputs = [
        pltpu.make_async_copy(source, target, in_sem.at[at])
        for at, (source, target) in enumerate(
            (
                (leaving_hbm, leaving_ref),
                (state_hbm, state_ref),
                (pairs_hbm, pairs_ref),
                (counts_hbm, counts_ref),
            )
        )
    ]
    for copy in inputs:
        copy.start()
    a = lax.axis_index("gx")
    na = lax.axis_size("gx")
    along = {
        step: {"gx": lax.rem(a + step + na, na)} for step in range(-reach, reach + 1) if step
    }
    wide_ref[...] = jnp.zeros_like(wide_ref)
    for copy in inputs:
        copy.wait()
    local = counts_ref[0].astype(f32)
    far = (counts_ref[1] - counts_ref[0]).astype(f32) * 0.125
    near[0:1, :] = jnp.full((1, 128), far)
    for m in range(count):
        dep[m] = state_ref[leaving_ref[m]]
    greet((up, down, *along.values()))
    asks = []
    for at, device in ((1, down), (2, up), (3, ahead)):
        copy = pltpu.make_async_remote_copy(
            src_ref=near.at[0:1],
            dst_ref=near.at[at : at + 1],
            send_sem=near_send.at[at - 1],
            recv_sem=near_recv.at[at - 1],
            device_id=device,
            device_id_type=MESH,
        )
        copy.start()
        asks.append(copy)
    depart = pltpu.make_async_remote_copy(
        src_ref=dep,
        dst_ref=cat.at[0:count],
        send_sem=dep_send,
        recv_sem=dep_recv,
        device_id=ahead,
        device_id_type=MESH,
    )
    depart.start()
    place = iota((8, 128), 1)
    slot = place + count
    for m in range(count):
        slot = jnp.where(place == leaving_ref[m], m, slot)
    slot_vec[...] = slot
    to_smem = pltpu.make_async_copy(slot_vec, slot_smem, local_sem)
    to_smem.start()
    lanes = pad.shape[1]
    pad[...] = jnp.zeros_like(pad)
    pad[0:2, 0 : pairs_ref.shape[1]] = pairs_ref[...]
    packed, begin = sort_pairs(lanes, pad, counts_ref[1])
    lists_ref[0] = jnp.zeros((8, 128), i32)
    for row in range(lanes // 128):
        lists_ref[0, row : row + 1, :] = packed[:, 128 * row : 128 * row + 128]
    lists_ref[0, 6:7, :] = begin
    copies = []
    for at, device in ((1, down), (2, up), (3, ahead)):
        copy = pltpu.make_async_remote_copy(
            src_ref=lists_ref.at[0],
            dst_ref=lists_ref.at[at],
            send_sem=list_send.at[at - 1],
            recv_sem=list_recv.at[at - 1],
            device_id=device,
            device_id_type=MESH,
        )
        copy.start()
        copies.append(copy)
    for copy in asks:
        copy.wait()
    load = local + 2.0 * far + 2.0 * near[1:2, :] + near[2:3, :] + 3.0 * near[3:4, :]
    wide_ref[reach : reach + 1, :] = jnp.where(iota((1, 128), 1) < 64, load, local)
    for at, step in enumerate(along):
        copy = pltpu.make_async_remote_copy(
            src_ref=wide_ref.at[reach : reach + 1],
            dst_ref=wide_ref.at[reach - step : reach - step + 1],
            send_sem=wide_send.at[at],
            recv_sem=wide_recv.at[at],
            device_id=along[step],
            device_id_type=MESH,
        )
        copy.start()
        copies.append(copy)
    to_smem.wait()
    depart.wait()

    def place_block(j, carry):
        moved[j] = cat[slot_smem[0, j]]
        return carry

    lax.fori_loop(0, blocks, place_block, 0)
    keep = pltpu.make_async_copy(moved, cols_ref.at[0], local_sem)
    keep.start()
    for at, device in ((1, ahead), (2, down), (3, up)):
        copy = pltpu.make_async_remote_copy(
            src_ref=moved,
            dst_ref=cols_ref.at[at],
            send_sem=col_send.at[at - 1],
            recv_sem=col_recv.at[at - 1],
            device_id=device,
            device_id_type=MESH,
        )
        copy.start()
        copies.append(copy)
    keep.wait()
    for copy in copies:
        copy.wait()


def build_tables(cols_ref, U, V, L, RT, extra, pieces, start, step):
    rows = iota((8, 128), 0)
    eye = (iota((128, 128), 0) == iota((128, 128), 1)).astype(bf16)
    c6 = jnp.where(rows == 6, 1.0, 0.0)
    c7 = jnp.where(rows == 7, 0.25, 0.0)
    ca = jnp.where(rows < 3, -2.0, 0.0)
    cb = jnp.where(rows < 6, -0.25, 0.0)
    ones = jnp.where(rows < 6, 1.0, 0.0)

    def dense(base):
        at = pl.ds(base, 8)
        x = [cols_ref[at, c, :] for c in range(3)]
        v = [cols_ref[at, c, :] for c in range(3, 6)]
        radius = cols_ref[at, 7, :]
        root = jnp.sqrt(radius)
        square = x[0] * x[0] + x[1] * x[1] + x[2] * x[2] + 0.5 * soften
        dot = x[0] * v[0] + x[1] * v[1] + x[2] * v[2]
        extra[at, 3, :] = jnp.ones((8, 128), f32)
        extra[at, 4, :] = root * cols_ref[at, 6, :]
        extra[at, 5, :] = root
        extra[at, 6, :] = square
        extra[at, 7, :] = dot
        for c, piece in enumerate(split3(square) + split3(0.25 * dot)):
            pieces[at, c, :] = piece
        return radius

    def swap(value):
        return jnp.where(rows < 3, pltpu.roll(value, 5, 0), pltpu.roll(value, 3, 0))

    def eight(base, shift, want_u, radius):
        naturals = []
        for q in range(8):
            i = base + q
            S = cols_ref[i]
            E = extra[i]
            G = pieces[i]
            hi, mid = split2(jnp.where(rows < 3, S, jnp.where(rows < 6, E, 0.0)))
            L[i] = jnp.concatenate([hi, mid], axis=0).astype(bf16)
            full = jnp.where(rows < 6, S, E)
            hi, mid = split2(full)
            if want_u:
                low = jnp.where(rows < 6, hi, full - hi - mid)
                naturals.append(jnp.concatenate([hi, low, mid, ones], axis=0).astype(bf16))
            a0 = hi * ca + c6
            a1 = mid * ca + c6
            b0 = swap(hi) * cb + c7
            b1 = swap(mid) * cb + c7
            A = jnp.concatenate([a0, a1, a0, jnp.where(rows < 3, G, 0.0)], axis=0)
            B = jnp.concatenate(
                [b0, b1, b0, jnp.where((rows >= 3) & (rows < 6), G, 0.0)], axis=0
            )
            V[i + shift, :, 0:128] = A.astype(bf16)
            V[i + shift, :, 128:256] = B.astype(bf16)
        if want_u:
            turned = dot_tt(eye, jnp.concatenate(naturals, axis=0))
            for q in range(8):
                U[base + q] = turned[:, 32 * q : 32 * q + 32].astype(bf16)
            RT[lax.shift_right_logical(base, 3), :, 0:8] = radius.T

    def body(t, carry):
        radius = [dense(96 * col + 8 * t) for col in range(4)]
        eight(8 * t, 0, True, radius[0])
        eight(96 + 8 * t, 192, True, radius[1])
        eight(192 + 8 * t, -96, False, None)
        eight(288 + 8 * t, -96, False, None)
        return step(step(carry))

    return lax.fori_loop(0, cols_ref.shape[0] // 32, body, start)


def shares(wide):
    rows = iota((8, 128), 0)

    def chain(load):
        local = jnp.where(rows < 7, pltpu.roll(load, 64, 1), 0.0)

        def step(given):
            now = load - given + pltpu.roll(given, 1, 0)
            change = 0.48 * (now - pltpu.roll(now, 7, 0))
            return jnp.minimum(jnp.maximum(given + change, 0.0), local)

        return step

    own = chain(wide[1:9, :])
    behind = chain(wide[0:8, :])

    def step(given):
        return own(given[0]), behind(given[1])

    def value(given):
        picked = (rows == reach - 1) & (iota((8, 128), 1) == 0)
        return jnp.sum(jnp.where(picked, given, 0.0)).astype(i32)

    start = jnp.zeros((8, 128), f32)
    return (start, start), step, value


def pair_kernel(
    lists_hbm,
    cols_hbm,
    wide_hbm,
    moved_ref,
    own_ref,
    sides_ref,
    lists_ref,
    cols_ref,
    wide,
    U,
    V,
    L,
    RT,
    extra,
    pieces,
    acc,
    sem,
    *rings,
):
    AB = rings[0:ring]
    M = rings[ring : 2 * ring]
    copies = [
        pltpu.make_async_copy(source, target, sem.at[at])
        for at, (source, target) in enumerate(
            ((cols_hbm, cols_ref), (lists_hbm, lists_ref), (wide_hbm, wide))
        )
    ]
    for copy in copies:
        copy.start()
    trash = acc.shape[0] - 1
    acc[...] = jnp.zeros_like(acc)
    for copy in copies:
        copy.wait()
    keep = pltpu.make_async_copy(cols_ref.at[0:96], moved_ref, sem.at[3])
    keep.start()
    given, step, value = shares(wide)
    given = build_tables(cols_ref, U, V, L, RT, extra, pieces, given, step)
    s_out = value(given[0])
    s_in = value(given[1])

    def begin(at, name):
        return lists_ref[at * 1024 + 6 * 128 + name]

    s_out = jnp.minimum(s_out, begin(0, 1))
    s_in = jnp.minimum(s_in, begin(3, 1))
    ends = []
    shifts = []
    so_far = 0
    for at, low, high in (
        (0, s_out, begin(0, 1)),
        (0, begin(0, 1), begin(0, 2)),
        (1, begin(1, 2), begin(1, 3)),
        (2, begin(2, 3), begin(2, 4)),
        (3, begin(3, 4), begin(3, 5)),
        (3, 0, s_in),
    ):
        shifts.append(at * 1024 + low - so_far)
        so_far = so_far + (high - low)
        ends.append(so_far)
    n = so_far
    last = jnp.maximum(n - 1, 0)

    def entry(k):
        k = jnp.minimum(k, last)
        shift = shifts[5]
        for at in range(4, -1, -1):
            shift = jnp.where(k < ends[at], shifts[at], shift)
        code = lists_ref[k + shift]
        code = code + jnp.where(k < ends[4], 0, 96 + 256 * 288)
        return code & 255, lax.shift_right_logical(code, 8)

    def spot(v):
        return jnp.where(v < 96, v, jnp.where(v < 288, v + 96, v - 192))

    def distances(k, at):
        u, v = entry(k)
        AB[at][...] = jnp.dot(U[u], V[v], preferred_element_type=f32)

    def weights(k, at):
        u, v = entry(k)
        rt = cols_ref[spot(v), 7:8, :]
        lane = jnp.full((8, 128), u & 7, i32)
        eighth = lax.shift_right_logical(u, 3)

        def radius(r):
            return jnp.take_along_axis(RT[eighth, r : r + 8, :], lane, axis=1)

        for r in range(0, 128, 16):
            A = AB[at][r : r + 16, 0:128]
            B = AB[at][r : r + 16, 128:256]
            R = jnp.concatenate([radius(r), radius(r + 8)], axis=0) + rt
            inv = lax.rsqrt(A)
            gap = R - A * inv
            inter = jnp.maximum(gap, 0.0)
            root = inter * lax.rsqrt(jnp.maximum(gap, tiny))
            W = (root * inv) * (inter - B * inv)
            G = root * lax.rsqrt(R)
            wh = W.astype(bf16)
            gh = G.astype(bf16)
            M[at][r : r + 16, 0:128] = wh
            M[at][r : r + 16, 128:256] = gh
            M[at][128 + r : 144 + r, 0:128] = (W - wh.astype(f32)).astype(bf16)
            M[at][128 + r : 144 + r, 128:256] = (G - gh.astype(f32)).astype(bf16)

    rows = iota((8, 128), 0)

    def folded(out):
        both = out[0:8] + out[8:16]
        return jnp.where(rows < 4, both[:, 0:128], both[:, 128:256])

    def sums(k, at):
        u, v = entry(k)
        w = spot(v)
        first = jnp.concatenate([L[u], L[u]], axis=1)
        second = jnp.concatenate([L[w], L[w]], axis=1)
        m = M[at]
        crossed = jnp.concatenate(
            [
                jnp.concatenate([m[0:128, 0:128], m[128:256, 0:128]], axis=1),
                jnp.concatenate([m[0:128, 128:256], m[128:256, 128:256]], axis=1),
            ],
            axis=0,
        )
        to_second = folded(jnp.dot(first, m[...], preferred_element_type=f32))
        to_first = folded(dot_tt(second, crossed))
        live = k < n
        u = jnp.where(live, u, trash)
        w = jnp.where(live, w, trash)
        acc[u] += to_first
        acc[w] += to_second

    for q in range(ring):
        distances(q, q)
    for q in range(lag_b):
        weights(q, q)

    def turn(t, carry):
        for q in range(group):
            k = t * group + q
            sums(k, q % ring)
            weights(k + lag_b, (q + lag_b) % ring)
            distances(k + ring, q % ring)
        return carry

    lax.fori_loop(0, lax.div(n + group - 1, group), turn, 0)

    def close(base, out_ref, out_base):
        at = pl.ds(base, 8)
        got = [acc[at, c, :] for c in range(6)]
        terms = []
        for c in range(3):
            hi, mid = split2(cols_ref[at, c, :])
            terms.append(stiffness * ((hi + mid) * got[3] - got[c]))
        root = conductance * extra[at, 5, :]
        terms.append(root * (got[4] - cols_ref[at, 6, :] * got[5]))
        for c in range(4):
            out_ref[pl.ds(out_base + c, 8, 4), :] = terms[c]

    def close_all(t, carry):
        close(8 * t, own_ref, 32 * t)
        for side in range(3):
            close(96 * (side + 1) + 8 * t, sides_ref, 384 * side + 32 * t)
        return carry

    lax.fori_loop(0, 12, close_all, 0)
    keep.wait()


def finish_kernel(
    moved_hbm,
    own_hbm,
    sides_ref,
    flags_hbm,
    cells_hbm,
    table_hbm,
    rates_ref,
    fluid_ref,
    moved_ref,
    own_ref,
    flags_ref,
    cells_ref,
    table_ref,
    in_sem,
    got,
    heat_in,
    to_fluid,
    sums,
    send,
    recv,
):
    ahead, behind, up, down = neighbours()
    inputs = [
        pltpu.make_async_copy(source, target, in_sem.at[at])
        for at, (source, target) in enumerate(
            (
                (moved_hbm, moved_ref),
                (flags_hbm, flags_ref),
                (cells_hbm, cells_ref),
                (table_hbm, table_ref),
                (own_hbm, own_ref),
            )
        )
    ]
    for copy in inputs:
        copy.start()
    greet((ahead, behind, up, down))
    copies = []
    span = got.shape[1]
    for at, device in ((0, behind), (1, up), (2, down)):
        copy = pltpu.make_async_remote_copy(
            src_ref=sides_ref.at[span * at : span * at + span],
            dst_ref=got.at[at],
            send_sem=send.at[at],
            recv_sem=recv.at[at],
            device_id=device,
            device_id_type=MESH,
        )
        copy.start()
        copies.append(copy)

    for copy in inputs:
        copy.wait()
    square = jnp.concatenate([table_ref[:, 16 * a : 16 * a + 16] for a in range(16)], axis=0)
    table = jnp.concatenate(split3(square), axis=0).astype(bf16)
    sums[...] = jnp.zeros_like(sums)
    sub = iota((16, 128), 0)

    def cells_of(g, carry):
        at = pl.ds(g * 8, 8)
        temper = moved_ref[at, 6, :]
        radius = moved_ref[at, 7, :]
        volume = 4.0 / 3.0 * math.pi * radius * radius * radius
        cell = cells_ref[at, :]
        high = lax.shift_right_logical(cell, 4)
        low = cell & 15
        fluid = []
        hots = []
        for c in range(8):
            hot_high = (sub == high[c : c + 1]).astype(f32)
            hot_low = (sub == low[c : c + 1]).astype(f32)
            parts = jnp.dot(table, hot_low.astype(bf16), preferred_element_type=f32)
            value = parts[0:16] + parts[16:32] + parts[32:48]
            fluid.append(jnp.sum(value * hot_high, axis=0, keepdims=True))
            hots.append((hot_high, hot_low))
        flow = film_gain * radius * radius * (temper - jnp.concatenate(fluid, axis=0))
        to_fluid[at, :] = flow
        pieces = split3(volume) + split3(flow)
        total = sums[...]
        for c in range(8):
            hot_high, hot_low = hots[c]
            spread = jnp.concatenate([hot_low * piece[c : c + 1] for piece in pieces], axis=0)
            total = total + dot_tt(hot_high.astype(bf16), spread.astype(bf16))
        sums[...] = total
        wall = wall_gain * flags_ref[at, :].astype(f32) * (wall_temp - temper) * radius
        heat_in[at, :] = wall - flow
        return carry

    lax.fori_loop(0, 12, cells_of, 0)
    total = sums[...]
    solid = (total[:, 0:16] + total[:, 16:32] + total[:, 32:48]) / cell_volume
    heat = total[:, 48:64] + total[:, 64:80] + total[:, 80:96]
    for a in range(16):
        fluid_ref[0:1, 16 * a : 16 * a + 16] = solid[a : a + 1]
        fluid_ref[1:2, 16 * a : 16 * a + 16] = heat[a : a + 1]
    for copy in copies:
        copy.wait()

    def combine(g, carry):
        at = pl.ds(g * 8, 8)
        radius = moved_ref[at, 7, :]
        volume = 4.0 / 3.0 * math.pi * radius * radius * radius
        inverse = 1.0 / volume
        for c in range(4):
            here = pl.ds(g * 32 + c, 8, 4)
            value = own_ref[here, :]
            for side in range(3):
                value = value + got[side, here, :]
            if c == 3:
                value = value + heat_in[at, :]
            value = value * inverse
            if c == 2:
                value = value - gravity
            rates_ref[at, c, :] = value
        return carry

    lax.fori_loop(0, 12, combine, 0)


def anywhere():
    return pl.BlockSpec(memory_space=pl.ANY)


def vmem():
    return pl.BlockSpec(memory_space=pltpu.VMEM)


def shards(state, leaving, pairs, counts, wall_flags, cell_index, fluid_temp):
    mine = state[0, 0]
    blocks = mine.shape[0]
    count = leaving.shape[2]
    lanes = -(-pairs.shape[3] // 128) * 128
    cols, lists, wide = pl.pallas_call(
        halo_kernel,
        out_shape=(
            jax.ShapeDtypeStruct((4, blocks, 8, 128), f32),
            jax.ShapeDtypeStruct((4, 8, 128), i32),
            jax.ShapeDtypeStruct((16, 128), f32),
        ),
        in_specs=[anywhere()] * 4,
        out_specs=(anywhere(), vmem(), vmem()),
        scratch_shapes=[
            pltpu.SMEM(leaving.shape[2:], i32),
            pltpu.SMEM(counts.shape[2:], i32),
            pltpu.VMEM(pairs.shape[2:], i32),
            pltpu.VMEM((count + blocks, 8, 128), f32),
            pltpu.VMEM((count, 8, 128), f32),
            pltpu.VMEM((blocks, 8, 128), f32),
            pltpu.VMEM((8, lanes), i32),
            pltpu.VMEM((8, 128), i32),
            pltpu.SMEM((8, 128), i32),
            pltpu.SemaphoreType.DMA,
            pltpu.SemaphoreType.DMA,
            pltpu.SemaphoreType.DMA((3,)),
            pltpu.SemaphoreType.DMA((3,)),
            pltpu.SemaphoreType.DMA((3,)),
            pltpu.SemaphoreType.DMA((3,)),
            pltpu.SemaphoreType.DMA,
            pltpu.SemaphoreType.DMA((4,)),
            pltpu.VMEM((8, 128), f32),
            pltpu.SemaphoreType.DMA((3,)),
            pltpu.SemaphoreType.DMA((3,)),
            pltpu.SemaphoreType.DMA((2 * reach,)),
            pltpu.SemaphoreType.DMA((2 * reach,)),
        ],
        compiler_params=pltpu.CompilerParams(
            collective_id=0, has_side_effects=True, vmem_limit_bytes=vmem_grant
        ),
        name="halo",
    )(leaving[0, 0], counts[0, 0], pairs[0, 0], mine)

    moved, own, sides = pl.pallas_call(
        pair_kernel,
        out_shape=(
            jax.ShapeDtypeStruct((blocks, 8, 128), f32),
            jax.ShapeDtypeStruct((4 * blocks, 128), f32),
            jax.ShapeDtypeStruct((12 * blocks, 128), f32),
        ),
        in_specs=[anywhere()] * 3,
        out_specs=(anywhere(), vmem(), vmem()),
        scratch_shapes=[
            pltpu.SMEM((4096,), i32),
            pltpu.VMEM((4 * blocks, 8, 128), f32),
            pltpu.VMEM((16, 128), f32),
            pltpu.VMEM((2 * blocks, 128, 32), bf16),
            pltpu.VMEM((4 * blocks, 32, 256), bf16),
            pltpu.VMEM((4 * blocks, 16, 128), bf16),
            pltpu.VMEM((blocks // 4, 128, 128), f32),
            pltpu.VMEM((4 * blocks, 8, 128), f32),
            pltpu.VMEM((4 * blocks, 8, 128), f32),
            pltpu.VMEM((4 * blocks + 1, 8, 128), f32),
            pltpu.SemaphoreType.DMA((4,)),
        ]
        + [pltpu.VMEM((128, 256), f32)] * ring
        + [pltpu.VMEM((256, 256), bf16)] * ring,
        compiler_params=pltpu.CompilerParams(vmem_limit_bytes=vmem_grant),
        name="contact",
    )(lists.reshape(4096), cols.reshape(4 * blocks, 8, 128), wide)

    rates, fluid = pl.pallas_call(
        finish_kernel,
        out_shape=(
            jax.ShapeDtypeStruct((blocks, 4, 128), f32),
            jax.ShapeDtypeStruct((2, 256), f32),
        ),
        in_specs=[anywhere()] * 6,
        out_specs=(vmem(), vmem()),
        scratch_shapes=[
            pltpu.VMEM((blocks, 8, 128), f32),
            pltpu.VMEM((4 * blocks, 128), f32),
            pltpu.VMEM((blocks, 128), i32),
            pltpu.VMEM((blocks, 128), i32),
            pltpu.VMEM((1, 256), f32),
            pltpu.SemaphoreType.DMA((5,)),
            pltpu.VMEM((3, 4 * blocks, 128), f32),
            pltpu.VMEM((blocks, 128), f32),
            pltpu.VMEM((blocks, 128), f32),
            pltpu.VMEM((16, 96), f32),
            pltpu.SemaphoreType.DMA((3,)),
            pltpu.SemaphoreType.DMA((3,)),
        ],
        compiler_params=pltpu.CompilerParams(
            collective_id=1, has_side_effects=True, vmem_limit_bytes=vmem_grant
        ),
        name="finish",
    )(
        moved,
        own,
        sides,
        wall_flags[0, 0],
        cell_index[0, 0],
        fluid_temp.reshape(1, 256),
    )
    return moved[None, None], rates[None, None], fluid.reshape(1, 1, 2, 256)


def solution(mesh):
    in_specs = (
        P("gx", "gy", None, None, None),
        P("gx", "gy", None),
        P("gx", "gy", None, None),
        P("gx", "gy", None),
        P("gx", "gy", None, None),
        P("gx", "gy", None, None),
        P("gx", "gy", None),
    )
    out_specs = (
        P("gx", "gy", None, None, None),
        P("gx", "gy", None, None, None),
        P("gx", "gy", None, None),
    )
    return jax.shard_map(shards, mesh=mesh, in_specs=in_specs, out_specs=out_specs, check_vma=False)
```

```python
import functools
import math

import jax
import jax.numpy as jnp
from jax import lax
from jax.experimental import pallas as pl
from jax.experimental.pallas import tpu as pltpu
from jax.sharding import PartitionSpec as P

soften = 0.01
stiffness = 0.2
damping = 0.05
conductance = 0.05
film_gain = 0.5
wall_gain = 2.0
wall_temp = 1.0
gravity = 1.0
cell_volume = 32.0

f32 = jnp.float32
bf16 = jnp.bfloat16
i32 = jnp.int32

tiny = 1e-30
group = 16
lag_a = 2
lag_b = 2
ring = lag_a + lag_b
reach = 4
vmem_grant = 56 * 2**20
MESH = pl.DeviceIdType.MESH


def iota(shape, dim):
    return lax.broadcasted_iota(i32, shape, dim)


def split2(value):
    hi = value.astype(bf16).astype(f32)
    return hi, (value - hi).astype(bf16).astype(f32)


def split3(value):
    hi = value.astype(bf16).astype(f32)
    rest = value - hi
    mid = rest.astype(bf16).astype(f32)
    return hi, mid, rest - mid


def dot_tt(left, right):
    return lax.dot_general(left, right, (((1,), (1,)), ((), ())), preferred_element_type=f32)


def neighbours():
    a = lax.axis_index("gx")
    b = lax.axis_index("gy")
    na = lax.axis_size("gx")
    nb = lax.axis_size("gy")
    return (
        {"gx": lax.rem(a + 1, na)},
        {"gx": lax.rem(a + na - 1, na)},
        {"gy": lax.rem(b + 1, nb)},
        {"gy": lax.rem(b + nb - 1, nb)},
    )


def greet(everyone):
    barrier = pltpu.get_barrier_semaphore()
    for device in everyone:
        pl.semaphore_signal(barrier, inc=1, device_id=device, device_id_type=MESH)
    pl.semaphore_wait(barrier, len(everyone))


def sort_pairs(lanes, pad, total):
    own = pad[0:1, :]
    code = pad[1:2, :]
    region = jnp.zeros_like(code)
    for step in range(1, 9):
        region = region + (code >= 96 * step).astype(i32)
    far = code - 96 * region
    live = iota((1, lanes), 1) < total

    def among(*names):
        hit = region == names[0]
        for name in names[1:]:
            hit = hit | (region == name)
        return hit

    kind = jnp.where(
        among(4),
        0,
        jnp.where(among(1, 5), 1, jnp.where(among(0, 3), 2, jnp.where(among(2), 3, 4))),
    )
    kind = jnp.where(live, kind, 5)
    u_far = among(0, 1, 2, 3)
    u = jnp.where(u_far, far, own) + jnp.where(among(4, 5, 3), 0, 96)
    v_slot = jnp.where(u_far, own, far)
    v_side = jnp.where(among(4, 1, 7), 0, jnp.where(among(5, 3, 0, 8), 1, 2))
    ranks = iota((8, lanes), 0)
    marks = (ranks == kind).astype(f32)
    before = (iota((lanes, lanes), 0) < iota((lanes, lanes), 1)).astype(bf16)
    seen = jnp.dot(marks.astype(bf16), before, preferred_element_type=f32)
    starts = jnp.sum((kind < ranks).astype(f32), axis=1, keepdims=True)
    place = jnp.sum(marks * (seen + starts), axis=0, keepdims=True)
    target = (iota((lanes, lanes), 0).astype(f32) == place).astype(bf16)
    rows = iota((8, lanes), 0)
    values = jnp.where(
        rows == 0, u, jnp.where(rows == 1, v_slot, jnp.where(rows == 2, v_side, 0))
    )
    moved = dot_tt(values.astype(bf16), target)
    packed = moved[0:1] + 256.0 * (moved[1:2] + 96.0 * moved[2:3])
    diag = iota((8, 128), 0) == iota((8, 128), 1)
    begin = jnp.sum(jnp.where(diag, starts, 0.0), axis=0, keepdims=True)
    return packed.astype(i32), begin.astype(i32)


def halo_kernel(
    leaving_hbm,
    counts_hbm,
    pairs_hbm,
    state_hbm,
    cols_ref,
    lists_ref,
    wide_ref,
    leaving_ref,
    counts_ref,
    pairs_ref,
    cat,
    dep,
    moved,
    pad,
    slot_vec,
    slot_smem,
    dep_send,
    dep_recv,
    list_send,
    list_recv,
    col_send,
    col_recv,
    local_sem,
    in_sem,
    near,
    near_send,
    near_recv,
    wide_send,
    wide_recv,
):
    blocks = state_hbm.shape[0]
    count = leaving_hbm.shape[0]
    ahead, behind, up, down = neighbours()
    state_ref = cat.at[count : count + blocks]
    inputs = [
        pltpu.make_async_copy(source, target, in_sem.at[at])
        for at, (source, target) in enumerate(
            (
                (leaving_hbm, leaving_ref),
                (state_hbm, state_ref),
                (pairs_hbm, pairs_ref),
                (counts_hbm, counts_ref),
            )
        )
    ]
    for copy in inputs:
        copy.start()
    a = lax.axis_index("gx")
    na = lax.axis_size("gx")
    along = {
        step: {"gx": lax.rem(a + step + na, na)} for step in range(-reach, reach + 1) if step
    }
    wide_ref[...] = jnp.zeros_like(wide_ref)
    for copy in inputs:
        copy.wait()
    local = counts_ref[0].astype(f32)
    far = (counts_ref[1] - counts_ref[0]).astype(f32) * 0.125
    near[0:1, :] = jnp.full((1, 128), far)
    for m in range(count):
        dep[m] = state_ref[leaving_ref[m]]
    greet((up, down, *along.values()))
    asks = []
    for at, device in ((1, down), (2, up), (3, ahead)):
        copy = pltpu.make_async_remote_copy(
            src_ref=near.at[0:1],
            dst_ref=near.at[at : at + 1],
            send_sem=near_send.at[at - 1],
            recv_sem=near_recv.at[at - 1],
            device_id=device,
            device_id_type=MESH,
        )
        copy.start()
        asks.append(copy)
    depart = pltpu.make_async_remote_copy(
        src_ref=dep,
        dst_ref=cat.at[0:count],
        send_sem=dep_send,
        recv_sem=dep_recv,
        device_id=ahead,
        device_id_type=MESH,
    )
    depart.start()
    place = iota((8, 128), 1)
    slot = place + count
    for m in range(count):
        slot = jnp.where(place == leaving_ref[m], m, slot)
    slot_vec[...] = slot
    to_smem = pltpu.make_async_copy(slot_vec, slot_smem, local_sem)
    to_smem.start()
    lanes = pad.shape[1]
    pad[...] = jnp.zeros_like(pad)
    pad[0:2, 0 : pairs_ref.shape[1]] = pairs_ref[...]
    packed, begin = sort_pairs(lanes, pad, counts_ref[1])
    lists_ref[0] = jnp.zeros((8, 128), i32)
    for row in range(lanes // 128):
        lists_ref[0, row : row + 1, :] = packed[:, 128 * row : 128 * row + 128]
    lists_ref[0, 6:7, :] = begin
    copies = []
    for at, device in ((1, down), (2, up), (3, ahead)):
        copy = pltpu.make_async_remote_copy(
            src_ref=lists_ref.at[0],
            dst_ref=lists_ref.at[at],
            send_sem=list_send.at[at - 1],
            recv_sem=list_recv.at[at - 1],
            device_id=device,
            device_id_type=MESH,
        )
        copy.start()
        copies.append(copy)
    for copy in asks:
        copy.wait()
    load = local + 2.0 * far + 2.0 * near[1:2, :] + near[2:3, :] + 3.0 * near[3:4, :]
    wide_ref[reach : reach + 1, :] = jnp.where(iota((1, 128), 1) < 64, load, local)
    for at, step in enumerate(along):
        copy = pltpu.make_async_remote_copy(
            src_ref=wide_ref.at[reach : reach + 1],
            dst_ref=wide_ref.at[reach - step : reach - step + 1],
            send_sem=wide_send.at[at],
            recv_sem=wide_recv.at[at],
            device_id=along[step],
            device_id_type=MESH,
        )
        copy.start()
        copies.append(copy)
    to_smem.wait()
    depart.wait()

    def place_block(j, carry):
        moved[j] = cat[slot_smem[0, j]]
        return carry

    lax.fori_loop(0, blocks, place_block, 0)
    keep = pltpu.make_async_copy(moved, cols_ref.at[0], local_sem)
    keep.start()
    for at, device in ((1, ahead), (2, down), (3, up)):
        copy = pltpu.make_async_remote_copy(
            src_ref=moved,
            dst_ref=cols_ref.at[at],
            send_sem=col_send.at[at - 1],
            recv_sem=col_recv.at[at - 1],
            device_id=device,
            device_id_type=MESH,
        )
        copy.start()
        copies.append(copy)
    keep.wait()
    for copy in copies:
        copy.wait()


def rows_of(base, c):
    return pl.ds(base * 8 + c, 8, 8)


def tile(i):
    return pl.ds(pl.multiple_of(i * 8, 8), 8)


def build_tables(cols_ref, U, V, L, RT, extra, pieces, start, step):
    rows = iota((8, 128), 0)
    eye = (iota((128, 128), 0) == iota((128, 128), 1)).astype(bf16)
    c6 = jnp.where(rows == 6, 1.0, 0.0)
    c7 = jnp.where(rows == 7, 0.25, 0.0)
    ca = jnp.where(rows < 3, -2.0, 0.0)
    cb = jnp.where(rows < 6, -0.25, 0.0)
    ones = jnp.where(rows < 6, 1.0, 0.0)

    def dense(base):
        x = [cols_ref[rows_of(base, c), :] for c in range(3)]
        v = [cols_ref[rows_of(base, c), :] for c in range(3, 6)]
        radius = cols_ref[rows_of(base, 7), :]
        root = jnp.sqrt(radius)
        square = x[0] * x[0] + x[1] * x[1] + x[2] * x[2] + 0.5 * soften
        dot = x[0] * v[0] + x[1] * v[1] + x[2] * v[2]
        extra[rows_of(base, 3), :] = jnp.ones((8, 128), f32)
        extra[rows_of(base, 4), :] = root * cols_ref[rows_of(base, 6), :]
        extra[rows_of(base, 5), :] = root
        extra[rows_of(base, 6), :] = square
        extra[rows_of(base, 7), :] = dot
        for c, piece in enumerate(split3(square) + split3(0.25 * dot)):
            pieces[rows_of(base, c), :] = piece
        return radius

    def swap(value):
        return jnp.where(rows < 3, pltpu.roll(value, 5, 0), pltpu.roll(value, 3, 0))

    def eight(base, shift, want_u, radius):
        naturals = []
        for q in range(8):
            i = base + q
            S = cols_ref[tile(i), :]
            E = extra[tile(i), :]
            G = pieces[tile(i), :]
            hi, mid = split2(jnp.where(rows < 3, S, jnp.where(rows < 6, E, 0.0)))
            L[i] = jnp.concatenate([hi, mid], axis=0).astype(bf16)
            full = jnp.where(rows < 6, S, E)
            hi, mid = split2(full)
            if want_u:
                low = jnp.where(rows < 6, hi, full - hi - mid)
                naturals.append(jnp.concatenate([hi, low, mid, ones], axis=0).astype(bf16))
            a0 = hi * ca + c6
            a1 = mid * ca + c6
            b0 = swap(hi) * cb + c7
            b1 = swap(mid) * cb + c7
            A = jnp.concatenate([a0, a1, a0, jnp.where(rows < 3, G, 0.0)], axis=0)
            B = jnp.concatenate(
                [b0, b1, b0, jnp.where((rows >= 3) & (rows < 6), G, 0.0)], axis=0
            )
            V[i + shift, :, 0:128] = A.astype(bf16)
            V[i + shift, :, 128:256] = B.astype(bf16)
        if want_u:
            turned = dot_tt(eye, jnp.concatenate(naturals, axis=0))
            for q in range(8):
                U[base + q] = turned[:, 32 * q : 32 * q + 32].astype(bf16)
            RT[lax.shift_right_logical(base, 3), :, 0:8] = radius.T

    def body(t, carry):
        radius = [dense(96 * col + 8 * t) for col in range(4)]
        eight(8 * t, 0, True, radius[0])
        eight(96 + 8 * t, 192, True, radius[1])
        eight(192 + 8 * t, -96, False, None)
        eight(288 + 8 * t, -96, False, None)
        return step(step(carry))

    return lax.fori_loop(0, cols_ref.shape[0] // 256, body, start)


def shares(wide):
    rows = iota((8, 128), 0)

    def chain(load):
        local = jnp.where(rows < 7, pltpu.roll(load, 64, 1), 0.0)

        def step(given):
            now = load - given + pltpu.roll(given, 1, 0)
            change = 0.48 * (now - pltpu.roll(now, 7, 0))
            return jnp.minimum(jnp.maximum(given + change, 0.0), local)

        return step

    own = chain(wide[1:9, :])
    behind = chain(wide[0:8, :])

    def step(given):
        return own(given[0]), behind(given[1])

    def value(given):
        picked = (rows == reach - 1) & (iota((8, 128), 1) == 0)
        return jnp.sum(jnp.where(picked, given, 0.0)).astype(i32)

    start = jnp.zeros((8, 128), f32)
    return (start, start), step, value


def pair_kernel(
    lists_hbm,
    cols_hbm,
    wide_hbm,
    moved_ref,
    own_ref,
    sides_ref,
    lists_ref,
    cols_ref,
    wide,
    U,
    V,
    L,
    RT,
    extra,
    pieces,
    acc,
    sem,
    *rings,
):
    AB = rings[0:ring]
    M = rings[ring : 2 * ring]
    copies = [
        pltpu.make_async_copy(source, target, sem.at[at])
        for at, (source, target) in enumerate(
            ((cols_hbm, cols_ref), (lists_hbm, lists_ref), (wide_hbm, wide))
        )
    ]
    for copy in copies:
        copy.start()
    trash = acc.shape[0] // 8 - 1
    acc[...] = jnp.zeros_like(acc)
    for copy in copies:
        copy.wait()
    keep = pltpu.make_async_copy(cols_ref.at[0:768], moved_ref, sem.at[3])
    keep.start()
    given, step, value = shares(wide)
    given = build_tables(cols_ref, U, V, L, RT, extra, pieces, given, step)
    s_out = value(given[0])
    s_in = value(given[1])

    def begin(at, name):
        return lists_ref[at * 1024 + 6 * 128 + name]

    s_out = jnp.minimum(s_out, begin(0, 1))
    s_in = jnp.minimum(s_in, begin(3, 1))
    ends = []
    shifts = []
    so_far = 0
    for at, low, high in (
        (0, s_out, begin(0, 1)),
        (0, begin(0, 1), begin(0, 2)),
        (1, begin(1, 2), begin(1, 3)),
        (2, begin(2, 3), begin(2, 4)),
        (3, begin(3, 4), begin(3, 5)),
        (3, 0, s_in),
    ):
        shifts.append(at * 1024 + low - so_far)
        so_far = so_far + (high - low)
        ends.append(so_far)
    n = so_far
    last = jnp.maximum(n - 1, 0)

    def entry(k):
        k = jnp.minimum(k, last)
        shift = shifts[5]
        for at in range(4, -1, -1):
            shift = jnp.where(k < ends[at], shifts[at], shift)
        code = lists_ref[k + shift]
        code = code + jnp.where(k < ends[4], 0, 96 + 256 * 288)
        return code & 255, lax.shift_right_logical(code, 8)

    def spot(v):
        return jnp.where(v < 96, v, jnp.where(v < 288, v + 96, v - 192))

    def distances(k, at):
        u, v = entry(k)
        AB[at][...] = jnp.dot(U[u], V[v], preferred_element_type=f32)

    def weights(k, at):
        u, v = entry(k)
        rt = cols_ref[pl.ds(spot(v) * 8 + 7, 1), :]
        lane = jnp.full((8, 128), u & 7, i32)
        eighth = lax.shift_right_logical(u, 3)

        def radius(r):
            return jnp.take_along_axis(RT[eighth, r : r + 8, :], lane, axis=1)

        for r in range(0, 128, 16):
            A = AB[at][r : r + 16, 0:128]
            B = AB[at][r : r + 16, 128:256]
            R = jnp.concatenate([radius(r), radius(r + 8)], axis=0) + rt
            inv = lax.rsqrt(A)
            gap = R - A * inv
            inter = jnp.maximum(gap, 0.0)
            root = inter * lax.rsqrt(jnp.maximum(gap, tiny))
            W = (root * inv) * (inter - B * inv)
            G = root * lax.rsqrt(R)
            wh = W.astype(bf16)
            gh = G.astype(bf16)
            M[at][r : r + 16, 0:128] = wh
            M[at][r : r + 16, 128:256] = gh
            M[at][128 + r : 144 + r, 0:128] = (W - wh.astype(f32)).astype(bf16)
            M[at][128 + r : 144 + r, 128:256] = (G - gh.astype(f32)).astype(bf16)

    rows = iota((8, 128), 0)

    def folded(out):
        both = out[0:8] + out[8:16]
        return jnp.where(rows < 4, both[:, 0:128], both[:, 128:256])

    def sums(k, at):
        u, v = entry(k)
        w = spot(v)
        first = jnp.concatenate([L[u], L[u]], axis=1)
        second = jnp.concatenate([L[w], L[w]], axis=1)
        m = M[at]
        crossed = jnp.concatenate(
            [
                jnp.concatenate([m[0:128, 0:128], m[128:256, 0:128]], axis=1),
                jnp.concatenate([m[0:128, 128:256], m[128:256, 128:256]], axis=1),
            ],
            axis=0,
        )
        to_second = folded(jnp.dot(first, m[...], preferred_element_type=f32))
        to_first = folded(dot_tt(second, crossed))
        live = k < n
        u = jnp.where(live, u, trash)
        w = jnp.where(live, w, trash)
        acc[tile(u), :] += to_first
        acc[tile(w), :] += to_second

    for q in range(ring):
        distances(q, q)
    for q in range(lag_b):
        weights(q, q)

    def turn(t, carry):
        for q in range(group):
            k = t * group + q
            sums(k, q % ring)
            weights(k + lag_b, (q + lag_b) % ring)
            distances(k + ring, q % ring)
        return carry

    lax.fori_loop(0, lax.div(n + group - 1, group), turn, 0)

    def close(base, out_ref, out_base):
        got = [acc[rows_of(base, c), :] for c in range(6)]
        terms = []
        for c in range(3):
            hi, mid = split2(cols_ref[rows_of(base, c), :])
            terms.append(stiffness * ((hi + mid) * got[3] - got[c]))
        root = conductance * extra[rows_of(base, 5), :]
        terms.append(root * (got[4] - cols_ref[rows_of(base, 6), :] * got[5]))
        for c in range(4):
            out_ref[pl.ds(out_base + c, 8, 4), :] = terms[c]

    def close_all(t, carry):
        close(8 * t, own_ref, 32 * t)
        for side in range(3):
            close(96 * (side + 1) + 8 * t, sides_ref, 384 * side + 32 * t)
        return carry

    lax.fori_loop(0, 12, close_all, 0)
    keep.wait()


def finish_kernel(
    moved_hbm,
    own_hbm,
    sides_ref,
    flags_hbm,
    cells_hbm,
    table_hbm,
    rates_ref,
    fluid_ref,
    moved_ref,
    own_ref,
    flags_ref,
    cells_ref,
    table_ref,
    in_sem,
    got,
    heat_in,
    to_fluid,
    sums,
    send,
    recv,
):
    ahead, behind, up, down = neighbours()
    inputs = [
        pltpu.make_async_copy(source, target, in_sem.at[at])
        for at, (source, target) in enumerate(
            (
                (moved_hbm, moved_ref),
                (flags_hbm, flags_ref),
                (cells_hbm, cells_ref),
                (table_hbm, table_ref),
                (own_hbm, own_ref),
            )
        )
    ]
    for copy in inputs:
        copy.start()
    greet((ahead, behind, up, down))
    copies = []
    span = got.shape[1]
    for at, device in ((0, behind), (1, up), (2, down)):
        copy = pltpu.make_async_remote_copy(
            src_ref=sides_ref.at[span * at : span * at + span],
            dst_ref=got.at[at],
            send_sem=send.at[at],
            recv_sem=recv.at[at],
            device_id=device,
            device_id_type=MESH,
        )
        copy.start()
        copies.append(copy)

    for copy in inputs:
        copy.wait()
    square = jnp.concatenate([table_ref[:, 16 * a : 16 * a + 16] for a in range(16)], axis=0)
    table = jnp.concatenate(split3(square), axis=0).astype(bf16)
    sums[...] = jnp.zeros_like(sums)
    sub = iota((16, 128), 0)

    def cells_of(g, carry):
        at = pl.ds(pl.multiple_of(g * 8, 8), 8)
        temper = moved_ref[rows_of(g * 8, 6), :]
        radius = moved_ref[rows_of(g * 8, 7), :]
        volume = 4.0 / 3.0 * math.pi * radius * radius * radius
        cell = cells_ref[at, :]
        high = lax.shift_right_logical(cell, 4)
        low = cell & 15
        fluid = []
        hots = []
        for c in range(8):
            hot_high = (sub == high[c : c + 1]).astype(f32)
            hot_low = (sub == low[c : c + 1]).astype(f32)
            parts = jnp.dot(table, hot_low.astype(bf16), preferred_element_type=f32)
            value = parts[0:16] + parts[16:32] + parts[32:48]
            fluid.append(jnp.sum(value * hot_high, axis=0, keepdims=True))
            hots.append((hot_high, hot_low))
        flow = film_gain * radius * radius * (temper - jnp.concatenate(fluid, axis=0))
        to_fluid[at, :] = flow
        pieces = split3(volume) + split3(flow)
        total = sums[...]
        for c in range(8):
            hot_high, hot_low = hots[c]
            spread = jnp.concatenate([hot_low * piece[c : c + 1] for piece in pieces], axis=0)
            total = total + dot_tt(hot_high.astype(bf16), spread.astype(bf16))
        sums[...] = total
        wall = wall_gain * flags_ref[at, :].astype(f32) * (wall_temp - temper) * radius
        heat_in[at, :] = wall - flow
        return carry

    lax.fori_loop(0, 12, cells_of, 0)
    total = sums[...]
    solid = (total[:, 0:16] + total[:, 16:32] + total[:, 32:48]) / cell_volume
    heat = total[:, 48:64] + total[:, 64:80] + total[:, 80:96]
    for a in range(16):
        fluid_ref[0:1, 16 * a : 16 * a + 16] = solid[a : a + 1]
        fluid_ref[1:2, 16 * a : 16 * a + 16] = heat[a : a + 1]
    for copy in copies:
        copy.wait()

    def combine(g, carry):
        at = pl.ds(pl.multiple_of(g * 8, 8), 8)
        radius = moved_ref[rows_of(g * 8, 7), :]
        volume = 4.0 / 3.0 * math.pi * radius * radius * radius
        inverse = 1.0 / volume
        for c in range(4):
            here = pl.ds(g * 32 + c, 8, 4)
            value = own_ref[here, :]
            for side in range(3):
                value = value + got[side, here, :]
            if c == 3:
                value = value + heat_in[at, :]
            value = value * inverse
            if c == 2:
                value = value - gravity
            rates_ref[here, :] = value
        return carry

    lax.fori_loop(0, 12, combine, 0)


def anywhere():
    return pl.BlockSpec(memory_space=pl.ANY)


def vmem():
    return pl.BlockSpec(memory_space=pltpu.VMEM)


def shards(state, leaving, pairs, counts, wall_flags, cell_index, fluid_temp):
    mine = state[0, 0]
    blocks = mine.shape[0]
    count = leaving.shape[2]
    lanes = -(-pairs.shape[3] // 128) * 128
    cols, lists, wide = pl.pallas_call(
        halo_kernel,
        out_shape=(
            jax.ShapeDtypeStruct((4, blocks, 8, 128), f32),
            jax.ShapeDtypeStruct((4, 8, 128), i32),
            jax.ShapeDtypeStruct((16, 128), f32),
        ),
        in_specs=[anywhere()] * 4,
        out_specs=(anywhere(), vmem(), vmem()),
        scratch_shapes=[
            pltpu.SMEM(leaving.shape[2:], i32),
            pltpu.SMEM(counts.shape[2:], i32),
            pltpu.VMEM(pairs.shape[2:], i32),
            pltpu.VMEM((count + blocks, 8, 128), f32),
            pltpu.VMEM((count, 8, 128), f32),
            pltpu.VMEM((blocks, 8, 128), f32),
            pltpu.VMEM((8, lanes), i32),
            pltpu.VMEM((8, 128), i32),
            pltpu.SMEM((8, 128), i32),
            pltpu.SemaphoreType.DMA,
            pltpu.SemaphoreType.DMA,
            pltpu.SemaphoreType.DMA((3,)),
            pltpu.SemaphoreType.DMA((3,)),
            pltpu.SemaphoreType.DMA((3,)),
            pltpu.SemaphoreType.DMA((3,)),
            pltpu.SemaphoreType.DMA,
            pltpu.SemaphoreType.DMA((4,)),
            pltpu.VMEM((8, 128), f32),
            pltpu.SemaphoreType.DMA((3,)),
            pltpu.SemaphoreType.DMA((3,)),
            pltpu.SemaphoreType.DMA((2 * reach,)),
            pltpu.SemaphoreType.DMA((2 * reach,)),
        ],
        compiler_params=pltpu.CompilerParams(
            collective_id=0, has_side_effects=True, vmem_limit_bytes=vmem_grant
        ),
        name="halo",
    )(leaving[0, 0], counts[0, 0], pairs[0, 0], mine)

    moved, own, sides = pl.pallas_call(
        pair_kernel,
        out_shape=(
            jax.ShapeDtypeStruct((8 * blocks, 128), f32),
            jax.ShapeDtypeStruct((4 * blocks, 128), f32),
            jax.ShapeDtypeStruct((12 * blocks, 128), f32),
        ),
        in_specs=[anywhere()] * 3,
        out_specs=(anywhere(), vmem(), vmem()),
        scratch_shapes=[
            pltpu.SMEM((4096,), i32),
            pltpu.VMEM((32 * blocks, 128), f32),
            pltpu.VMEM((16, 128), f32),
            pltpu.VMEM((2 * blocks, 128, 32), bf16),
            pltpu.VMEM((4 * blocks, 32, 256), bf16),
            pltpu.VMEM((4 * blocks, 16, 128), bf16),
            pltpu.VMEM((blocks // 4, 128, 128), f32),
            pltpu.VMEM((32 * blocks, 128), f32),
            pltpu.VMEM((32 * blocks, 128), f32),
            pltpu.VMEM((32 * blocks + 8, 128), f32),
            pltpu.SemaphoreType.DMA((4,)),
        ]
        + [pltpu.VMEM((128, 256), f32)] * ring
        + [pltpu.VMEM((256, 256), bf16)] * ring,
        compiler_params=pltpu.CompilerParams(vmem_limit_bytes=vmem_grant),
        name="contact",
    )(lists.reshape(4096), cols.reshape(32 * blocks, 128), wide)

    rates, fluid = pl.pallas_call(
        finish_kernel,
        out_shape=(
            jax.ShapeDtypeStruct((4 * blocks, 128), f32),
            jax.ShapeDtypeStruct((2, 256), f32),
        ),
        in_specs=[anywhere()] * 6,
        out_specs=(vmem(), vmem()),
        scratch_shapes=[
            pltpu.VMEM((8 * blocks, 128), f32),
            pltpu.VMEM((4 * blocks, 128), f32),
            pltpu.VMEM((blocks, 128), i32),
            pltpu.VMEM((blocks, 128), i32),
            pltpu.VMEM((1, 256), f32),
            pltpu.SemaphoreType.DMA((5,)),
            pltpu.VMEM((3, 4 * blocks, 128), f32),
            pltpu.VMEM((blocks, 128), f32),
            pltpu.VMEM((blocks, 128), f32),
            pltpu.VMEM((16, 96), f32),
            pltpu.SemaphoreType.DMA((3,)),
            pltpu.SemaphoreType.DMA((3,)),
        ],
        compiler_params=pltpu.CompilerParams(
            collective_id=1, has_side_effects=True, vmem_limit_bytes=vmem_grant
        ),
        name="finish",
    )(
        moved,
        own,
        sides,
        wall_flags[0, 0],
        cell_index[0, 0],
        fluid_temp.reshape(1, 256),
    )
    return (
        moved.reshape(1, 1, blocks, 8, 128),
        rates.reshape(1, 1, blocks, 4, 128),
        fluid[None, None],
    )


def solution(mesh):
    in_specs = (
        P("gx", "gy", None, None, None),
        P("gx", "gy", None),
        P("gx", "gy", None, None),
        P("gx", "gy", None),
        P("gx", "gy", None, None),
        P("gx", "gy", None, None),
        P("gx", "gy", None),
    )
    out_specs = (
        P("gx", "gy", None, None, None),
        P("gx", "gy", None, None, None),
        P("gx", "gy", None, None),
    )
    return jax.shard_map(shards, mesh=mesh, in_specs=in_specs, out_specs=out_specs, check_vma=False)
```

```python
import functools
import math

import jax
import jax.numpy as jnp
from jax import lax
from jax.experimental import pallas as pl
from jax.experimental.pallas import tpu as pltpu
from jax.sharding import PartitionSpec as P

soften = 0.01
stiffness = 0.2
damping = 0.05
conductance = 0.05
film_gain = 0.5
wall_gain = 2.0
wall_temp = 1.0
gravity = 1.0
cell_volume = 32.0

f32 = jnp.float32
bf16 = jnp.bfloat16
i32 = jnp.int32

tiny = 1e-30
group = 16
lag_a = 2
lag_b = 2
ring = lag_a + lag_b
reach = 4
vmem_grant = 56 * 2**20
MESH = pl.DeviceIdType.MESH


def iota(shape, dim):
    return lax.broadcasted_iota(i32, shape, dim)


def split2(value):
    hi = value.astype(bf16).astype(f32)
    return hi, (value - hi).astype(bf16).astype(f32)


def split3(value):
    hi = value.astype(bf16).astype(f32)
    rest = value - hi
    mid = rest.astype(bf16).astype(f32)
    return hi, mid, rest - mid


def dot_tt(left, right):
    return lax.dot_general(left, right, (((1,), (1,)), ((), ())), preferred_element_type=f32)


def neighbours():
    a = lax.axis_index("gx")
    b = lax.axis_index("gy")
    na = lax.axis_size("gx")
    nb = lax.axis_size("gy")
    return (
        {"gx": lax.rem(a + 1, na)},
        {"gx": lax.rem(a + na - 1, na)},
        {"gy": lax.rem(b + 1, nb)},
        {"gy": lax.rem(b + nb - 1, nb)},
    )


def greet(everyone):
    barrier = pltpu.get_barrier_semaphore()
    for device in everyone:
        pl.semaphore_signal(barrier, inc=1, device_id=device, device_id_type=MESH)
    pl.semaphore_wait(barrier, len(everyone))


def sort_pairs(lanes, pad, total):
    own = pad[0:1, :]
    code = pad[1:2, :]
    region = jnp.zeros_like(code)
    for step in range(1, 9):
        region = region + (code >= 96 * step).astype(i32)
    far = code - 96 * region
    live = iota((1, lanes), 1) < total

    def among(*names):
        hit = region == names[0]
        for name in names[1:]:
            hit = hit | (region == name)
        return hit

    kind = jnp.where(
        among(4),
        0,
        jnp.where(among(1, 5), 1, jnp.where(among(0, 3), 2, jnp.where(among(2), 3, 4))),
    )
    kind = jnp.where(live, kind, 5)
    u_far = among(0, 1, 2, 3)
    u = jnp.where(u_far, far, own) + jnp.where(among(4, 5, 3), 0, 96)
    v_slot = jnp.where(u_far, own, far)
    v_side = jnp.where(among(4, 1, 7), 0, jnp.where(among(5, 3, 0, 8), 1, 2))
    ranks = iota((8, lanes), 0)
    marks = (ranks == kind).astype(f32)
    before = (iota((lanes, lanes), 0) < iota((lanes, lanes), 1)).astype(bf16)
    seen = jnp.dot(marks.astype(bf16), before, preferred_element_type=f32)
    starts = jnp.sum((kind < ranks).astype(f32), axis=1, keepdims=True)
    place = jnp.sum(marks * (seen + starts), axis=0, keepdims=True)
    target = (iota((lanes, lanes), 0).astype(f32) == place).astype(bf16)
    rows = iota((8, lanes), 0)
    values = jnp.where(
        rows == 0, u, jnp.where(rows == 1, v_slot, jnp.where(rows == 2, v_side, 0))
    )
    moved = dot_tt(values.astype(bf16), target)
    packed = moved[0:1] + 512.0 * (moved[1:2] + 96.0 * moved[2:3])
    diag = iota((8, 128), 0) == iota((8, 128), 1)
    begin = jnp.sum(jnp.where(diag, starts, 0.0), axis=0, keepdims=True)
    return packed.astype(i32), begin.astype(i32)


def halo_kernel(
    leaving_hbm,
    counts_hbm,
    pairs_hbm,
    state_hbm,
    cols_ref,
    lists_ref,
    wide_ref,
    leaving_ref,
    counts_ref,
    pairs_ref,
    cat,
    dep,
    moved,
    pad,
    slot_vec,
    slot_smem,
    dep_send,
    dep_recv,
    list_send,
    list_recv,
    col_send,
    col_recv,
    local_sem,
    in_sem,
    near,
    near_send,
    near_recv,
    wide_send,
    wide_recv,
):
    blocks = state_hbm.shape[0]
    count = leaving_hbm.shape[0]
    ahead, behind, up, down = neighbours()
    state_ref = cat.at[count : count + blocks]
    inputs = [
        pltpu.make_async_copy(source, target, in_sem.at[at])
        for at, (source, target) in enumerate(
            (
                (leaving_hbm, leaving_ref),
                (state_hbm, state_ref),
                (pairs_hbm, pairs_ref),
                (counts_hbm, counts_ref),
            )
        )
    ]
    for copy in inputs:
        copy.start()
    a = lax.axis_index("gx")
    na = lax.axis_size("gx")
    along = {
        step: {"gx": lax.rem(a + step + na, na)} for step in range(-reach, reach + 1) if step
    }
    wide_ref[...] = jnp.zeros_like(wide_ref)
    for copy in inputs:
        copy.wait()
    local = counts_ref[0].astype(f32)
    far = (counts_ref[1] - counts_ref[0]).astype(f32) * 0.125
    near[0:1, :] = jnp.full((1, 128), far)
    for m in range(count):
        dep[m] = state_ref[leaving_ref[m]]
    b = lax.axis_index("gy")
    nb = lax.axis_size("gy")
    across = {"gy": lax.rem(b + 2, nb)}
    greet((up, down, across, *along.values()))
    depart = pltpu.make_async_remote_copy(
        src_ref=dep,
        dst_ref=cat.at[0:count],
        send_sem=dep_send,
        recv_sem=dep_recv,
        device_id=ahead,
        device_id_type=MESH,
    )
    depart.start()
    asks = []
    for at, device in ((1, down), (2, up), (3, ahead)):
        copy = pltpu.make_async_remote_copy(
            src_ref=near.at[0:1],
            dst_ref=near.at[at : at + 1],
            send_sem=near_send.at[at - 1],
            recv_sem=near_recv.at[at - 1],
            device_id=device,
            device_id_type=MESH,
        )
        copy.start()
        asks.append(copy)
    for copy in asks:
        copy.wait()
    lane = iota((1, 128), 1)
    load = local + 2.0 * far + 2.0 * near[1:2, :] + near[2:3, :] + 3.0 * near[3:4, :]
    near[4:5, :] = jnp.where(lane < 64, load, local)
    tells = []
    for at, device in ((5, down), (6, up), (7, across)):
        copy = pltpu.make_async_remote_copy(
            src_ref=near.at[4:5],
            dst_ref=near.at[at : at + 1],
            send_sem=near_send.at[at - 2],
            recv_sem=near_recv.at[at - 2],
            device_id=device,
            device_id_type=MESH,
        )
        copy.start()
        tells.append(copy)
    place = iota((8, 128), 1)
    slot = place + count
    for m in range(count):
        slot = jnp.where(place == leaving_ref[m], m, slot)
    slot_vec[...] = slot
    to_smem = pltpu.make_async_copy(slot_vec, slot_smem, local_sem)
    to_smem.start()
    lanes = pad.shape[1]
    pad[...] = jnp.zeros_like(pad)
    pad[0:2, 0 : pairs_ref.shape[1]] = pairs_ref[...]
    packed, begin = sort_pairs(lanes, pad, counts_ref[1])
    lists_ref[0] = jnp.zeros((8, 128), i32)
    for row in range(lanes // 128):
        lists_ref[0, row : row + 1, :] = packed[:, 128 * row : 128 * row + 128]
    lists_ref[0, 6:7, :] = begin
    copies = []
    for at, device in ((1, down), (2, up), (3, ahead)):
        copy = pltpu.make_async_remote_copy(
            src_ref=lists_ref.at[0],
            dst_ref=lists_ref.at[at],
            send_sem=list_send.at[at - 1],
            recv_sem=list_recv.at[at - 1],
            device_id=device,
            device_id_type=MESH,
        )
        copy.start()
        copies.append(copy)
    for copy in tells:
        copy.wait()
    turn = lane & 3
    row = near[4:5, :]
    for at, step in ((5, 1), (6, nb - 1), (7, 2)):
        row = jnp.where(turn == lax.rem(b + step, nb), near[at : at + 1, :], row)
    wide_ref[reach : reach + 1, :] = row
    for at, step in enumerate(along):
        copy = pltpu.make_async_remote_copy(
            src_ref=wide_ref.at[reach : reach + 1],
            dst_ref=wide_ref.at[reach - step : reach - step + 1],
            send_sem=wide_send.at[at],
            recv_sem=wide_recv.at[at],
            device_id=along[step],
            device_id_type=MESH,
        )
        copy.start()
        copies.append(copy)
    to_smem.wait()
    depart.wait()

    def place_block(j, carry):
        moved[j] = cat[slot_smem[0, j]]
        return carry

    lax.fori_loop(0, blocks, place_block, 0)
    keep = pltpu.make_async_copy(moved, cols_ref.at[0], local_sem)
    keep.start()
    for at, device in ((1, ahead), (2, down), (3, up)):
        copy = pltpu.make_async_remote_copy(
            src_ref=moved,
            dst_ref=cols_ref.at[at],
            send_sem=col_send.at[at - 1],
            recv_sem=col_recv.at[at - 1],
            device_id=device,
            device_id_type=MESH,
        )
        copy.start()
        copies.append(copy)
    keep.wait()
    for copy in copies:
        copy.wait()


def rows_of(base, c):
    return pl.ds(base * 8 + c, 8, 8)


def tile(i):
    return pl.ds(pl.multiple_of(i * 8, 8), 8)


def build_tables(cols_ref, U, V, L, RT, extra, pieces, start, step):
    rows = iota((8, 128), 0)
    eye = (iota((128, 128), 0) == iota((128, 128), 1)).astype(bf16)
    c6 = jnp.where(rows == 6, 1.0, 0.0)
    c7 = jnp.where(rows == 7, 0.25, 0.0)
    ca = jnp.where(rows < 3, -2.0, 0.0)
    cb = jnp.where(rows < 6, -0.25, 0.0)
    ones = jnp.where(rows < 6, 1.0, 0.0)

    def dense(base):
        x = [cols_ref[rows_of(base, c), :] for c in range(3)]
        v = [cols_ref[rows_of(base, c), :] for c in range(3, 6)]
        radius = cols_ref[rows_of(base, 7), :]
        root = jnp.sqrt(radius)
        square = x[0] * x[0] + x[1] * x[1] + x[2] * x[2] + 0.5 * soften
        dot = x[0] * v[0] + x[1] * v[1] + x[2] * v[2]
        extra[rows_of(base, 3), :] = jnp.ones((8, 128), f32)
        extra[rows_of(base, 4), :] = root * cols_ref[rows_of(base, 6), :]
        extra[rows_of(base, 5), :] = root
        extra[rows_of(base, 6), :] = square
        extra[rows_of(base, 7), :] = dot
        for c, piece in enumerate(split3(square) + split3(0.25 * dot)):
            pieces[rows_of(base, c), :] = piece
        return radius

    def swap(value):
        return jnp.where(rows < 3, pltpu.roll(value, 5, 0), pltpu.roll(value, 3, 0))

    def eight(base, shift, u_base, radius):
        naturals = []
        for q in range(8):
            i = base + q
            S = cols_ref[tile(i), :]
            E = extra[tile(i), :]
            G = pieces[tile(i), :]
            hi, mid = split2(jnp.where(rows < 3, S, jnp.where(rows < 6, E, 0.0)))
            L[i] = jnp.concatenate([hi, mid], axis=0).astype(bf16)
            full = jnp.where(rows < 6, S, E)
            hi, mid = split2(full)
            if u_base is not None:
                low = jnp.where(rows < 6, hi, full - hi - mid)
                naturals.append(jnp.concatenate([hi, low, mid, ones], axis=0).astype(bf16))
            a0 = hi * ca + c6
            a1 = mid * ca + c6
            b0 = swap(hi) * cb + c7
            b1 = swap(mid) * cb + c7
            A = jnp.concatenate([a0, a1, a0, jnp.where(rows < 3, G, 0.0)], axis=0)
            B = jnp.concatenate(
                [b0, b1, b0, jnp.where((rows >= 3) & (rows < 6), G, 0.0)], axis=0
            )
            V[i + shift, :, 0:128] = A.astype(bf16)
            V[i + shift, :, 128:256] = B.astype(bf16)
        if u_base is not None:
            turned = dot_tt(eye, jnp.concatenate(naturals, axis=0))
            for q in range(8):
                U[u_base + q] = turned[:, 32 * q : 32 * q + 32].astype(bf16)
            RT[lax.shift_right_logical(u_base, 3), :, 0:8] = radius.T

    def body(t, carry):
        radius = [dense(96 * col + 8 * t) for col in range(4)]
        eight(8 * t, 0, 8 * t, radius[0])
        eight(96 + 8 * t, 192, 96 + 8 * t, radius[1])
        eight(192 + 8 * t, -96, None, None)
        eight(288 + 8 * t, -96, 192 + 8 * t, radius[3])
        return step(step(carry))

    return lax.fori_loop(0, cols_ref.shape[0] // 256, body, start)


def shares(wide):
    rows = iota((8, 128), 0)
    lanes = iota((8, 128), 1)
    b = lax.axis_index("gy")
    nb = lax.axis_size("gy")

    def chain(load):
        local = pltpu.roll(load, 64, 1)
        passing = jnp.where(rows < 7, local, 0.0)

        def step(given):
            ahead, up = given
            now = load - ahead - up + pltpu.roll(ahead, 1, 0) + pltpu.roll(up, 1, 1)
            ahead = ahead + 0.24 * (now - pltpu.roll(now, 7, 0))
            ahead = jnp.minimum(jnp.maximum(ahead, 0.0), jnp.maximum(passing - up, 0.0))
            up = up + 0.24 * (now - pltpu.roll(now, 127, 1))
            up = jnp.minimum(jnp.maximum(up, 0.0), jnp.maximum(local - ahead, 0.0))
            return ahead, up

        return step

    own = chain(wide[1:9, :])
    behind = chain(wide[0:8, :])

    def step(given):
        return own(given[0]), behind(given[1])

    def value(given, shift):
        column = lax.rem(b + shift + nb, nb)
        picked = (rows == reach - 1) & (lanes == column + 32)
        return jnp.sum(jnp.where(picked, given, 0.0)).astype(i32)

    start = jnp.zeros((8, 128), f32)
    return ((start, start), (start, start)), step, value


def pair_kernel(
    lists_hbm,
    cols_hbm,
    wide_hbm,
    moved_ref,
    own_ref,
    sides_ref,
    lists_ref,
    cols_ref,
    wide,
    U,
    V,
    L,
    RT,
    extra,
    pieces,
    acc,
    sem,
    *rings,
):
    AB = rings[0:ring]
    M = rings[ring : 2 * ring]
    copies = [
        pltpu.make_async_copy(source, target, sem.at[at])
        for at, (source, target) in enumerate(
            ((cols_hbm, cols_ref), (lists_hbm, lists_ref), (wide_hbm, wide))
        )
    ]
    for copy in copies:
        copy.start()
    trash = acc.shape[0] // 8 - 1
    acc[...] = jnp.zeros_like(acc)
    for copy in copies:
        copy.wait()
    keep = pltpu.make_async_copy(cols_ref.at[0:768], moved_ref, sem.at[3])
    keep.start()
    given, step, value = shares(wide)
    given = build_tables(cols_ref, U, V, L, RT, extra, pieces, given, step)
    ahead_out = value(given[0][0], 0)
    up_out = value(given[0][1], 0)
    ahead_in = value(given[1][0], 0)
    ahead_down = value(given[0][0], -1)
    up_in = value(given[0][1], -1)

    def begin(at, name):
        return lists_ref[at * 1024 + 6 * 128 + name]

    def cut(at, first, second):
        first = jnp.minimum(first, begin(at, 1))
        return first, jnp.minimum(first + second, begin(at, 1))

    _, kept = cut(0, ahead_out, up_out)
    ahead_in = jnp.minimum(ahead_in, begin(3, 1))
    up_low, up_high = cut(2, ahead_down, up_in)
    ends = []
    shifts = []
    so_far = 0
    for at, low, high in (
        (0, kept, begin(0, 1)),
        (0, begin(0, 1), begin(0, 2)),
        (1, begin(1, 2), begin(1, 3)),
        (2, begin(2, 3), begin(2, 4)),
        (3, begin(3, 4), begin(3, 5)),
        (3, 0, ahead_in),
        (2, up_low, up_high),
    ):
        shifts.append(at * 1024 + low - so_far)
        so_far = so_far + (high - low)
        ends.append(so_far)
    n = so_far
    last = jnp.maximum(n - 1, 0)

    def entry(k):
        k = jnp.minimum(k, last)
        shift = shifts[6]
        for at in range(5, -1, -1):
            shift = jnp.where(k < ends[at], shifts[at], shift)
        code = lists_ref[k + shift]
        code = code + jnp.where(
            k < ends[4], 0, jnp.where(k < ends[5], 96 + 512 * 288, 192 + 512 * 192)
        )
        return code & 511, lax.shift_right_logical(code, 9)

    def spot_u(u):
        return jnp.where(u < 192, u, u + 96)

    def spot(v):
        return jnp.where(v < 96, v, jnp.where(v < 288, v + 96, v - 192))

    def distances(k, at):
        u, v = entry(k)
        AB[at][...] = jnp.dot(U[u], V[v], preferred_element_type=f32)

    def weights(k, at):
        u, v = entry(k)
        rt = cols_ref[pl.ds(spot(v) * 8 + 7, 1), :]
        lane = jnp.full((8, 128), u & 7, i32)
        eighth = lax.shift_right_logical(u, 3)

        def radius(r):
            return jnp.take_along_axis(RT[eighth, r : r + 8, :], lane, axis=1)

        for r in range(0, 128, 16):
            A = AB[at][r : r + 16, 0:128]
            B = AB[at][r : r + 16, 128:256]
            R = jnp.concatenate([radius(r), radius(r + 8)], axis=0) + rt
            inv = lax.rsqrt(A)
            gap = R - A * inv
            inter = jnp.maximum(gap, 0.0)
            root = inter * lax.rsqrt(jnp.maximum(gap, tiny))
            W = (root * inv) * (inter - B * inv)
            G = root * lax.rsqrt(R)
            wh = W.astype(bf16)
            gh = G.astype(bf16)
            M[at][r : r + 16, 0:128] = wh
            M[at][r : r + 16, 128:256] = gh
            M[at][128 + r : 144 + r, 0:128] = (W - wh.astype(f32)).astype(bf16)
            M[at][128 + r : 144 + r, 128:256] = (G - gh.astype(f32)).astype(bf16)

    rows = iota((8, 128), 0)

    def folded(out):
        both = out[0:8] + out[8:16]
        return jnp.where(rows < 4, both[:, 0:128], both[:, 128:256])

    def sums(k, at):
        u, v = entry(k)
        w = spot(v)
        o = spot_u(u)
        first = jnp.concatenate([L[o], L[o]], axis=1)
        second = jnp.concatenate([L[w], L[w]], axis=1)
        m = M[at]
        crossed = jnp.concatenate(
            [
                jnp.concatenate([m[0:128, 0:128], m[128:256, 0:128]], axis=1),
                jnp.concatenate([m[0:128, 128:256], m[128:256, 128:256]], axis=1),
            ],
            axis=0,
        )
        to_second = folded(jnp.dot(first, m[...], preferred_element_type=f32))
        to_first = folded(dot_tt(second, crossed))
        live = k < n
        o = jnp.where(live, o, trash)
        w = jnp.where(live, w, trash)
        acc[tile(o), :] += to_first
        acc[tile(w), :] += to_second

    for q in range(ring):
        distances(q, q)
    for q in range(lag_b):
        weights(q, q)

    def turn(t, carry):
        for q in range(group):
            k = t * group + q
            sums(k, q % ring)
            weights(k + lag_b, (q + lag_b) % ring)
            distances(k + ring, q % ring)
        return carry

    lax.fori_loop(0, lax.div(n + group - 1, group), turn, 0)

    def close(base, out_ref, out_base):
        got = [acc[rows_of(base, c), :] for c in range(6)]
        terms = []
        for c in range(3):
            hi, mid = split2(cols_ref[rows_of(base, c), :])
            terms.append(stiffness * ((hi + mid) * got[3] - got[c]))
        root = conductance * extra[rows_of(base, 5), :]
        terms.append(root * (got[4] - cols_ref[rows_of(base, 6), :] * got[5]))
        for c in range(4):
            out_ref[pl.ds(out_base + c, 8, 4), :] = terms[c]

    def close_all(t, carry):
        close(8 * t, own_ref, 32 * t)
        for side in range(3):
            close(96 * (side + 1) + 8 * t, sides_ref, 384 * side + 32 * t)
        return carry

    lax.fori_loop(0, 12, close_all, 0)
    keep.wait()


def finish_kernel(
    moved_hbm,
    sides_ref,
    flags_hbm,
    cells_hbm,
    table_hbm,
    mix_ref,
    fluid_ref,
    moved_ref,
    flags_ref,
    cells_ref,
    table_ref,
    in_sem,
    sums,
    send,
    recv,
):
    ahead, behind, up, down = neighbours()
    inputs = [
        pltpu.make_async_copy(source, target, in_sem.at[at])
        for at, (source, target) in enumerate(
            (
                (moved_hbm, moved_ref),
                (flags_hbm, flags_ref),
                (cells_hbm, cells_ref),
                (table_hbm, table_ref),
            )
        )
    ]
    for copy in inputs:
        copy.start()
    greet((ahead, behind, up, down))
    copies = []
    span = sides_ref.shape[0] // 3
    blocks = span // 4
    for at, device in ((0, behind), (1, up), (2, down)):
        copy = pltpu.make_async_remote_copy(
            src_ref=sides_ref.at[span * at : span * at + span],
            dst_ref=mix_ref.at[span * at : span * at + span],
            send_sem=send.at[at],
            recv_sem=recv.at[at],
            device_id=device,
            device_id_type=MESH,
        )
        copy.start()
        copies.append(copy)

    for copy in inputs:
        copy.wait()
    square = jnp.concatenate([table_ref[:, 16 * a : 16 * a + 16] for a in range(16)], axis=0)
    table = jnp.concatenate(split3(square), axis=0).astype(bf16)
    sums[...] = jnp.zeros_like(sums)
    sub = iota((16, 128), 0)

    def cells_of(g, carry):
        at = pl.ds(pl.multiple_of(g * 8, 8), 8)
        temper = moved_ref[rows_of(g * 8, 6), :]
        radius = moved_ref[rows_of(g * 8, 7), :]
        volume = 4.0 / 3.0 * math.pi * radius * radius * radius
        cell = cells_ref[at, :]
        high = lax.shift_right_logical(cell, 4)
        low = cell & 15
        fluid = []
        hots = []
        for c in range(8):
            hot_high = (sub == high[c : c + 1]).astype(f32)
            hot_low = (sub == low[c : c + 1]).astype(f32)
            parts = jnp.dot(table, hot_low.astype(bf16), preferred_element_type=f32)
            value = parts[0:16] + parts[16:32] + parts[32:48]
            fluid.append(jnp.sum(value * hot_high, axis=0, keepdims=True))
            hots.append((hot_high, hot_low))
        flow = film_gain * radius * radius * (temper - jnp.concatenate(fluid, axis=0))
        pieces = split3(volume) + split3(flow)
        total = sums[...]
        for c in range(8):
            hot_high, hot_low = hots[c]
            spread = jnp.concatenate([hot_low * piece[c : c + 1] for piece in pieces], axis=0)
            total = total + dot_tt(hot_high.astype(bf16), spread.astype(bf16))
        sums[...] = total
        wall = wall_gain * flags_ref[at, :].astype(f32) * (wall_temp - temper) * radius
        mix_ref[pl.ds(pl.multiple_of(3 * span + g * 8, 8), 8), :] = wall - flow
        mix_ref[pl.ds(pl.multiple_of(3 * span + blocks + g * 8, 8), 8), :] = 1.0 / volume
        return carry

    lax.fori_loop(0, 12, cells_of, 0)
    total = sums[...]
    solid = (total[:, 0:16] + total[:, 16:32] + total[:, 32:48]) / cell_volume
    heat = total[:, 48:64] + total[:, 64:80] + total[:, 80:96]
    for a in range(16):
        fluid_ref[0:1, 16 * a : 16 * a + 16] = solid[a : a + 1]
        fluid_ref[1:2, 16 * a : 16 * a + 16] = heat[a : a + 1]
    for copy in copies:
        copy.wait()


def rates_kernel(
    own_hbm, mix_hbm, fluid_hbm, rates_ref, fluid_ref, own, mix, fluid, sem
):
    copies = [
        pltpu.make_async_copy(source, target, sem.at[at])
        for at, (source, target) in enumerate(
            ((mix_hbm, mix), (own_hbm, own), (fluid_hbm, fluid))
        )
    ]
    for copy in copies:
        copy.start()
    for copy in copies:
        copy.wait()
    fluid_ref[...] = fluid[...]
    span = own.shape[0]
    blocks = span // 4

    def combine(g, carry):
        at = pl.multiple_of(g * 8, 8)
        inverse = mix[pl.ds(3 * span + blocks + at, 8), :]
        for c in range(4):
            here = pl.ds(g * 32 + c, 8, 4)
            value = own[here, :]
            for side in range(3):
                value = value + mix[pl.ds(span * side + g * 32 + c, 8, 4), :]
            if c == 3:
                value = value + mix[pl.ds(3 * span + at, 8), :]
            value = value * inverse
            if c == 2:
                value = value - gravity
            rates_ref[here, :] = value
        return carry

    lax.fori_loop(0, blocks // 8, combine, 0, unroll=4)


def anywhere():
    return pl.BlockSpec(memory_space=pl.ANY)


def vmem():
    return pl.BlockSpec(memory_space=pltpu.VMEM)


def shards(state, leaving, pairs, counts, wall_flags, cell_index, fluid_temp):
    mine = state[0, 0]
    blocks = mine.shape[0]
    count = leaving.shape[2]
    lanes = -(-pairs.shape[3] // 128) * 128
    cols, lists, wide = pl.pallas_call(
        halo_kernel,
        out_shape=(
            jax.ShapeDtypeStruct((4, blocks, 8, 128), f32),
            jax.ShapeDtypeStruct((4, 8, 128), i32),
            jax.ShapeDtypeStruct((16, 128), f32),
        ),
        in_specs=[anywhere()] * 4,
        out_specs=(anywhere(), vmem(), vmem()),
        scratch_shapes=[
            pltpu.SMEM(leaving.shape[2:], i32),
            pltpu.SMEM(counts.shape[2:], i32),
            pltpu.VMEM(pairs.shape[2:], i32),
            pltpu.VMEM((count + blocks, 8, 128), f32),
            pltpu.VMEM((count, 8, 128), f32),
            pltpu.VMEM((blocks, 8, 128), f32),
            pltpu.VMEM((8, lanes), i32),
            pltpu.VMEM((8, 128), i32),
            pltpu.SMEM((8, 128), i32),
            pltpu.SemaphoreType.DMA,
            pltpu.SemaphoreType.DMA,
            pltpu.SemaphoreType.DMA((3,)),
            pltpu.SemaphoreType.DMA((3,)),
            pltpu.SemaphoreType.DMA((3,)),
            pltpu.SemaphoreType.DMA((3,)),
            pltpu.SemaphoreType.DMA,
            pltpu.SemaphoreType.DMA((4,)),
            pltpu.VMEM((8, 128), f32),
            pltpu.SemaphoreType.DMA((6,)),
            pltpu.SemaphoreType.DMA((6,)),
            pltpu.SemaphoreType.DMA((2 * reach,)),
            pltpu.SemaphoreType.DMA((2 * reach,)),
        ],
        compiler_params=pltpu.CompilerParams(
            collective_id=0, has_side_effects=True, vmem_limit_bytes=vmem_grant
        ),
        name="halo",
    )(leaving[0, 0], counts[0, 0], pairs[0, 0], mine)

    moved, own, sides = pl.pallas_call(
        pair_kernel,
        out_shape=(
            jax.ShapeDtypeStruct((8 * blocks, 128), f32),
            jax.ShapeDtypeStruct((4 * blocks, 128), f32),
            jax.ShapeDtypeStruct((12 * blocks, 128), f32),
        ),
        in_specs=[anywhere()] * 3,
        out_specs=(anywhere(), vmem(), vmem()),
        scratch_shapes=[
            pltpu.SMEM((4096,), i32),
            pltpu.VMEM((32 * blocks, 128), f32),
            pltpu.VMEM((16, 128), f32),
            pltpu.VMEM((3 * blocks, 128, 32), bf16),
            pltpu.VMEM((4 * blocks, 32, 256), bf16),
            pltpu.VMEM((4 * blocks, 16, 128), bf16),
            pltpu.VMEM((3 * blocks // 8, 128, 128), f32),
            pltpu.VMEM((32 * blocks, 128), f32),
            pltpu.VMEM((32 * blocks, 128), f32),
            pltpu.VMEM((32 * blocks + 8, 128), f32),
            pltpu.SemaphoreType.DMA((4,)),
        ]
        + [pltpu.VMEM((128, 256), f32)] * ring
        + [pltpu.VMEM((256, 256), bf16)] * ring,
        compiler_params=pltpu.CompilerParams(vmem_limit_bytes=vmem_grant),
        name="contact",
    )(lists.reshape(4096), cols.reshape(32 * blocks, 128), wide)

    mix, fluid = pl.pallas_call(
        finish_kernel,
        out_shape=(
            jax.ShapeDtypeStruct((14 * blocks, 128), f32),
            jax.ShapeDtypeStruct((2, 256), f32),
        ),
        in_specs=[anywhere()] * 5,
        out_specs=(vmem(), vmem()),
        scratch_shapes=[
            pltpu.VMEM((8 * blocks, 128), f32),
            pltpu.VMEM((blocks, 128), i32),
            pltpu.VMEM((blocks, 128), i32),
            pltpu.VMEM((1, 256), f32),
            pltpu.SemaphoreType.DMA((4,)),
            pltpu.VMEM((16, 96), f32),
            pltpu.SemaphoreType.DMA((3,)),
            pltpu.SemaphoreType.DMA((3,)),
        ],
        compiler_params=pltpu.CompilerParams(
            collective_id=1, has_side_effects=True, vmem_limit_bytes=vmem_grant
        ),
        name="finish",
    )(moved, sides, wall_flags[0, 0], cell_index[0, 0], fluid_temp.reshape(1, 256))

    rates, fluid = pl.pallas_call(
        rates_kernel,
        out_shape=(
            jax.ShapeDtypeStruct((4 * blocks, 128), f32),
            jax.ShapeDtypeStruct((2, 256), f32),
        ),
        in_specs=[anywhere()] * 3,
        out_specs=(vmem(), vmem()),
        scratch_shapes=[
            pltpu.VMEM((4 * blocks, 128), f32),
            pltpu.VMEM((14 * blocks, 128), f32),
            pltpu.VMEM((2, 256), f32),
            pltpu.SemaphoreType.DMA((3,)),
        ],
        compiler_params=pltpu.CompilerParams(vmem_limit_bytes=vmem_grant),
        name="rates",
    )(own, mix, fluid)
    return (
        moved.reshape(1, 1, blocks, 8, 128),
        rates.reshape(1, 1, blocks, 4, 128),
        fluid[None, None],
    )


def solution(mesh):
    in_specs = (
        P("gx", "gy", None, None, None),
        P("gx", "gy", None),
        P("gx", "gy", None, None),
        P("gx", "gy", None),
        P("gx", "gy", None, None),
        P("gx", "gy", None, None),
        P("gx", "gy", None),
    )
    out_specs = (
        P("gx", "gy", None, None, None),
        P("gx", "gy", None, None, None),
        P("gx", "gy", None, None),
    )
    return jax.shard_map(shards, mesh=mesh, in_specs=in_specs, out_specs=out_specs, check_vma=False)
```

```python
import functools
import math

import jax
import jax.numpy as jnp
from jax import lax
from jax.experimental import pallas as pl
from jax.experimental.pallas import tpu as pltpu
from jax.sharding import PartitionSpec as P

soften = 0.01
stiffness = 0.2
damping = 0.05
conductance = 0.05
film_gain = 0.5
wall_gain = 2.0
wall_temp = 1.0
gravity = 1.0
cell_volume = 32.0

f32 = jnp.float32
bf16 = jnp.bfloat16
i32 = jnp.int32

tiny = 1e-30
group = 16
lag_a = 2
lag_b = 2
ring = lag_a + lag_b
reach = 4
vmem_grant = 56 * 2**20
MESH = pl.DeviceIdType.MESH


def iota(shape, dim):
    return lax.broadcasted_iota(i32, shape, dim)


def split2(value):
    hi = value.astype(bf16).astype(f32)
    return hi, (value - hi).astype(bf16).astype(f32)


def split3(value):
    hi = value.astype(bf16).astype(f32)
    rest = value - hi
    mid = rest.astype(bf16).astype(f32)
    return hi, mid, rest - mid


def dot_tt(left, right):
    return lax.dot_general(left, right, (((1,), (1,)), ((), ())), preferred_element_type=f32)


def neighbours():
    a = lax.axis_index("gx")
    b = lax.axis_index("gy")
    na = lax.axis_size("gx")
    nb = lax.axis_size("gy")
    return (
        {"gx": lax.rem(a + 1, na)},
        {"gx": lax.rem(a + na - 1, na)},
        {"gy": lax.rem(b + 1, nb)},
        {"gy": lax.rem(b + nb - 1, nb)},
    )


def greet(everyone):
    barrier = pltpu.get_barrier_semaphore()
    for device in everyone:
        pl.semaphore_signal(barrier, inc=1, device_id=device, device_id_type=MESH)
    pl.semaphore_wait(barrier, len(everyone))


def sort_pairs(lanes, pad, total):
    own = pad[0:1, :]
    code = pad[1:2, :]
    region = jnp.zeros_like(code)
    for step in range(1, 9):
        region = region + (code >= 96 * step).astype(i32)
    far = code - 96 * region
    live = iota((1, lanes), 1) < total

    def among(*names):
        hit = region == names[0]
        for name in names[1:]:
            hit = hit | (region == name)
        return hit

    kind = jnp.where(
        among(4),
        0,
        jnp.where(among(1, 5), 1, jnp.where(among(0, 3), 2, jnp.where(among(2), 3, 4))),
    )
    kind = jnp.where(live, kind, 5)
    u_far = among(0, 1, 2, 3)
    u = jnp.where(u_far, far, own) + jnp.where(among(4, 5, 3), 0, 96)
    v_slot = jnp.where(u_far, own, far)
    v_side = jnp.where(among(4, 1, 7), 0, jnp.where(among(5, 3, 0, 8), 1, 2))
    ranks = iota((8, lanes), 0)
    marks = (ranks == kind).astype(f32)
    before = (iota((lanes, lanes), 0) < iota((lanes, lanes), 1)).astype(bf16)
    seen = jnp.dot(marks.astype(bf16), before, preferred_element_type=f32)
    starts = jnp.sum((kind < ranks).astype(f32), axis=1, keepdims=True)
    place = jnp.sum(marks * (seen + starts), axis=0, keepdims=True)
    target = (iota((lanes, lanes), 0).astype(f32) == place).astype(bf16)
    rows = iota((8, lanes), 0)
    values = jnp.where(
        rows == 0, u, jnp.where(rows == 1, v_slot, jnp.where(rows == 2, v_side, 0))
    )
    moved = dot_tt(values.astype(bf16), target)
    packed = moved[0:1] + 512.0 * (moved[1:2] + 96.0 * moved[2:3])
    diag = iota((8, 128), 0) == iota((8, 128), 1)
    begin = jnp.sum(jnp.where(diag, starts, 0.0), axis=0, keepdims=True)
    return packed.astype(i32), begin.astype(i32)


def halo_kernel(
    leaving_hbm,
    counts_hbm,
    pairs_hbm,
    state_hbm,
    cols_ref,
    lists_ref,
    wide_ref,
    leaving_ref,
    counts_ref,
    pairs_ref,
    cat,
    dep,
    moved,
    pad,
    slot_vec,
    slot_smem,
    dep_send,
    dep_recv,
    list_send,
    list_recv,
    col_send,
    col_recv,
    local_sem,
    in_sem,
    near,
    near_send,
    near_recv,
    wide_send,
    wide_recv,
):
    blocks = state_hbm.shape[0]
    count = leaving_hbm.shape[0]
    ahead, behind, up, down = neighbours()
    state_ref = cat.at[count : count + blocks]
    inputs = [
        pltpu.make_async_copy(source, target, in_sem.at[at])
        for at, (source, target) in enumerate(
            (
                (leaving_hbm, leaving_ref),
                (state_hbm, state_ref),
                (pairs_hbm, pairs_ref),
                (counts_hbm, counts_ref),
            )
        )
    ]
    for copy in inputs:
        copy.start()
    a = lax.axis_index("gx")
    na = lax.axis_size("gx")
    along = {
        step: {"gx": lax.rem(a + step + na, na)} for step in range(-reach, reach + 1) if step
    }
    wide_ref[...] = jnp.zeros_like(wide_ref)
    for copy in inputs:
        copy.wait()
    local = counts_ref[0].astype(f32)
    far = (counts_ref[1] - counts_ref[0]).astype(f32) * 0.125
    lane = iota((1, 128), 1)
    near[0:1, :] = jnp.where(lane < 64, far, local)
    for m in range(count):
        dep[m] = state_ref[leaving_ref[m]]
    b = lax.axis_index("gy")
    nb = lax.axis_size("gy")
    across = {"gy": lax.rem(b + 2, nb)}
    greet((up, down, across, *along.values()))
    asks = []
    for at, device in ((1, down), (2, up), (3, across)):
        copy = pltpu.make_async_remote_copy(
            src_ref=near.at[0:1],
            dst_ref=near.at[at : at + 1],
            send_sem=near_send.at[at - 1],
            recv_sem=near_recv.at[at - 1],
            device_id=device,
            device_id_type=MESH,
        )
        copy.start()
        asks.append(copy)
    depart = pltpu.make_async_remote_copy(
        src_ref=dep,
        dst_ref=cat.at[0:count],
        send_sem=dep_send,
        recv_sem=dep_recv,
        device_id=ahead,
        device_id_type=MESH,
    )
    depart.start()
    place = iota((8, 128), 1)
    slot = place + count
    for m in range(count):
        slot = jnp.where(place == leaving_ref[m], m, slot)
    slot_vec[...] = slot
    to_smem = pltpu.make_async_copy(slot_vec, slot_smem, local_sem)
    to_smem.start()
    lanes = pad.shape[1]
    pad[...] = jnp.zeros_like(pad)
    pad[0:2, 0 : pairs_ref.shape[1]] = pairs_ref[...]
    packed, begin = sort_pairs(lanes, pad, counts_ref[1])
    lists_ref[0] = jnp.zeros((8, 128), i32)
    for row in range(lanes // 128):
        lists_ref[0, row : row + 1, :] = packed[:, 128 * row : 128 * row + 128]
    lists_ref[0, 6:7, :] = begin
    copies = []
    for copy in asks:
        copy.wait()
    turn = lane & 3
    row = near[0:1, :]
    for at, step in ((1, 1), (2, nb - 1), (3, 2)):
        row = jnp.where(turn == lax.rem(b + step, nb), near[at : at + 1, :], row)
    wide_ref[reach : reach + 1, :] = row
    for at, step in enumerate(along):
        copy = pltpu.make_async_remote_copy(
            src_ref=wide_ref.at[reach : reach + 1],
            dst_ref=wide_ref.at[reach - step : reach - step + 1],
            send_sem=wide_send.at[at],
            recv_sem=wide_recv.at[at],
            device_id=along[step],
            device_id_type=MESH,
        )
        copy.start()
        copies.append(copy)
    for at, device in ((1, down), (2, up), (3, ahead)):
        copy = pltpu.make_async_remote_copy(
            src_ref=lists_ref.at[0],
            dst_ref=lists_ref.at[at],
            send_sem=list_send.at[at - 1],
            recv_sem=list_recv.at[at - 1],
            device_id=device,
            device_id_type=MESH,
        )
        copy.start()
        copies.append(copy)
    to_smem.wait()
    depart.wait()

    def place_block(j, carry):
        moved[j] = cat[slot_smem[0, j]]
        return carry

    lax.fori_loop(0, blocks, place_block, 0)
    keep = pltpu.make_async_copy(moved, cols_ref.at[0], local_sem)
    keep.start()
    for at, device in ((1, ahead), (2, down), (3, up)):
        copy = pltpu.make_async_remote_copy(
            src_ref=moved,
            dst_ref=cols_ref.at[at],
            send_sem=col_send.at[at - 1],
            recv_sem=col_recv.at[at - 1],
            device_id=device,
            device_id_type=MESH,
        )
        copy.start()
        copies.append(copy)
    keep.wait()
    for copy in copies:
        copy.wait()


def rows_of(base, c):
    return pl.ds(base * 8 + c, 8, 8)


def tile(i):
    return pl.ds(pl.multiple_of(i * 8, 8), 8)


def build_tables(cols_ref, U, V, L, RT, extra, pieces, natural, start, step, never, spare):
    rows = iota((8, 128), 0)
    eye = (iota((128, 128), 0) == iota((128, 128), 1)).astype(bf16)
    eyes = jnp.concatenate([eye, eye, eye], axis=1)
    c6 = jnp.where(rows == 6, 1.0, 0.0)
    c7 = jnp.where(rows == 7, 0.25, 0.0)
    ca = jnp.where(rows < 3, -2.0, 0.0)
    cb = jnp.where(rows < 6, -0.25, 0.0)
    ones = jnp.where(rows < 6, 1.0, 0.0)

    def dense(base):
        x = [cols_ref[rows_of(base, c), :] for c in range(3)]
        v = [cols_ref[rows_of(base, c), :] for c in range(3, 6)]
        radius = cols_ref[rows_of(base, 7), :]
        root = jnp.sqrt(radius)
        square = x[0] * x[0] + x[1] * x[1] + x[2] * x[2] + 0.5 * soften
        dot = x[0] * v[0] + x[1] * v[1] + x[2] * v[2]
        extra[rows_of(base, 3), :] = jnp.ones((8, 128), f32)
        extra[rows_of(base, 4), :] = root * cols_ref[rows_of(base, 6), :]
        extra[rows_of(base, 5), :] = root
        extra[rows_of(base, 6), :] = square
        extra[rows_of(base, 7), :] = dot
        for c, piece in enumerate(split3(square) + split3(0.25 * dot)):
            pieces[rows_of(base, c), :] = piece

    def swap(value):
        return jnp.where(rows < 3, pltpu.roll(value, 5, 0), pltpu.roll(value, 3, 0))

    def eight(base, shift, at, held=None):
        for q in range(8):
            i = base + q
            S = cols_ref[tile(i), :]
            if held is not None:
                S = jnp.where(never, held, S)
            E = extra[tile(i), :]
            G = pieces[tile(i), :]
            hi, mid = split2(jnp.where(rows < 3, S, jnp.where(rows < 6, E, 0.0)))
            L[i] = jnp.concatenate([hi, mid], axis=0).astype(bf16)
            full = jnp.where(rows < 6, S, E)
            hi, mid = split2(full)
            if at is not None:
                low = jnp.where(rows < 6, hi, full - hi - mid)
                natural[at, 32 * q : 32 * q + 32, :] = jnp.concatenate(
                    [hi, low, mid, ones], axis=0
                ).astype(bf16)
            a0 = hi * ca + c6
            a1 = mid * ca + c6
            b0 = swap(hi) * cb + c7
            b1 = swap(mid) * cb + c7
            A = jnp.concatenate([a0, a1, a0, jnp.where(rows < 3, G, 0.0)], axis=0)
            B = jnp.concatenate(
                [b0, b1, b0, jnp.where((rows >= 3) & (rows < 6), G, 0.0)], axis=0
            )
            V[i + shift, :, 0:128] = A.astype(bf16)
            V[i + shift, :, 128:256] = B.astype(bf16)

    def turn(at, u_base):
        turned = dot_tt(eye, natural[at]).astype(bf16)
        for q in range(8):
            U[u_base + q, :, 0:32] = turned[:, 32 * q : 32 * q + 32]

    def column(base, u_base):
        radius = cols_ref[rows_of(base, 7), :]
        three = jnp.concatenate(split3(radius), axis=1).astype(bf16)
        RT[lax.shift_right_logical(u_base, 3), :, 0:8] = dot_tt(eyes, three)

    def turns(t):
        turn(0, 8 * t)
        turn(1, 96 + 8 * t)
        turn(2, 192 + 8 * t)
        column(8 * t, 8 * t)
        column(96 + 8 * t, 96 + 8 * t)
        column(288 + 8 * t, 192 + 8 * t)

    def body(t, carry):
        turns(jnp.maximum(t - 1, 0))
        for col in range(4):
            dense(96 * col + 8 * t)
        eight(8 * t, 0, 0)
        eight(96 + 8 * t, 192, 1)
        eight(288 + 8 * t, -96, 2)
        held = U[spare, 0:16, :].astype(f32)[0:8]
        eight(192 + 8 * t, -96, None, held)
        return step(carry)

    count = cols_ref.shape[0] // 256
    carry = lax.fori_loop(0, count, body, start)
    turns(count - 1)
    return carry


def shares(wide):
    rows = iota((8, 128), 0)
    lanes = iota((8, 128), 1)
    b = lax.axis_index("gy")
    nb = lax.axis_size("gy")
    own = wide[1:9, :]
    behind = wide[0:8, :]
    far = jnp.where(lanes < 64, own, pltpu.roll(behind, 64, 1))
    local = jnp.where(lanes < 64, pltpu.roll(own, 64, 1), behind)
    load = (
        local
        + 2.0 * far
        + 2.0 * pltpu.roll(far, 127, 1)
        + pltpu.roll(far, 1, 1)
        + 3.0 * jnp.where(rows == 0, far, pltpu.roll(far, 1, 0))
    )
    passing = jnp.where(rows < 7, local, 0.0)

    def step(given):
        ahead, up = given
        now = load - ahead - up + pltpu.roll(ahead, 1, 0) + pltpu.roll(up, 1, 1)
        ahead = ahead + 0.26 * (now - pltpu.roll(now, 7, 0))
        ahead = jnp.minimum(jnp.maximum(ahead, 0.0), jnp.maximum(passing - up, 0.0))
        up = up + 0.26 * (now - pltpu.roll(now, 127, 1))
        up = jnp.minimum(jnp.maximum(up, 0.0), jnp.maximum(local - ahead, 0.0))
        return ahead, up

    def value(given, shift, base):
        column = lax.rem(b + shift + nb, nb)
        picked = (rows == reach - 1) & (lanes == column + base)
        return jnp.sum(jnp.where(picked, given, 0.0)).astype(i32)

    start = jnp.zeros((8, 128), f32)
    return (start, start), step, value


def pair_kernel(
    lists_hbm,
    cols_hbm,
    wide_hbm,
    moved_ref,
    own_ref,
    sides_ref,
    lists_ref,
    cols_ref,
    wide,
    U,
    V,
    L,
    RT,
    extra,
    pieces,
    natural,
    acc,
    sem,
    *rings,
):
    AB = rings[0:ring]
    M = rings[ring : 2 * ring]
    copies = [
        pltpu.make_async_copy(source, target, sem.at[at])
        for at, (source, target) in enumerate(
            ((cols_hbm, cols_ref), (lists_hbm, lists_ref), (wide_hbm, wide))
        )
    ]
    for copy in copies:
        copy.start()
    trash = acc.shape[0] // 8 - 1
    acc[...] = jnp.zeros_like(acc)
    for copy in copies:
        copy.wait()
    keep = pltpu.make_async_copy(cols_ref.at[0:768], moved_ref, sem.at[3])
    keep.start()
    given, step, value = shares(wide)
    first = lists_ref[0]
    given = build_tables(cols_ref, U, V, L, RT, extra, pieces, natural, given, step, first < 0, first & 63)
    ahead_out = value(given[0], 0, 32)
    up_out = value(given[1], 0, 32)
    ahead_in = value(given[0], 0, 96)
    ahead_down = value(given[0], -1, 32)
    up_in = value(given[1], -1, 32)

    def begin(at, name):
        return lists_ref[at * 1024 + 6 * 128 + name]

    def cut(at, first, second):
        first = jnp.minimum(first, begin(at, 1))
        return first, jnp.minimum(first + second, begin(at, 1))

    _, kept = cut(0, ahead_out, up_out)
    ahead_in = jnp.minimum(ahead_in, begin(3, 1))
    up_low, up_high = cut(2, ahead_down, up_in)
    ends = []
    shifts = []
    so_far = 0
    for at, low, high in (
        (0, kept, begin(0, 1)),
        (0, begin(0, 1), begin(0, 2)),
        (1, begin(1, 2), begin(1, 3)),
        (2, begin(2, 3), begin(2, 4)),
        (3, begin(3, 4), begin(3, 5)),
        (3, 0, ahead_in),
        (2, up_low, up_high),
    ):
        shifts.append(at * 1024 + low - so_far)
        so_far = so_far + (high - low)
        ends.append(so_far)
    n = so_far
    last = jnp.maximum(n - 1, 0)

    def entry(k):
        k = jnp.minimum(k, last)
        shift = shifts[6]
        for at in range(5, -1, -1):
            shift = jnp.where(k < ends[at], shifts[at], shift)
        code = lists_ref[k + shift]
        code = code + jnp.where(
            k < ends[4], 0, jnp.where(k < ends[5], 96 + 512 * 288, 192 + 512 * 192)
        )
        return code & 511, lax.shift_right_logical(code, 9)

    def spot_u(u):
        return jnp.where(u < 192, u, u + 96)

    def spot(v):
        return jnp.where(v < 96, v, jnp.where(v < 288, v + 96, v - 192))

    def distances(k, at):
        u, v = entry(k)
        AB[at][...] = jnp.dot(U[u, :, 0:32], V[v], preferred_element_type=f32)

    def weights(k, at):
        u, v = entry(k)
        rt = cols_ref[pl.ds(spot(v) * 8 + 7, 1), :]
        lane = jnp.full((8, 128), u & 7, i32)
        eighth = lax.shift_right_logical(u, 3)

        def radius(r):
            return jnp.take_along_axis(RT[eighth, r : r + 8, :], lane, axis=1)

        for r in range(0, 128, 16):
            A = AB[at][r : r + 16, 0:128]
            B = AB[at][r : r + 16, 128:256]
            R = jnp.concatenate([radius(r), radius(r + 8)], axis=0) + rt
            inv = lax.rsqrt(A)
            gap = R - A * inv
            inter = jnp.maximum(gap, 0.0)
            root = inter * lax.rsqrt(jnp.maximum(gap, tiny))
            W = (root * inv) * (inter - B * inv)
            G = root * lax.rsqrt(R)
            wh = W.astype(bf16)
            gh = G.astype(bf16)
            M[at][r : r + 16, 0:128] = wh
            M[at][r : r + 16, 128:256] = gh
            M[at][128 + r : 144 + r, 0:128] = (W - wh.astype(f32)).astype(bf16)
            M[at][128 + r : 144 + r, 128:256] = (G - gh.astype(f32)).astype(bf16)

    rows = iota((8, 128), 0)

    def folded(out):
        both = out[0:8] + out[8:16]
        return jnp.where(rows < 4, both[:, 0:128], both[:, 128:256])

    def sums(k, at):
        u, v = entry(k)
        w = spot(v)
        o = spot_u(u)
        first = jnp.concatenate([L[o], L[o]], axis=1)
        second = jnp.concatenate([L[w], L[w]], axis=1)
        m = M[at]
        crossed = jnp.concatenate(
            [
                jnp.concatenate([m[0:128, 0:128], m[128:256, 0:128]], axis=1),
                jnp.concatenate([m[0:128, 128:256], m[128:256, 128:256]], axis=1),
            ],
            axis=0,
        )
        to_second = folded(jnp.dot(first, m[...], preferred_element_type=f32))
        to_first = folded(dot_tt(second, crossed))
        live = k < n
        o = jnp.where(live, o, trash)
        w = jnp.where(live, w, trash)
        acc[tile(o), :] += to_first
        acc[tile(w), :] += to_second

    for q in range(ring):
        distances(q, q)
    for q in range(lag_b):
        weights(q, q)

    def turn(t, carry):
        for q in range(group):
            k = t * group + q
            sums(k, q % ring)
            weights(k + lag_b, (q + lag_b) % ring)
            distances(k + ring, q % ring)
        return carry

    lax.fori_loop(0, lax.div(n + group - 1, group), turn, 0)

    def close(base, out_ref, out_base):
        got = [acc[rows_of(base, c), :] for c in range(6)]
        terms = []
        for c in range(3):
            hi, mid = split2(cols_ref[rows_of(base, c), :])
            terms.append(stiffness * ((hi + mid) * got[3] - got[c]))
        root = conductance * extra[rows_of(base, 5), :]
        terms.append(root * (got[4] - cols_ref[rows_of(base, 6), :] * got[5]))
        for c in range(4):
            out_ref[pl.ds(out_base + c, 8, 4), :] = terms[c]

    def close_all(t, carry):
        close(8 * t, own_ref, 32 * t)
        for side in range(3):
            close(96 * (side + 1) + 8 * t, sides_ref, 384 * side + 32 * t)
        return carry

    lax.fori_loop(0, 12, close_all, 0)
    keep.wait()


def finish_kernel(
    moved_hbm,
    sides_ref,
    flags_hbm,
    cells_hbm,
    table_hbm,
    mix_ref,
    fluid_ref,
    moved_ref,
    flags_ref,
    cells_ref,
    table_ref,
    in_sem,
    sums,
    send,
    recv,
):
    ahead, behind, up, down = neighbours()
    inputs = [
        pltpu.make_async_copy(source, target, in_sem.at[at])
        for at, (source, target) in enumerate(
            (
                (moved_hbm, moved_ref),
                (flags_hbm, flags_ref),
                (cells_hbm, cells_ref),
                (table_hbm, table_ref),
            )
        )
    ]
    for copy in inputs:
        copy.start()
    greet((ahead, behind, up, down))
    copies = []
    span = sides_ref.shape[0] // 3
    blocks = span // 4
    for at, device in ((0, behind), (1, up), (2, down)):
        copy = pltpu.make_async_remote_copy(
            src_ref=sides_ref.at[span * at : span * at + span],
            dst_ref=mix_ref.at[span * at : span * at + span],
            send_sem=send.at[at],
            recv_sem=recv.at[at],
            device_id=device,
            device_id_type=MESH,
        )
        copy.start()
        copies.append(copy)

    for copy in inputs:
        copy.wait()
    square = jnp.concatenate([table_ref[:, 16 * a : 16 * a + 16] for a in range(16)], axis=0)
    table = jnp.concatenate(split3(square), axis=0).astype(bf16)
    sums[...] = jnp.zeros_like(sums)
    sub = iota((16, 128), 0)

    def cells_of(g, carry):
        at = pl.ds(pl.multiple_of(g * 8, 8), 8)
        temper = moved_ref[rows_of(g * 8, 6), :]
        radius = moved_ref[rows_of(g * 8, 7), :]
        volume = 4.0 / 3.0 * math.pi * radius * radius * radius
        cell = cells_ref[at, :]
        high = lax.shift_right_logical(cell, 4)
        low = cell & 15
        fluid = []
        hots = []
        for c in range(8):
            hot_high = (sub == high[c : c + 1]).astype(f32)
            hot_low = (sub == low[c : c + 1]).astype(f32)
            parts = jnp.dot(table, hot_low.astype(bf16), preferred_element_type=f32)
            value = parts[0:16] + parts[16:32] + parts[32:48]
            fluid.append(jnp.sum(value * hot_high, axis=0, keepdims=True))
            hots.append((hot_high, hot_low))
        flow = film_gain * radius * radius * (temper - jnp.concatenate(fluid, axis=0))
        pieces = split3(volume) + split3(flow)
        total = sums[...]
        for c in range(8):
            hot_high, hot_low = hots[c]
            spread = jnp.concatenate([hot_low * piece[c : c + 1] for piece in pieces], axis=0)
            total = total + dot_tt(hot_high.astype(bf16), spread.astype(bf16))
        sums[...] = total
        wall = wall_gain * flags_ref[at, :].astype(f32) * (wall_temp - temper) * radius
        mix_ref[pl.ds(pl.multiple_of(3 * span + g * 8, 8), 8), :] = wall - flow
        mix_ref[pl.ds(pl.multiple_of(3 * span + blocks + g * 8, 8), 8), :] = 1.0 / volume
        return carry

    lax.fori_loop(0, 12, cells_of, 0)
    total = sums[...]
    solid = (total[:, 0:16] + total[:, 16:32] + total[:, 32:48]) / cell_volume
    heat = total[:, 48:64] + total[:, 64:80] + total[:, 80:96]
    for a in range(16):
        fluid_ref[0:1, 16 * a : 16 * a + 16] = solid[a : a + 1]
        fluid_ref[1:2, 16 * a : 16 * a + 16] = heat[a : a + 1]
    for copy in copies:
        copy.wait()


def rates_kernel(
    own_hbm, mix_hbm, fluid_hbm, rates_ref, fluid_ref, own, mix, fluid, sem
):
    copies = [
        pltpu.make_async_copy(source, target, sem.at[at])
        for at, (source, target) in enumerate(
            ((mix_hbm, mix), (own_hbm, own), (fluid_hbm, fluid))
        )
    ]
    for copy in copies:
        copy.start()
    for copy in copies:
        copy.wait()
    fluid_ref[...] = fluid[...]
    span = own.shape[0]
    blocks = span // 4

    def combine(g, carry):
        at = pl.multiple_of(g * 8, 8)
        inverse = mix[pl.ds(3 * span + blocks + at, 8), :]
        for c in range(4):
            here = pl.ds(g * 32 + c, 8, 4)
            value = own[here, :]
            for side in range(3):
                value = value + mix[pl.ds(span * side + g * 32 + c, 8, 4), :]
            if c == 3:
                value = value + mix[pl.ds(3 * span + at, 8), :]
            value = value * inverse
            if c == 2:
                value = value - gravity
            rates_ref[here, :] = value
        return carry

    lax.fori_loop(0, blocks // 8, combine, 0, unroll=4)


def anywhere():
    return pl.BlockSpec(memory_space=pl.ANY)


def vmem():
    return pl.BlockSpec(memory_space=pltpu.VMEM)


def shards(state, leaving, pairs, counts, wall_flags, cell_index, fluid_temp):
    mine = state[0, 0]
    blocks = mine.shape[0]
    count = leaving.shape[2]
    lanes = -(-pairs.shape[3] // 128) * 128
    cols, lists, wide = pl.pallas_call(
        halo_kernel,
        out_shape=(
            jax.ShapeDtypeStruct((4, blocks, 8, 128), f32),
            jax.ShapeDtypeStruct((4, 8, 128), i32),
            jax.ShapeDtypeStruct((16, 128), f32),
        ),
        in_specs=[anywhere()] * 4,
        out_specs=(anywhere(), vmem(), vmem()),
        scratch_shapes=[
            pltpu.SMEM(leaving.shape[2:], i32),
            pltpu.SMEM(counts.shape[2:], i32),
            pltpu.VMEM(pairs.shape[2:], i32),
            pltpu.VMEM((count + blocks, 8, 128), f32),
            pltpu.VMEM((count, 8, 128), f32),
            pltpu.VMEM((blocks, 8, 128), f32),
            pltpu.VMEM((8, lanes), i32),
            pltpu.VMEM((8, 128), i32),
            pltpu.SMEM((8, 128), i32),
            pltpu.SemaphoreType.DMA,
            pltpu.SemaphoreType.DMA,
            pltpu.SemaphoreType.DMA((3,)),
            pltpu.SemaphoreType.DMA((3,)),
            pltpu.SemaphoreType.DMA((3,)),
            pltpu.SemaphoreType.DMA((3,)),
            pltpu.SemaphoreType.DMA,
            pltpu.SemaphoreType.DMA((4,)),
            pltpu.VMEM((8, 128), f32),
            pltpu.SemaphoreType.DMA((3,)),
            pltpu.SemaphoreType.DMA((3,)),
            pltpu.SemaphoreType.DMA((2 * reach,)),
            pltpu.SemaphoreType.DMA((2 * reach,)),
        ],
        compiler_params=pltpu.CompilerParams(
            collective_id=0, has_side_effects=True, vmem_limit_bytes=vmem_grant
        ),
        name="halo",
    )(leaving[0, 0], counts[0, 0], pairs[0, 0], mine)

    moved, own, sides = pl.pallas_call(
        pair_kernel,
        out_shape=(
            jax.ShapeDtypeStruct((8 * blocks, 128), f32),
            jax.ShapeDtypeStruct((4 * blocks, 128), f32),
            jax.ShapeDtypeStruct((12 * blocks, 128), f32),
        ),
        in_specs=[anywhere()] * 3,
        out_specs=(anywhere(), vmem(), vmem()),
        scratch_shapes=[
            pltpu.SMEM((4096,), i32),
            pltpu.VMEM((32 * blocks, 128), f32),
            pltpu.VMEM((16, 128), f32),
            pltpu.VMEM((3 * blocks, 128, 128), bf16),
            pltpu.VMEM((4 * blocks, 32, 256), bf16),
            pltpu.VMEM((4 * blocks, 16, 128), bf16),
            pltpu.VMEM((3 * blocks // 8, 128, 128), f32),
            pltpu.VMEM((32 * blocks, 128), f32),
            pltpu.VMEM((32 * blocks, 128), f32),
            pltpu.VMEM((3, 256, 128), bf16),
            pltpu.VMEM((32 * blocks + 8, 128), f32),
            pltpu.SemaphoreType.DMA((4,)),
        ]
        + [pltpu.VMEM((128, 256), f32)] * ring
        + [pltpu.VMEM((256, 256), bf16)] * ring,
        compiler_params=pltpu.CompilerParams(vmem_limit_bytes=vmem_grant),
        name="contact",
    )(lists.reshape(4096), cols.reshape(32 * blocks, 128), wide)

    mix, fluid = pl.pallas_call(
        finish_kernel,
        out_shape=(
            jax.ShapeDtypeStruct((14 * blocks, 128), f32),
            jax.ShapeDtypeStruct((2, 256), f32),
        ),
        in_specs=[anywhere()] * 5,
        out_specs=(vmem(), vmem()),
        scratch_shapes=[
            pltpu.VMEM((8 * blocks, 128), f32),
            pltpu.VMEM((blocks, 128), i32),
            pltpu.VMEM((blocks, 128), i32),
            pltpu.VMEM((1, 256), f32),
            pltpu.SemaphoreType.DMA((4,)),
            pltpu.VMEM((16, 96), f32),
            pltpu.SemaphoreType.DMA((3,)),
            pltpu.SemaphoreType.DMA((3,)),
        ],
        compiler_params=pltpu.CompilerParams(
            collective_id=1, has_side_effects=True, vmem_limit_bytes=vmem_grant
        ),
        name="finish",
    )(moved, sides, wall_flags[0, 0], cell_index[0, 0], fluid_temp.reshape(1, 256))

    rates, fluid = pl.pallas_call(
        rates_kernel,
        out_shape=(
            jax.ShapeDtypeStruct((4 * blocks, 128), f32),
            jax.ShapeDtypeStruct((2, 256), f32),
        ),
        in_specs=[anywhere()] * 3,
        out_specs=(vmem(), vmem()),
        scratch_shapes=[
            pltpu.VMEM((4 * blocks, 128), f32),
            pltpu.VMEM((14 * blocks, 128), f32),
            pltpu.VMEM((2, 256), f32),
            pltpu.SemaphoreType.DMA((3,)),
        ],
        compiler_params=pltpu.CompilerParams(vmem_limit_bytes=vmem_grant),
        name="rates",
    )(own, mix, fluid)
    return (
        moved.reshape(1, 1, blocks, 8, 128),
        rates.reshape(1, 1, blocks, 4, 128),
        fluid[None, None],
    )


def solution(mesh):
    in_specs = (
        P("gx", "gy", None, None, None),
        P("gx", "gy", None),
        P("gx", "gy", None, None),
        P("gx", "gy", None),
        P("gx", "gy", None, None),
        P("gx", "gy", None, None),
        P("gx", "gy", None),
    )
    out_specs = (
        P("gx", "gy", None, None, None),
        P("gx", "gy", None, None, None),
        P("gx", "gy", None, None),
    )
    return jax.shard_map(shards, mesh=mesh, in_specs=in_specs, out_specs=out_specs, check_vma=False)
```

```python
import functools
import math

import jax
import jax.numpy as jnp
from jax import lax
from jax.experimental import pallas as pl
from jax.experimental.pallas import tpu as pltpu
from jax.sharding import PartitionSpec as P

soften = 0.01
stiffness = 0.2
damping = 0.05
conductance = 0.05
film_gain = 0.5
wall_gain = 2.0
wall_temp = 1.0
gravity = 1.0
cell_volume = 32.0

f32 = jnp.float32
bf16 = jnp.bfloat16
i32 = jnp.int32

tiny = 1e-30
group = 16
lag_a = 2
lag_b = 2
ring = lag_a + lag_b
reach = 4
lateness = (37.0, 28.0, 22.0, 125.0, 20.0)
vmem_grant = 56 * 2**20
MESH = pl.DeviceIdType.MESH


def iota(shape, dim):
    return lax.broadcasted_iota(i32, shape, dim)


def split2(value):
    hi = value.astype(bf16).astype(f32)
    return hi, (value - hi).astype(bf16).astype(f32)


def split3(value):
    hi = value.astype(bf16).astype(f32)
    rest = value - hi
    mid = rest.astype(bf16).astype(f32)
    return hi, mid, rest - mid


def dot_tt(left, right):
    return lax.dot_general(left, right, (((1,), (1,)), ((), ())), preferred_element_type=f32)


def neighbours():
    a = lax.axis_index("gx")
    b = lax.axis_index("gy")
    na = lax.axis_size("gx")
    nb = lax.axis_size("gy")
    return (
        {"gx": lax.rem(a + 1, na)},
        {"gx": lax.rem(a + na - 1, na)},
        {"gy": lax.rem(b + 1, nb)},
        {"gy": lax.rem(b + nb - 1, nb)},
    )


def greet(everyone):
    barrier = pltpu.get_barrier_semaphore()
    for device in everyone:
        pl.semaphore_signal(barrier, inc=1, device_id=device, device_id_type=MESH)
    pl.semaphore_wait(barrier, len(everyone))


def sort_pairs(lanes, pad, total):
    own = pad[0:1, :]
    code = pad[1:2, :]
    region = jnp.zeros_like(code)
    for step in range(1, 9):
        region = region + (code >= 96 * step).astype(i32)
    far = code - 96 * region
    live = iota((1, lanes), 1) < total

    def among(*names):
        hit = region == names[0]
        for name in names[1:]:
            hit = hit | (region == name)
        return hit

    kind = jnp.where(
        among(4),
        0,
        jnp.where(among(1, 5), 1, jnp.where(among(0, 3), 2, jnp.where(among(2), 3, 4))),
    )
    kind = jnp.where(live, kind, 5)
    u_far = among(0, 1, 2, 3)
    u = jnp.where(u_far, far, own) + jnp.where(among(4, 5, 3), 0, 96)
    v_slot = jnp.where(u_far, own, far)
    v_side = jnp.where(among(4, 1, 7), 0, jnp.where(among(5, 3, 0, 8), 1, 2))
    ranks = iota((8, lanes), 0)
    marks = (ranks == kind).astype(f32)
    before = (iota((lanes, lanes), 0) < iota((lanes, lanes), 1)).astype(bf16)
    seen = jnp.dot(marks.astype(bf16), before, preferred_element_type=f32)
    starts = jnp.sum((kind < ranks).astype(f32), axis=1, keepdims=True)
    place = jnp.sum(marks * (seen + starts), axis=0, keepdims=True)
    target = (iota((lanes, lanes), 0).astype(f32) == place).astype(bf16)
    rows = iota((8, lanes), 0)
    values = jnp.where(
        rows == 0, u, jnp.where(rows == 1, v_slot, jnp.where(rows == 2, v_side, 0))
    )
    moved = dot_tt(values.astype(bf16), target)
    packed = moved[0:1] + 512.0 * (moved[1:2] + 96.0 * moved[2:3])
    diag = iota((8, 128), 0) == iota((8, 128), 1)
    begin = jnp.sum(jnp.where(diag, starts, 0.0), axis=0, keepdims=True)
    return packed.astype(i32), begin.astype(i32)


def halo_kernel(
    leaving_hbm,
    counts_hbm,
    pairs_hbm,
    state_hbm,
    cols_ref,
    lists_ref,
    wide_ref,
    leaving_ref,
    counts_ref,
    pairs_ref,
    cat,
    dep,
    moved,
    pad,
    slot_vec,
    slot_smem,
    dep_send,
    dep_recv,
    list_send,
    list_recv,
    col_send,
    col_recv,
    local_sem,
    in_sem,
    near,
    near_send,
    near_recv,
    wide_send,
    wide_recv,
):
    blocks = state_hbm.shape[0]
    count = leaving_hbm.shape[0]
    ahead, behind, up, down = neighbours()
    state_ref = cat.at[count : count + blocks]
    inputs = [
        pltpu.make_async_copy(source, target, in_sem.at[at])
        for at, (source, target) in enumerate(
            (
                (leaving_hbm, leaving_ref),
                (state_hbm, state_ref),
                (pairs_hbm, pairs_ref),
                (counts_hbm, counts_ref),
            )
        )
    ]
    for copy in inputs:
        copy.start()
    a = lax.axis_index("gx")
    na = lax.axis_size("gx")
    along = {
        step: {"gx": lax.rem(a + step + na, na)} for step in range(-reach, reach + 1) if step
    }
    wide_ref[...] = jnp.zeros_like(wide_ref)
    for copy in inputs:
        copy.wait()
    local = counts_ref[0].astype(f32)
    far = (counts_ref[1] - counts_ref[0]).astype(f32) * 0.125
    lane = iota((1, 128), 1)
    near[0:1, :] = jnp.where(lane < 64, far, local)
    for m in range(count):
        dep[m] = state_ref[leaving_ref[m]]
    b = lax.axis_index("gy")
    nb = lax.axis_size("gy")
    across = {"gy": lax.rem(b + 2, nb)}
    greet((up, down, across, *along.values()))
    asks = []
    for at, device in ((1, down), (2, up), (3, across)):
        copy = pltpu.make_async_remote_copy(
            src_ref=near.at[0:1],
            dst_ref=near.at[at : at + 1],
            send_sem=near_send.at[at - 1],
            recv_sem=near_recv.at[at - 1],
            device_id=device,
            device_id_type=MESH,
        )
        copy.start()
        asks.append(copy)
    depart = pltpu.make_async_remote_copy(
        src_ref=dep,
        dst_ref=cat.at[0:count],
        send_sem=dep_send,
        recv_sem=dep_recv,
        device_id=ahead,
        device_id_type=MESH,
    )
    depart.start()
    place = iota((8, 128), 1)
    slot = place + count
    for m in range(count):
        slot = jnp.where(place == leaving_ref[m], m, slot)
    slot_vec[...] = slot
    to_smem = pltpu.make_async_copy(slot_vec, slot_smem, local_sem)
    to_smem.start()
    lanes = pad.shape[1]
    pad[...] = jnp.zeros_like(pad)
    pad[0:2, 0 : pairs_ref.shape[1]] = pairs_ref[...]
    packed, begin = sort_pairs(lanes, pad, counts_ref[1])
    lists_ref[0] = jnp.zeros((8, 128), i32)
    for row in range(lanes // 128):
        lists_ref[0, row : row + 1, :] = packed[:, 128 * row : 128 * row + 128]
    lists_ref[0, 6:7, :] = begin
    copies = []
    for copy in asks:
        copy.wait()
    turn = lane & 3
    row = near[0:1, :]
    for at, step in ((1, 1), (2, nb - 1), (3, 2)):
        row = jnp.where(turn == lax.rem(b + step, nb), near[at : at + 1, :], row)
    wide_ref[reach : reach + 1, :] = row
    for at, step in enumerate(along):
        copy = pltpu.make_async_remote_copy(
            src_ref=wide_ref.at[reach : reach + 1],
            dst_ref=wide_ref.at[reach - step : reach - step + 1],
            send_sem=wide_send.at[at],
            recv_sem=wide_recv.at[at],
            device_id=along[step],
            device_id_type=MESH,
        )
        copy.start()
        copies.append(copy)
    for at, device in ((1, down), (2, up), (3, ahead)):
        copy = pltpu.make_async_remote_copy(
            src_ref=lists_ref.at[0],
            dst_ref=lists_ref.at[at],
            send_sem=list_send.at[at - 1],
            recv_sem=list_recv.at[at - 1],
            device_id=device,
            device_id_type=MESH,
        )
        copy.start()
        copies.append(copy)
    to_smem.wait()
    depart.wait()

    def place_block(j, carry):
        moved[j] = cat[slot_smem[0, j]]
        return carry

    lax.fori_loop(0, blocks, place_block, 0)
    keep = pltpu.make_async_copy(moved, cols_ref.at[0], local_sem)
    keep.start()
    for at, device in ((1, ahead), (2, down), (3, up)):
        copy = pltpu.make_async_remote_copy(
            src_ref=moved,
            dst_ref=cols_ref.at[at],
            send_sem=col_send.at[at - 1],
            recv_sem=col_recv.at[at - 1],
            device_id=device,
            device_id_type=MESH,
        )
        copy.start()
        copies.append(copy)
    keep.wait()
    for copy in copies:
        copy.wait()


def rows_of(base, c):
    return pl.ds(base * 8 + c, 8, 8)


def tile(i):
    return pl.ds(pl.multiple_of(i * 8, 8), 8)


def build_tables(cols_ref, U, V, L, RT, extra, pieces, natural, start, step, never, spare):
    rows = iota((8, 128), 0)
    eye = (iota((128, 128), 0) == iota((128, 128), 1)).astype(bf16)
    eyes = jnp.concatenate([eye, eye, eye], axis=1)
    c6 = jnp.where(rows == 6, 1.0, 0.0)
    c7 = jnp.where(rows == 7, 0.25, 0.0)
    ca = jnp.where(rows < 3, -2.0, 0.0)
    cb = jnp.where(rows < 6, -0.25, 0.0)
    ones = jnp.where(rows < 6, 1.0, 0.0)

    def dense(base):
        x = [cols_ref[rows_of(base, c), :] for c in range(3)]
        v = [cols_ref[rows_of(base, c), :] for c in range(3, 6)]
        radius = cols_ref[rows_of(base, 7), :]
        root = jnp.sqrt(radius)
        square = x[0] * x[0] + x[1] * x[1] + x[2] * x[2] + 0.5 * soften
        dot = x[0] * v[0] + x[1] * v[1] + x[2] * v[2]
        extra[rows_of(base, 3), :] = jnp.ones((8, 128), f32)
        extra[rows_of(base, 4), :] = root * cols_ref[rows_of(base, 6), :]
        extra[rows_of(base, 5), :] = root
        extra[rows_of(base, 6), :] = square
        extra[rows_of(base, 7), :] = dot
        for c, piece in enumerate(split3(square) + split3(0.25 * dot)):
            pieces[rows_of(base, c), :] = piece

    def swap(value):
        return jnp.where(rows < 3, pltpu.roll(value, 5, 0), pltpu.roll(value, 3, 0))

    def eight(base, shift, at, held=None):
        for q in range(8):
            i = base + q
            S = cols_ref[tile(i), :]
            if held is not None:
                S = jnp.where(never, held, S)
            E = extra[tile(i), :]
            G = pieces[tile(i), :]
            hi, mid = split2(jnp.where(rows < 3, S, jnp.where(rows < 6, E, 0.0)))
            L[i] = jnp.concatenate([hi, mid], axis=0).astype(bf16)
            full = jnp.where(rows < 6, S, E)
            hi, mid = split2(full)
            if at is not None:
                low = jnp.where(rows < 6, hi, full - hi - mid)
                natural[at, 32 * q : 32 * q + 32, :] = jnp.concatenate(
                    [hi, low, mid, ones], axis=0
                ).astype(bf16)
            a0 = hi * ca + c6
            a1 = mid * ca + c6
            b0 = swap(hi) * cb + c7
            b1 = swap(mid) * cb + c7
            A = jnp.concatenate([a0, a1, a0, jnp.where(rows < 3, G, 0.0)], axis=0)
            B = jnp.concatenate(
                [b0, b1, b0, jnp.where((rows >= 3) & (rows < 6), G, 0.0)], axis=0
            )
            V[i + shift, :, 0:128] = A.astype(bf16)
            V[i + shift, :, 128:256] = B.astype(bf16)

    def turn(at, u_base):
        turned = dot_tt(eye, natural[at]).astype(bf16)
        for q in range(8):
            U[u_base + q, :, 0:32] = turned[:, 32 * q : 32 * q + 32]

    def column(base, u_base):
        radius = cols_ref[rows_of(base, 7), :]
        three = jnp.concatenate(split3(radius), axis=1).astype(bf16)
        RT[lax.shift_right_logical(u_base, 3), :, 0:8] = dot_tt(eyes, three)

    def turns(t):
        turn(0, 8 * t)
        turn(1, 96 + 8 * t)
        turn(2, 192 + 8 * t)
        column(8 * t, 8 * t)
        column(96 + 8 * t, 96 + 8 * t)
        column(288 + 8 * t, 192 + 8 * t)

    def body(t, carry):
        turns(jnp.maximum(t - 1, 0))
        for col in range(4):
            dense(96 * col + 8 * t)
        eight(8 * t, 0, 0)
        eight(96 + 8 * t, 192, 1)
        eight(288 + 8 * t, -96, 2)
        held = U[spare, 0:16, :].astype(f32)[0:8]
        eight(192 + 8 * t, -96, None, held)
        return step(carry)

    count = cols_ref.shape[0] // 256
    carry = lax.fori_loop(0, count, body, start)
    turns(count - 1)
    return carry


def shares(wide):
    rows = iota((8, 128), 0)
    lanes = iota((8, 128), 1)
    b = lax.axis_index("gy")
    nb = lax.axis_size("gy")
    own = wide[1:9, :]
    behind = wide[0:8, :]
    far = jnp.where(lanes < 64, own, pltpu.roll(behind, 64, 1))
    local = jnp.where(lanes < 64, pltpu.roll(own, 64, 1), behind)
    load = (
        local
        + 2.0 * far
        + 2.0 * pltpu.roll(far, 127, 1)
        + pltpu.roll(far, 1, 1)
        + 3.0 * jnp.where(rows == 0, far, pltpu.roll(far, 1, 0))
    )
    column = lax.axis_index("gx") + rows - (reach - 1) - jnp.where(lanes < 64, 0, 1)
    phase = (column + 32) & 15
    for at, late in enumerate(lateness):
        load = load + jnp.where(phase == at, late, 0.0)
    passing = jnp.where(rows < 7, local, 0.0)

    def step(given):
        ahead, up = given
        now = load - ahead - up + pltpu.roll(ahead, 1, 0) + pltpu.roll(up, 1, 1)
        ahead = ahead + 0.26 * (now - pltpu.roll(now, 7, 0))
        ahead = jnp.minimum(jnp.maximum(ahead, 0.0), jnp.maximum(passing - up, 0.0))
        up = up + 0.26 * (now - pltpu.roll(now, 127, 1))
        up = jnp.minimum(jnp.maximum(up, 0.0), jnp.maximum(local - ahead, 0.0))
        return ahead, up

    def value(given, shift, base):
        column = lax.rem(b + shift + nb, nb)
        picked = (rows == reach - 1) & (lanes == column + base)
        return jnp.sum(jnp.where(picked, given, 0.0)).astype(i32)

    start = jnp.zeros((8, 128), f32)
    return (start, start), step, value


def pair_kernel(
    lists_hbm,
    cols_hbm,
    wide_hbm,
    moved_ref,
    own_ref,
    sides_ref,
    lists_ref,
    cols_ref,
    wide,
    U,
    V,
    L,
    RT,
    extra,
    pieces,
    natural,
    acc,
    sem,
    *rings,
):
    AB = rings[0:ring]
    M = rings[ring : 2 * ring]
    copies = [
        pltpu.make_async_copy(source, target, sem.at[at])
        for at, (source, target) in enumerate(
            ((cols_hbm, cols_ref), (lists_hbm, lists_ref), (wide_hbm, wide))
        )
    ]
    for copy in copies:
        copy.start()
    trash = acc.shape[0] // 8 - 1
    acc[...] = jnp.zeros_like(acc)
    for copy in copies:
        copy.wait()
    keep = pltpu.make_async_copy(cols_ref.at[0:768], moved_ref, sem.at[3])
    keep.start()
    given, step, value = shares(wide)
    first = lists_ref[0]
    given = build_tables(cols_ref, U, V, L, RT, extra, pieces, natural, given, step, first < 0, first & 63)
    ahead_out = value(given[0], 0, 32)
    up_out = value(given[1], 0, 32)
    ahead_in = value(given[0], 0, 96)
    ahead_down = value(given[0], -1, 32)
    up_in = value(given[1], -1, 32)

    def begin(at, name):
        return lists_ref[at * 1024 + 6 * 128 + name]

    def cut(at, first, second):
        first = jnp.minimum(first, begin(at, 1))
        return first, jnp.minimum(first + second, begin(at, 1))

    _, kept = cut(0, ahead_out, up_out)
    ahead_in = jnp.minimum(ahead_in, begin(3, 1))
    up_low, up_high = cut(2, ahead_down, up_in)
    ends = []
    shifts = []
    so_far = 0
    for at, low, high in (
        (0, kept, begin(0, 1)),
        (0, begin(0, 1), begin(0, 2)),
        (1, begin(1, 2), begin(1, 3)),
        (2, begin(2, 3), begin(2, 4)),
        (3, begin(3, 4), begin(3, 5)),
        (3, 0, ahead_in),
        (2, up_low, up_high),
    ):
        shifts.append(at * 1024 + low - so_far)
        so_far = so_far + (high - low)
        ends.append(so_far)
    n = so_far
    last = jnp.maximum(n - 1, 0)

    def entry(k):
        k = jnp.minimum(k, last)
        shift = shifts[6]
        for at in range(5, -1, -1):
            shift = jnp.where(k < ends[at], shifts[at], shift)
        code = lists_ref[k + shift]
        code = code + jnp.where(
            k < ends[4], 0, jnp.where(k < ends[5], 96 + 512 * 288, 192 + 512 * 192)
        )
        return code & 511, lax.shift_right_logical(code, 9)

    def spot_u(u):
        return jnp.where(u < 192, u, u + 96)

    def spot(v):
        return jnp.where(v < 96, v, jnp.where(v < 288, v + 96, v - 192))

    def distances(k, at):
        u, v = entry(k)
        AB[at][...] = jnp.dot(U[u, :, 0:32], V[v], preferred_element_type=f32)

    def weights(k, at):
        u, v = entry(k)
        rt = cols_ref[pl.ds(spot(v) * 8 + 7, 1), :]
        lane = jnp.full((8, 128), u & 7, i32)
        eighth = lax.shift_right_logical(u, 3)

        def radius(r):
            return jnp.take_along_axis(RT[eighth, r : r + 8, :], lane, axis=1)

        for r in range(0, 128, 16):
            A = AB[at][r : r + 16, 0:128]
            B = AB[at][r : r + 16, 128:256]
            R = jnp.concatenate([radius(r), radius(r + 8)], axis=0) + rt
            inv = lax.rsqrt(A)
            gap = R - A * inv
            inter = jnp.maximum(gap, 0.0)
            root = inter * lax.rsqrt(jnp.maximum(gap, tiny))
            W = (root * inv) * (inter - B * inv)
            G = root * lax.rsqrt(R)
            wh = W.astype(bf16)
            gh = G.astype(bf16)
            M[at][r : r + 16, 0:128] = wh
            M[at][r : r + 16, 128:256] = gh
            M[at][128 + r : 144 + r, 0:128] = (W - wh.astype(f32)).astype(bf16)
            M[at][128 + r : 144 + r, 128:256] = (G - gh.astype(f32)).astype(bf16)

    rows = iota((8, 128), 0)

    def folded(out):
        both = out[0:8] + out[8:16]
        return jnp.where(rows < 4, both[:, 0:128], both[:, 128:256])

    def sums(k, at):
        u, v = entry(k)
        w = spot(v)
        o = spot_u(u)
        first = jnp.concatenate([L[o], L[o]], axis=1)
        second = jnp.concatenate([L[w], L[w]], axis=1)
        m = M[at]
        crossed = jnp.concatenate(
            [
                jnp.concatenate([m[0:128, 0:128], m[128:256, 0:128]], axis=1),
                jnp.concatenate([m[0:128, 128:256], m[128:256, 128:256]], axis=1),
            ],
            axis=0,
        )
        to_second = folded(jnp.dot(first, m[...], preferred_element_type=f32))
        to_first = folded(dot_tt(second, crossed))
        live = k < n
        o = jnp.where(live, o, trash)
        w = jnp.where(live, w, trash)
        acc[tile(o), :] += to_first
        acc[tile(w), :] += to_second

    for q in range(ring):
        distances(q, q)
    for q in range(lag_b):
        weights(q, q)

    def turn(t, carry):
        for q in range(group):
            k = t * group + q
            sums(k, q % ring)
            weights(k + lag_b, (q + lag_b) % ring)
            distances(k + ring, q % ring)
        return carry

    lax.fori_loop(0, lax.div(n + group - 1, group), turn, 0)

    def close(base, out_ref, out_base):
        got = [acc[rows_of(base, c), :] for c in range(6)]
        terms = []
        for c in range(3):
            hi, mid = split2(cols_ref[rows_of(base, c), :])
            terms.append(stiffness * ((hi + mid) * got[3] - got[c]))
        root = conductance * extra[rows_of(base, 5), :]
        terms.append(root * (got[4] - cols_ref[rows_of(base, 6), :] * got[5]))
        for c in range(4):
            out_ref[pl.ds(out_base + c, 8, 4), :] = terms[c]

    def close_all(t, carry):
        close(8 * t, own_ref, 32 * t)
        for side in range(3):
            close(96 * (side + 1) + 8 * t, sides_ref, 384 * side + 32 * t)
        return carry

    lax.fori_loop(0, 12, close_all, 0)
    keep.wait()


def finish_kernel(
    moved_hbm,
    sides_ref,
    flags_hbm,
    cells_hbm,
    table_hbm,
    mix_ref,
    fluid_ref,
    moved_ref,
    flags_ref,
    cells_ref,
    table_ref,
    in_sem,
    sums,
    send,
    recv,
):
    ahead, behind, up, down = neighbours()
    inputs = [
        pltpu.make_async_copy(source, target, in_sem.at[at])
        for at, (source, target) in enumerate(
            (
                (moved_hbm, moved_ref),
                (flags_hbm, flags_ref),
                (cells_hbm, cells_ref),
                (table_hbm, table_ref),
            )
        )
    ]
    for copy in inputs:
        copy.start()
    greet((ahead, behind, up, down))
    copies = []
    span = sides_ref.shape[0] // 3
    blocks = span // 4
    for at, device in ((0, behind), (1, up), (2, down)):
        copy = pltpu.make_async_remote_copy(
            src_ref=sides_ref.at[span * at : span * at + span],
            dst_ref=mix_ref.at[span * at : span * at + span],
            send_sem=send.at[at],
            recv_sem=recv.at[at],
            device_id=device,
            device_id_type=MESH,
        )
        copy.start()
        copies.append(copy)

    for copy in inputs:
        copy.wait()
    square = jnp.concatenate([table_ref[:, 16 * a : 16 * a + 16] for a in range(16)], axis=0)
    table = jnp.concatenate(split3(square), axis=0).astype(bf16)
    sums[...] = jnp.zeros_like(sums)
    sub = iota((16, 128), 0)

    def cells_of(g, carry):
        at = pl.ds(pl.multiple_of(g * 8, 8), 8)
        temper = moved_ref[rows_of(g * 8, 6), :]
        radius = moved_ref[rows_of(g * 8, 7), :]
        volume = 4.0 / 3.0 * math.pi * radius * radius * radius
        cell = cells_ref[at, :]
        high = lax.shift_right_logical(cell, 4)
        low = cell & 15
        fluid = []
        hots = []
        for c in range(8):
            hot_high = (sub == high[c : c + 1]).astype(f32)
            hot_low = (sub == low[c : c + 1]).astype(f32)
            parts = jnp.dot(table, hot_low.astype(bf16), preferred_element_type=f32)
            value = parts[0:16] + parts[16:32] + parts[32:48]
            fluid.append(jnp.sum(value * hot_high, axis=0, keepdims=True))
            hots.append((hot_high, hot_low))
        flow = film_gain * radius * radius * (temper - jnp.concatenate(fluid, axis=0))
        pieces = split3(volume) + split3(flow)
        total = sums[...]
        for c in range(8):
            hot_high, hot_low = hots[c]
            spread = jnp.concatenate([hot_low * piece[c : c + 1] for piece in pieces], axis=0)
            total = total + dot_tt(hot_high.astype(bf16), spread.astype(bf16))
        sums[...] = total
        wall = wall_gain * flags_ref[at, :].astype(f32) * (wall_temp - temper) * radius
        mix_ref[pl.ds(pl.multiple_of(3 * span + g * 8, 8), 8), :] = wall - flow
        mix_ref[pl.ds(pl.multiple_of(3 * span + blocks + g * 8, 8), 8), :] = 1.0 / volume
        return carry

    lax.fori_loop(0, 12, cells_of, 0)
    total = sums[...]
    solid = (total[:, 0:16] + total[:, 16:32] + total[:, 32:48]) / cell_volume
    heat = total[:, 48:64] + total[:, 64:80] + total[:, 80:96]
    for a in range(16):
        fluid_ref[0:1, 16 * a : 16 * a + 16] = solid[a : a + 1]
        fluid_ref[1:2, 16 * a : 16 * a + 16] = heat[a : a + 1]
    for copy in copies:
        copy.wait()


def rates_kernel(
    own_hbm, mix_hbm, fluid_hbm, rates_ref, fluid_ref, own, mix, fluid, sem
):
    copies = [
        pltpu.make_async_copy(source, target, sem.at[at])
        for at, (source, target) in enumerate(
            ((mix_hbm, mix), (own_hbm, own), (fluid_hbm, fluid))
        )
    ]
    for copy in copies:
        copy.start()
    for copy in copies:
        copy.wait()
    fluid_ref[...] = fluid[...]
    span = own.shape[0]
    blocks = span // 4

    def combine(g, carry):
        at = pl.multiple_of(g * 8, 8)
        inverse = mix[pl.ds(3 * span + blocks + at, 8), :]
        for c in range(4):
            here = pl.ds(g * 32 + c, 8, 4)
            value = own[here, :]
            for side in range(3):
                value = value + mix[pl.ds(span * side + g * 32 + c, 8, 4), :]
            if c == 3:
                value = value + mix[pl.ds(3 * span + at, 8), :]
            value = value * inverse
            if c == 2:
                value = value - gravity
            rates_ref[here, :] = value
        return carry

    lax.fori_loop(0, blocks // 8, combine, 0, unroll=4)


def anywhere():
    return pl.BlockSpec(memory_space=pl.ANY)


def vmem():
    return pl.BlockSpec(memory_space=pltpu.VMEM)


def shards(state, leaving, pairs, counts, wall_flags, cell_index, fluid_temp):
    mine = state[0, 0]
    blocks = mine.shape[0]
    count = leaving.shape[2]
    lanes = -(-pairs.shape[3] // 128) * 128
    cols, lists, wide = pl.pallas_call(
        halo_kernel,
        out_shape=(
            jax.ShapeDtypeStruct((4, blocks, 8, 128), f32),
            jax.ShapeDtypeStruct((4, 8, 128), i32),
            jax.ShapeDtypeStruct((16, 128), f32),
        ),
        in_specs=[anywhere()] * 4,
        out_specs=(anywhere(), vmem(), vmem()),
        scratch_shapes=[
            pltpu.SMEM(leaving.shape[2:], i32),
            pltpu.SMEM(counts.shape[2:], i32),
            pltpu.VMEM(pairs.shape[2:], i32),
            pltpu.VMEM((count + blocks, 8, 128), f32),
            pltpu.VMEM((count, 8, 128), f32),
            pltpu.VMEM((blocks, 8, 128), f32),
            pltpu.VMEM((8, lanes), i32),
            pltpu.VMEM((8, 128), i32),
            pltpu.SMEM((8, 128), i32),
            pltpu.SemaphoreType.DMA,
            pltpu.SemaphoreType.DMA,
            pltpu.SemaphoreType.DMA((3,)),
            pltpu.SemaphoreType.DMA((3,)),
            pltpu.SemaphoreType.DMA((3,)),
            pltpu.SemaphoreType.DMA((3,)),
            pltpu.SemaphoreType.DMA,
            pltpu.SemaphoreType.DMA((4,)),
            pltpu.VMEM((8, 128), f32),
            pltpu.SemaphoreType.DMA((3,)),
            pltpu.SemaphoreType.DMA((3,)),
            pltpu.SemaphoreType.DMA((2 * reach,)),
            pltpu.SemaphoreType.DMA((2 * reach,)),
        ],
        compiler_params=pltpu.CompilerParams(
            collective_id=0, has_side_effects=True, vmem_limit_bytes=vmem_grant
        ),
        name="halo",
    )(leaving[0, 0], counts[0, 0], pairs[0, 0], mine)

    moved, own, sides = pl.pallas_call(
        pair_kernel,
        out_shape=(
            jax.ShapeDtypeStruct((8 * blocks, 128), f32),
            jax.ShapeDtypeStruct((4 * blocks, 128), f32),
            jax.ShapeDtypeStruct((12 * blocks, 128), f32),
        ),
        in_specs=[anywhere()] * 3,
        out_specs=(anywhere(), vmem(), vmem()),
        scratch_shapes=[
            pltpu.SMEM((4096,), i32),
            pltpu.VMEM((32 * blocks, 128), f32),
            pltpu.VMEM((16, 128), f32),
            pltpu.VMEM((3 * blocks, 128, 128), bf16),
            pltpu.VMEM((4 * blocks, 32, 256), bf16),
            pltpu.VMEM((4 * blocks, 16, 128), bf16),
            pltpu.VMEM((3 * blocks // 8, 128, 128), f32),
            pltpu.VMEM((32 * blocks, 128), f32),
            pltpu.VMEM((32 * blocks, 128), f32),
            pltpu.VMEM((3, 256, 128), bf16),
            pltpu.VMEM((32 * blocks + 8, 128), f32),
            pltpu.SemaphoreType.DMA((4,)),
        ]
        + [pltpu.VMEM((128, 256), f32)] * ring
        + [pltpu.VMEM((256, 256), bf16)] * ring,
        compiler_params=pltpu.CompilerParams(vmem_limit_bytes=vmem_grant),
        name="contact",
    )(lists.reshape(4096), cols.reshape(32 * blocks, 128), wide)

    mix, fluid = pl.pallas_call(
        finish_kernel,
        out_shape=(
            jax.ShapeDtypeStruct((14 * blocks, 128), f32),
            jax.ShapeDtypeStruct((2, 256), f32),
        ),
        in_specs=[anywhere()] * 5,
        out_specs=(vmem(), vmem()),
        scratch_shapes=[
            pltpu.VMEM((8 * blocks, 128), f32),
            pltpu.VMEM((blocks, 128), i32),
            pltpu.VMEM((blocks, 128), i32),
            pltpu.VMEM((1, 256), f32),
            pltpu.SemaphoreType.DMA((4,)),
            pltpu.VMEM((16, 96), f32),
            pltpu.SemaphoreType.DMA((3,)),
            pltpu.SemaphoreType.DMA((3,)),
        ],
        compiler_params=pltpu.CompilerParams(
            collective_id=1, has_side_effects=True, vmem_limit_bytes=vmem_grant
        ),
        name="finish",
    )(moved, sides, wall_flags[0, 0], cell_index[0, 0], fluid_temp.reshape(1, 256))

    rates, fluid = pl.pallas_call(
        rates_kernel,
        out_shape=(
            jax.ShapeDtypeStruct((4 * blocks, 128), f32),
            jax.ShapeDtypeStruct((2, 256), f32),
        ),
        in_specs=[anywhere()] * 3,
        out_specs=(vmem(), vmem()),
        scratch_shapes=[
            pltpu.VMEM((4 * blocks, 128), f32),
            pltpu.VMEM((14 * blocks, 128), f32),
            pltpu.VMEM((2, 256), f32),
            pltpu.SemaphoreType.DMA((3,)),
        ],
        compiler_params=pltpu.CompilerParams(vmem_limit_bytes=vmem_grant),
        name="rates",
    )(own, mix, fluid)
    return (
        moved.reshape(1, 1, blocks, 8, 128),
        rates.reshape(1, 1, blocks, 4, 128),
        fluid[None, None],
    )


def solution(mesh):
    in_specs = (
        P("gx", "gy", None, None, None),
        P("gx", "gy", None),
        P("gx", "gy", None, None),
        P("gx", "gy", None),
        P("gx", "gy", None, None),
        P("gx", "gy", None, None),
        P("gx", "gy", None),
    )
    out_specs = (
        P("gx", "gy", None, None, None),
        P("gx", "gy", None, None, None),
        P("gx", "gy", None, None),
    )
    return jax.shard_map(shards, mesh=mesh, in_specs=in_specs, out_specs=out_specs, check_vma=False)
```

```python
import functools
import math

import jax
import jax.numpy as jnp
from jax import lax
from jax.experimental import pallas as pl
from jax.experimental.pallas import tpu as pltpu
from jax.sharding import PartitionSpec as P

soften = 0.01
stiffness = 0.2
damping = 0.05
conductance = 0.05
film_gain = 0.5
wall_gain = 2.0
wall_temp = 1.0
gravity = 1.0
cell_volume = 32.0

f32 = jnp.float32
bf16 = jnp.bfloat16
i32 = jnp.int32

tiny = 1e-30
group = 16
lag_a = 2
lag_b = 2
ring = lag_a + lag_b
reach = 4
lateness = (50.0, 28.0, 22.0, 125.0, 20.0, 0.0, 0.0, 0.0, 0.0, 0.0, 0.0, 0.0, 30.0, 0.0, 0.0, 25.0)
early = 80
early_turn = 7
vmem_grant = 56 * 2**20
MESH = pl.DeviceIdType.MESH


def iota(shape, dim):
    return lax.broadcasted_iota(i32, shape, dim)


def split2(value):
    hi = value.astype(bf16).astype(f32)
    return hi, (value - hi).astype(bf16).astype(f32)


def split3(value):
    hi = value.astype(bf16).astype(f32)
    rest = value - hi
    mid = rest.astype(bf16).astype(f32)
    return hi, mid, rest - mid


def dot_tt(left, right):
    return lax.dot_general(left, right, (((1,), (1,)), ((), ())), preferred_element_type=f32)


def neighbours():
    a = lax.axis_index("gx")
    b = lax.axis_index("gy")
    na = lax.axis_size("gx")
    nb = lax.axis_size("gy")
    return (
        {"gx": lax.rem(a + 1, na)},
        {"gx": lax.rem(a + na - 1, na)},
        {"gy": lax.rem(b + 1, nb)},
        {"gy": lax.rem(b + nb - 1, nb)},
    )


def greet(everyone):
    barrier = pltpu.get_barrier_semaphore()
    for device in everyone:
        pl.semaphore_signal(barrier, inc=1, device_id=device, device_id_type=MESH)
    pl.semaphore_wait(barrier, len(everyone))


def sort_pairs(lanes, pad, total):
    own = pad[0:1, :]
    code = pad[1:2, :]
    region = jnp.zeros_like(code)
    for step in range(1, 9):
        region = region + (code >= 96 * step).astype(i32)
    far = code - 96 * region
    live = iota((1, lanes), 1) < total

    def among(*names):
        hit = region == names[0]
        for name in names[1:]:
            hit = hit | (region == name)
        return hit

    kind = jnp.where(
        among(4),
        0,
        jnp.where(among(1, 5), 1, jnp.where(among(0, 3), 2, jnp.where(among(2), 3, 4))),
    )
    kind = jnp.where(live, kind, 5)
    u_far = among(0, 1, 2, 3)
    u = jnp.where(u_far, far, own) + jnp.where(among(4, 5, 3), 0, 96)
    v_slot = jnp.where(u_far, own, far)
    v_side = jnp.where(among(4, 1, 7), 0, jnp.where(among(5, 3, 0, 8), 1, 2))
    ranks = iota((8, lanes), 0)
    marks = (ranks == kind).astype(f32)
    before = (iota((lanes, lanes), 0) < iota((lanes, lanes), 1)).astype(bf16)
    seen = jnp.dot(marks.astype(bf16), before, preferred_element_type=f32)
    starts = jnp.sum((kind < ranks).astype(f32), axis=1, keepdims=True)
    place = jnp.sum(marks * (seen + starts), axis=0, keepdims=True)
    target = (iota((lanes, lanes), 0).astype(f32) == place).astype(bf16)
    rows = iota((8, lanes), 0)
    values = jnp.where(
        rows == 0, u, jnp.where(rows == 1, v_slot, jnp.where(rows == 2, v_side, 0))
    )
    moved = dot_tt(values.astype(bf16), target)
    packed = moved[0:1] + 512.0 * (moved[1:2] + 96.0 * moved[2:3])
    diag = iota((8, 128), 0) == iota((8, 128), 1)
    begin = jnp.sum(jnp.where(diag, starts, 0.0), axis=0, keepdims=True)
    return packed.astype(i32), begin.astype(i32)


def own_pairs(list_smem, refs, rings, early_ref):
    cols_ref, U, V, L, RT = refs[0:5]
    AB = rings[0:ring]
    M = rings[ring : 2 * ring]
    build_own_tables(refs)

    def entry(k):
        k = jnp.minimum(k, early - 1)
        code = list_smem[lax.shift_right_logical(k, 7), k & 127]
        u = jnp.minimum(code & 511, 95)
        v = jnp.minimum(lax.shift_right_logical(code, 9), 95)
        return u, v

    def same(block):
        return block

    distances, weights, both = pair_machine(entry, same, same, cols_ref, U, V, L, RT, AB, M)
    for q in range(ring):
        distances(q, q)
    for q in range(lag_b):
        weights(q, q)

    def turn(t, carry):
        for q in range(group):
            k = t * group + q
            _, _, to_first, to_second = both(k, q % ring)
            early_ref[tile(2 * k), :] = to_first
            early_ref[tile(2 * k + 1), :] = to_second
            weights(k + lag_b, (q + lag_b) % ring)
            distances(k + ring, q % ring)
        return carry

    lax.fori_loop(0, early // group, turn, 0)


def halo_kernel(
    leaving_hbm,
    counts_hbm,
    pairs_hbm,
    state_hbm,
    cols_ref,
    lists_ref,
    wide_ref,
    early_ref,
    leaving_ref,
    counts_ref,
    pairs_ref,
    cat,
    dep,
    moved,
    pad,
    slot_vec,
    slot_smem,
    dep_send,
    dep_recv,
    list_send,
    list_recv,
    col_send,
    col_recv,
    local_sem,
    in_sem,
    near,
    near_send,
    near_recv,
    wide_send,
    wide_recv,
    list_smem,
    U,
    V,
    L,
    RT,
    extra,
    pieces,
    natural,
    *rings,
):
    blocks = state_hbm.shape[0]
    count = leaving_hbm.shape[0]
    ahead, behind, up, down = neighbours()
    state_ref = cat.at[count : count + blocks]
    inputs = [
        pltpu.make_async_copy(source, target, in_sem.at[at])
        for at, (source, target) in enumerate(
            (
                (leaving_hbm, leaving_ref),
                (state_hbm, state_ref),
                (pairs_hbm, pairs_ref),
                (counts_hbm, counts_ref),
            )
        )
    ]
    for copy in inputs:
        copy.start()
    a = lax.axis_index("gx")
    na = lax.axis_size("gx")
    along = {
        step: {"gx": lax.rem(a + step + na, na)} for step in range(-reach, reach + 1) if step
    }
    wide_ref[...] = jnp.zeros_like(wide_ref)
    for copy in inputs:
        copy.wait()
    local = jnp.maximum(counts_ref[0] - early, 0).astype(f32)
    far = (counts_ref[1] - counts_ref[0]).astype(f32) * 0.125
    lane = iota((1, 128), 1)
    near[0:1, :] = jnp.where(lane < 64, far, local)
    for m in range(count):
        dep[m] = state_ref[leaving_ref[m]]
    b = lax.axis_index("gy")
    nb = lax.axis_size("gy")
    across = {"gy": lax.rem(b + 2, nb)}
    greet((up, down, across, *along.values()))
    asks = []
    for at, device in ((1, down), (2, up), (3, across)):
        copy = pltpu.make_async_remote_copy(
            src_ref=near.at[0:1],
            dst_ref=near.at[at : at + 1],
            send_sem=near_send.at[at - 1],
            recv_sem=near_recv.at[at - 1],
            device_id=device,
            device_id_type=MESH,
        )
        copy.start()
        asks.append(copy)
    depart = pltpu.make_async_remote_copy(
        src_ref=dep,
        dst_ref=cat.at[0:count],
        send_sem=dep_send,
        recv_sem=dep_recv,
        device_id=ahead,
        device_id_type=MESH,
    )
    depart.start()
    place = iota((8, 128), 1)
    slot = place + count
    for m in range(count):
        slot = jnp.where(place == leaving_ref[m], m, slot)
    slot_vec[...] = slot
    to_smem = pltpu.make_async_copy(slot_vec, slot_smem, local_sem)
    to_smem.start()
    lanes = pad.shape[1]
    pad[...] = jnp.zeros_like(pad)
    pad[0:2, 0 : pairs_ref.shape[1]] = pairs_ref[...]
    packed, begin = sort_pairs(lanes, pad, counts_ref[1])
    lists_ref[0] = jnp.zeros((8, 128), i32)
    for row in range(lanes // 128):
        lists_ref[0, row : row + 1, :] = packed[:, 128 * row : 128 * row + 128]
    lists_ref[0, 6:7, :] = begin
    copies = []
    for copy in asks:
        copy.wait()
    turn = lane & 3
    row = near[0:1, :]
    for at, step in ((1, 1), (2, nb - 1), (3, 2)):
        row = jnp.where(turn == lax.rem(b + step, nb), near[at : at + 1, :], row)
    wide_ref[reach : reach + 1, :] = row
    for at, step in enumerate(along):
        copy = pltpu.make_async_remote_copy(
            src_ref=wide_ref.at[reach : reach + 1],
            dst_ref=wide_ref.at[reach - step : reach - step + 1],
            send_sem=wide_send.at[at],
            recv_sem=wide_recv.at[at],
            device_id=along[step],
            device_id_type=MESH,
        )
        copy.start()
        copies.append(copy)
    for at, device in ((1, down), (2, up), (3, ahead)):
        copy = pltpu.make_async_remote_copy(
            src_ref=lists_ref.at[0],
            dst_ref=lists_ref.at[at],
            send_sem=list_send.at[at - 1],
            recv_sem=list_recv.at[at - 1],
            device_id=device,
            device_id_type=MESH,
        )
        copy.start()
        copies.append(copy)
    to_smem.wait()
    own_list = pltpu.make_async_copy(lists_ref.at[0], list_smem, local_sem)
    own_list.start()
    own_list.wait()
    depart.wait()

    def place_block(j, carry):
        moved[tile(j), :] = cat[slot_smem[0, j]]
        return carry

    lax.fori_loop(0, blocks, place_block, 0)
    keep = pltpu.make_async_copy(moved, cols_ref.at[0], local_sem)
    keep.start()
    for at, device in ((1, ahead), (2, down), (3, up)):
        copy = pltpu.make_async_remote_copy(
            src_ref=moved,
            dst_ref=cols_ref.at[at],
            send_sem=col_send.at[at - 1],
            recv_sem=col_recv.at[at - 1],
            device_id=device,
            device_id_type=MESH,
        )
        copy.start()
        copies.append(copy)
    keep.wait()
    own_pairs(
        list_smem, (moved, U, V, L, RT, extra, pieces, natural), rings, early_ref
    )
    for copy in copies:
        copy.wait()


def rows_of(base, c):
    return pl.ds(base * 8 + c, 8, 8)


def tile(i):
    return pl.ds(pl.multiple_of(i * 8, 8), 8)


def table_steps(cols_ref, U, V, L, RT, extra, pieces, natural, never):
    rows = iota((8, 128), 0)
    eye = (iota((128, 128), 0) == iota((128, 128), 1)).astype(bf16)
    eyes = jnp.concatenate([eye, eye, eye], axis=1)
    c6 = jnp.where(rows == 6, 1.0, 0.0)
    c7 = jnp.where(rows == 7, 0.25, 0.0)
    ca = jnp.where(rows < 3, -2.0, 0.0)
    cb = jnp.where(rows < 6, -0.25, 0.0)
    ones = jnp.where(rows < 6, 1.0, 0.0)

    def dense(base):
        x = [cols_ref[rows_of(base, c), :] for c in range(3)]
        v = [cols_ref[rows_of(base, c), :] for c in range(3, 6)]
        radius = cols_ref[rows_of(base, 7), :]
        root = jnp.sqrt(radius)
        square = x[0] * x[0] + x[1] * x[1] + x[2] * x[2] + 0.5 * soften
        dot = x[0] * v[0] + x[1] * v[1] + x[2] * v[2]
        extra[rows_of(base, 3), :] = jnp.ones((8, 128), f32)
        extra[rows_of(base, 4), :] = root * cols_ref[rows_of(base, 6), :]
        extra[rows_of(base, 5), :] = root
        extra[rows_of(base, 6), :] = square
        extra[rows_of(base, 7), :] = dot
        for c, piece in enumerate(split3(square) + split3(0.25 * dot)):
            pieces[rows_of(base, c), :] = piece

    def swap(value):
        return jnp.where(rows < 3, pltpu.roll(value, 5, 0), pltpu.roll(value, 3, 0))

    def eight(base, shift, at, held=None):
        for q in range(8):
            i = base + q
            S = cols_ref[tile(i), :]
            if held is not None:
                S = jnp.where(never, held, S)
            E = extra[tile(i), :]
            G = pieces[tile(i), :]
            hi, mid = split2(jnp.where(rows < 3, S, jnp.where(rows < 6, E, 0.0)))
            L[i] = jnp.concatenate([hi, mid], axis=0).astype(bf16)
            full = jnp.where(rows < 6, S, E)
            hi, mid = split2(full)
            if at is not None:
                low = jnp.where(rows < 6, hi, full - hi - mid)
                natural[at, 32 * q : 32 * q + 32, :] = jnp.concatenate(
                    [hi, low, mid, ones], axis=0
                ).astype(bf16)
            a0 = hi * ca + c6
            a1 = mid * ca + c6
            b0 = swap(hi) * cb + c7
            b1 = swap(mid) * cb + c7
            A = jnp.concatenate([a0, a1, a0, jnp.where(rows < 3, G, 0.0)], axis=0)
            B = jnp.concatenate(
                [b0, b1, b0, jnp.where((rows >= 3) & (rows < 6), G, 0.0)], axis=0
            )
            V[i + shift, :, 0:128] = A.astype(bf16)
            V[i + shift, :, 128:256] = B.astype(bf16)

    def turn(at, u_base):
        turned = dot_tt(eye, natural[at]).astype(bf16)
        for q in range(8):
            U[u_base + q, :, 0:32] = turned[:, 32 * q : 32 * q + 32]

    def column(base, u_base):
        radius = cols_ref[rows_of(base, 7), :]
        three = jnp.concatenate(split3(radius), axis=1).astype(bf16)
        RT[lax.shift_right_logical(u_base, 3), :, 0:8] = dot_tt(eyes, three)

    return dense, eight, turn, column


def build_tables(refs, first, start, step):
    dense, eight, turn, column = table_steps(*refs, first < 0)
    cols_ref, U = refs[0:2]

    def turns(t):
        turn(0, 8 * t)
        turn(1, 96 + 8 * t)
        turn(2, 192 + 8 * t)
        column(8 * t, 8 * t)
        column(96 + 8 * t, 96 + 8 * t)
        column(288 + 8 * t, 192 + 8 * t)

    def body(t, carry):
        turns(jnp.maximum(t - 1, 0))
        for col in range(4):
            dense(96 * col + 8 * t)
        eight(8 * t, 0, 0)
        eight(96 + 8 * t, 192, 1)
        eight(288 + 8 * t, -96, 2)
        held = U[first & 63, 0:16, :].astype(f32)[0:8]
        eight(192 + 8 * t, -96, None, held)
        return step(t, carry)

    count = cols_ref.shape[0] // 256
    carry = lax.fori_loop(0, count, body, start)
    turns(count - 1)
    return carry


def build_own_tables(refs):
    dense, eight, turn, column = table_steps(*refs, None)

    def body(t, carry):
        dense(8 * t)
        eight(8 * t, 0, 0)
        turn(0, 8 * t)
        column(8 * t, 8 * t)
        return carry

    lax.fori_loop(0, refs[0].shape[0] // 64, body, 0)


def shares(wide):
    rows = iota((8, 128), 0)
    lanes = iota((8, 128), 1)
    b = lax.axis_index("gy")
    nb = lax.axis_size("gy")
    own = wide[1:9, :]
    behind = wide[0:8, :]
    far = jnp.where(lanes < 64, own, pltpu.roll(behind, 64, 1))
    local = jnp.where(lanes < 64, pltpu.roll(own, 64, 1), behind)
    load = (
        local
        + 2.0 * far
        + 2.0 * pltpu.roll(far, 127, 1)
        + pltpu.roll(far, 1, 1)
        + 3.0 * jnp.where(rows == 0, far, pltpu.roll(far, 1, 0))
    )
    column = lax.axis_index("gx") + rows - (reach - 1) - jnp.where(lanes < 64, 0, 1)
    phase = (column + 32) & 15
    for at, late in enumerate(lateness):
        load = load + jnp.where(phase == at, late, 0.0)
    passing = jnp.where(rows < 7, local, 0.0)

    def step(given):
        ahead, up = given
        now = load - ahead - up + pltpu.roll(ahead, 1, 0) + pltpu.roll(up, 1, 1)
        ahead = ahead + 0.26 * (now - pltpu.roll(now, 7, 0))
        ahead = jnp.minimum(jnp.maximum(ahead, 0.0), jnp.maximum(passing - up, 0.0))
        up = up + 0.26 * (now - pltpu.roll(now, 127, 1))
        up = jnp.minimum(jnp.maximum(up, 0.0), jnp.maximum(local - ahead, 0.0))
        return ahead, up

    def value(given, shift, base):
        column = lax.rem(b + shift + nb, nb)
        picked = (rows == reach - 1) & (lanes == column + base)
        return jnp.sum(jnp.where(picked, given, 0.0)).astype(i32)

    start = jnp.zeros((8, 128), f32)
    return (start, start), step, value


def pair_machine(entry, spot, spot_u, cols_ref, U, V, L, RT, AB, M):
    def distances(k, at):
        u, v = entry(k)
        AB[at][...] = jnp.dot(U[u, :, 0:32], V[v], preferred_element_type=f32)

    def weights(k, at):
        u, v = entry(k)
        rt = cols_ref[pl.ds(spot(v) * 8 + 7, 1), :]
        lane = jnp.full((8, 128), u & 7, i32)
        eighth = lax.shift_right_logical(u, 3)

        def radius(r):
            return jnp.take_along_axis(RT[eighth, r : r + 8, :], lane, axis=1)

        for r in range(0, 128, 16):
            A = AB[at][r : r + 16, 0:128]
            B = AB[at][r : r + 16, 128:256]
            R = jnp.concatenate([radius(r), radius(r + 8)], axis=0) + rt
            inv = lax.rsqrt(A)
            gap = R - A * inv
            inter = jnp.maximum(gap, 0.0)
            root = inter * lax.rsqrt(jnp.maximum(gap, tiny))
            W = (root * inv) * (inter - B * inv)
            G = root * lax.rsqrt(R)
            wh = W.astype(bf16)
            gh = G.astype(bf16)
            M[at][r : r + 16, 0:128] = wh
            M[at][r : r + 16, 128:256] = gh
            M[at][128 + r : 144 + r, 0:128] = (W - wh.astype(f32)).astype(bf16)
            M[at][128 + r : 144 + r, 128:256] = (G - gh.astype(f32)).astype(bf16)

    rows = iota((8, 128), 0)

    def folded(out):
        both = out[0:8] + out[8:16]
        return jnp.where(rows < 4, both[:, 0:128], both[:, 128:256])

    def both(k, at):
        u, v = entry(k)
        w = spot(v)
        o = spot_u(u)
        first = jnp.concatenate([L[o], L[o]], axis=1)
        second = jnp.concatenate([L[w], L[w]], axis=1)
        m = M[at]
        crossed = jnp.concatenate(
            [
                jnp.concatenate([m[0:128, 0:128], m[128:256, 0:128]], axis=1),
                jnp.concatenate([m[0:128, 128:256], m[128:256, 128:256]], axis=1),
            ],
            axis=0,
        )
        to_second = folded(jnp.dot(first, m[...], preferred_element_type=f32))
        to_first = folded(dot_tt(second, crossed))
        return o, w, to_first, to_second

    return distances, weights, both


def pair_kernel(
    lists_hbm,
    cols_hbm,
    wide_hbm,
    early_hbm,
    moved_ref,
    own_ref,
    sides_ref,
    lists_ref,
    cols_ref,
    wide,
    U,
    V,
    L,
    RT,
    extra,
    pieces,
    natural,
    acc,
    before,
    sem,
    *rings,
):
    AB = rings[0:ring]
    M = rings[ring : 2 * ring]
    copies = [
        pltpu.make_async_copy(source, target, sem.at[at])
        for at, (source, target) in enumerate(
            (
                (cols_hbm, cols_ref),
                (lists_hbm, lists_ref),
                (wide_hbm, wide),
                (early_hbm, before.at[0 : 16 * early]),
            )
        )
    ]
    for copy in copies:
        copy.start()
    trash = acc.shape[0] // 8 - 1
    acc[...] = jnp.zeros_like(acc)
    for copy in copies:
        copy.wait()
    keep = pltpu.make_async_copy(cols_ref.at[0:768], moved_ref, sem.at[4])
    keep.start()
    given, step, value = shares(wide)
    first = lists_ref[0]
    done = jnp.minimum(lists_ref[6 * 128 + 1], early)

    def turn_in(t, carry):
        for q in range(early_turn):
            k = t * early_turn + q
            live = k < done
            code = lists_ref[k]
            o = jnp.where(live, code & 511, trash)
            w = jnp.where(live, lax.shift_right_logical(code, 9), trash)
            acc[tile(o), :] += before[tile(2 * k), :]
            acc[tile(w), :] += before[tile(2 * k + 1), :]
        return step(carry)

    refs = (cols_ref, U, V, L, RT, extra, pieces, natural)
    given = build_tables(refs, first, given, turn_in)
    ahead_out = value(given[0], 0, 32)
    up_out = value(given[1], 0, 32)
    ahead_in = value(given[0], 0, 96)
    ahead_down = value(given[0], -1, 32)
    up_in = value(given[1], -1, 32)

    def begin(at, name):
        return lists_ref[at * 1024 + 6 * 128 + name]

    def cut(at, first, second):
        end = begin(at, 1)
        low = jnp.minimum(end, early)
        first = jnp.minimum(low + first, end)
        return low, first, jnp.minimum(first + second, end)

    _, _, kept = cut(0, ahead_out, up_out)
    ahead_low, ahead_high, _ = cut(3, ahead_in, 0)
    _, up_low, up_high = cut(2, ahead_down, up_in)
    ends = []
    shifts = []
    so_far = 0
    for at, low, high in (
        (0, kept, begin(0, 1)),
        (0, begin(0, 1), begin(0, 2)),
        (1, begin(1, 2), begin(1, 3)),
        (2, begin(2, 3), begin(2, 4)),
        (3, begin(3, 4), begin(3, 5)),
        (3, ahead_low, ahead_high),
        (2, up_low, up_high),
    ):
        shifts.append(at * 1024 + low - so_far)
        so_far = so_far + (high - low)
        ends.append(so_far)
    n = so_far
    last = jnp.maximum(n - 1, 0)

    def entry(k):
        k = jnp.minimum(k, last)
        shift = shifts[6]
        for at in range(5, -1, -1):
            shift = jnp.where(k < ends[at], shifts[at], shift)
        code = lists_ref[k + shift]
        code = code + jnp.where(
            k < ends[4], 0, jnp.where(k < ends[5], 96 + 512 * 288, 192 + 512 * 192)
        )
        return code & 511, lax.shift_right_logical(code, 9)

    def spot_u(u):
        return jnp.where(u < 192, u, u + 96)

    def spot(v):
        return jnp.where(v < 96, v, jnp.where(v < 288, v + 96, v - 192))

    distances, weights, both = pair_machine(entry, spot, spot_u, cols_ref, U, V, L, RT, AB, M)

    def sums(k, at):
        o, w, to_first, to_second = both(k, at)
        live = k < n
        o = jnp.where(live, o, trash)
        w = jnp.where(live, w, trash)
        acc[tile(o), :] += to_first
        acc[tile(w), :] += to_second

    for q in range(ring):
        distances(q, q)
    for q in range(lag_b):
        weights(q, q)

    def turn(t, carry):
        for q in range(group):
            k = t * group + q
            sums(k, q % ring)
            weights(k + lag_b, (q + lag_b) % ring)
            distances(k + ring, q % ring)
        return carry

    lax.fori_loop(0, lax.div(n + group - 1, group), turn, 0)

    def close(base, out_ref, out_base):
        got = [acc[rows_of(base, c), :] for c in range(6)]
        terms = []
        for c in range(3):
            hi, mid = split2(cols_ref[rows_of(base, c), :])
            terms.append(stiffness * ((hi + mid) * got[3] - got[c]))
        root = conductance * extra[rows_of(base, 5), :]
        terms.append(root * (got[4] - cols_ref[rows_of(base, 6), :] * got[5]))
        for c in range(4):
            out_ref[pl.ds(out_base + c, 8, 4), :] = terms[c]

    def close_all(t, carry):
        close(8 * t, own_ref, 32 * t)
        for side in range(3):
            close(96 * (side + 1) + 8 * t, sides_ref, 384 * side + 32 * t)
        return carry

    lax.fori_loop(0, 12, close_all, 0)
    keep.wait()


def finish_kernel(
    moved_hbm,
    sides_ref,
    flags_hbm,
    cells_hbm,
    table_hbm,
    mix_ref,
    fluid_ref,
    moved_ref,
    flags_ref,
    cells_ref,
    table_ref,
    in_sem,
    sums,
    send,
    recv,
):
    ahead, behind, up, down = neighbours()
    inputs = [
        pltpu.make_async_copy(source, target, in_sem.at[at])
        for at, (source, target) in enumerate(
            (
                (moved_hbm, moved_ref),
                (flags_hbm, flags_ref),
                (cells_hbm, cells_ref),
                (table_hbm, table_ref),
            )
        )
    ]
    for copy in inputs:
        copy.start()
    greet((ahead, behind, up, down))
    copies = []
    span = sides_ref.shape[0] // 3
    blocks = span // 4
    for at, device in ((0, behind), (1, up), (2, down)):
        copy = pltpu.make_async_remote_copy(
            src_ref=sides_ref.at[span * at : span * at + span],
            dst_ref=mix_ref.at[span * at : span * at + span],
            send_sem=send.at[at],
            recv_sem=recv.at[at],
            device_id=device,
            device_id_type=MESH,
        )
        copy.start()
        copies.append(copy)

    for copy in inputs:
        copy.wait()
    square = jnp.concatenate([table_ref[:, 16 * a : 16 * a + 16] for a in range(16)], axis=0)
    table = jnp.concatenate(split3(square), axis=0).astype(bf16)
    sums[...] = jnp.zeros_like(sums)
    sub = iota((16, 128), 0)

    def cells_of(g, carry):
        at = pl.ds(pl.multiple_of(g * 8, 8), 8)
        temper = moved_ref[rows_of(g * 8, 6), :]
        radius = moved_ref[rows_of(g * 8, 7), :]
        volume = 4.0 / 3.0 * math.pi * radius * radius * radius
        cell = cells_ref[at, :]
        high = lax.shift_right_logical(cell, 4)
        low = cell & 15
        fluid = []
        hots = []
        for c in range(8):
            hot_high = (sub == high[c : c + 1]).astype(f32)
            hot_low = (sub == low[c : c + 1]).astype(f32)
            parts = jnp.dot(table, hot_low.astype(bf16), preferred_element_type=f32)
            value = parts[0:16] + parts[16:32] + parts[32:48]
            fluid.append(jnp.sum(value * hot_high, axis=0, keepdims=True))
            hots.append((hot_high, hot_low))
        flow = film_gain * radius * radius * (temper - jnp.concatenate(fluid, axis=0))
        pieces = split3(volume) + split3(flow)
        total = sums[...]
        for c in range(8):
            hot_high, hot_low = hots[c]
            spread = jnp.concatenate([hot_low * piece[c : c + 1] for piece in pieces], axis=0)
            total = total + dot_tt(hot_high.astype(bf16), spread.astype(bf16))
        sums[...] = total
        wall = wall_gain * flags_ref[at, :].astype(f32) * (wall_temp - temper) * radius
        mix_ref[pl.ds(pl.multiple_of(3 * span + g * 8, 8), 8), :] = wall - flow
        mix_ref[pl.ds(pl.multiple_of(3 * span + blocks + g * 8, 8), 8), :] = 1.0 / volume
        return carry

    lax.fori_loop(0, 12, cells_of, 0)
    total = sums[...]
    solid = (total[:, 0:16] + total[:, 16:32] + total[:, 32:48]) / cell_volume
    heat = total[:, 48:64] + total[:, 64:80] + total[:, 80:96]
    for a in range(16):
        fluid_ref[0:1, 16 * a : 16 * a + 16] = solid[a : a + 1]
        fluid_ref[1:2, 16 * a : 16 * a + 16] = heat[a : a + 1]
    for copy in copies:
        copy.wait()


def rates_kernel(
    own_hbm, mix_hbm, fluid_hbm, rates_ref, fluid_ref, own, mix, fluid, sem
):
    copies = [
        pltpu.make_async_copy(source, target, sem.at[at])
        for at, (source, target) in enumerate(
            ((mix_hbm, mix), (own_hbm, own), (fluid_hbm, fluid))
        )
    ]
    for copy in copies:
        copy.start()
    for copy in copies:
        copy.wait()
    fluid_ref[...] = fluid[...]
    span = own.shape[0]
    blocks = span // 4

    def combine(g, carry):
        at = pl.multiple_of(g * 8, 8)
        inverse = mix[pl.ds(3 * span + blocks + at, 8), :]
        for c in range(4):
            here = pl.ds(g * 32 + c, 8, 4)
            value = own[here, :]
            for side in range(3):
                value = value + mix[pl.ds(span * side + g * 32 + c, 8, 4), :]
            if c == 3:
                value = value + mix[pl.ds(3 * span + at, 8), :]
            value = value * inverse
            if c == 2:
                value = value - gravity
            rates_ref[here, :] = value
        return carry

    lax.fori_loop(0, blocks // 8, combine, 0, unroll=4)


def anywhere():
    return pl.BlockSpec(memory_space=pl.ANY)


def vmem():
    return pl.BlockSpec(memory_space=pltpu.VMEM)


def shards(state, leaving, pairs, counts, wall_flags, cell_index, fluid_temp):
    mine = state[0, 0]
    blocks = mine.shape[0]
    count = leaving.shape[2]
    lanes = -(-pairs.shape[3] // 128) * 128
    cols, lists, wide, ahead_of = pl.pallas_call(
        halo_kernel,
        out_shape=(
            jax.ShapeDtypeStruct((4, 8 * blocks, 128), f32),
            jax.ShapeDtypeStruct((4, 8, 128), i32),
            jax.ShapeDtypeStruct((16, 128), f32),
            jax.ShapeDtypeStruct((16 * early, 128), f32),
        ),
        in_specs=[anywhere()] * 4,
        out_specs=(anywhere(), vmem(), vmem(), vmem()),
        scratch_shapes=[
            pltpu.SMEM(leaving.shape[2:], i32),
            pltpu.SMEM(counts.shape[2:], i32),
            pltpu.VMEM(pairs.shape[2:], i32),
            pltpu.VMEM((count + blocks, 8, 128), f32),
            pltpu.VMEM((count, 8, 128), f32),
            pltpu.VMEM((8 * blocks, 128), f32),
            pltpu.VMEM((8, lanes), i32),
            pltpu.VMEM((8, 128), i32),
            pltpu.SMEM((8, 128), i32),
            pltpu.SemaphoreType.DMA,
            pltpu.SemaphoreType.DMA,
            pltpu.SemaphoreType.DMA((3,)),
            pltpu.SemaphoreType.DMA((3,)),
            pltpu.SemaphoreType.DMA((3,)),
            pltpu.SemaphoreType.DMA((3,)),
            pltpu.SemaphoreType.DMA,
            pltpu.SemaphoreType.DMA((4,)),
            pltpu.VMEM((8, 128), f32),
            pltpu.SemaphoreType.DMA((3,)),
            pltpu.SemaphoreType.DMA((3,)),
            pltpu.SemaphoreType.DMA((2 * reach,)),
            pltpu.SemaphoreType.DMA((2 * reach,)),
            pltpu.SMEM((8, 128), i32),
            pltpu.VMEM((blocks, 128, 128), bf16),
            pltpu.VMEM((blocks, 32, 256), bf16),
            pltpu.VMEM((blocks, 16, 128), bf16),
            pltpu.VMEM((blocks // 8, 128, 128), f32),
            pltpu.VMEM((8 * blocks, 128), f32),
            pltpu.VMEM((8 * blocks, 128), f32),
            pltpu.VMEM((1, 256, 128), bf16),
        ]
        + [pltpu.VMEM((128, 256), f32)] * ring
        + [pltpu.VMEM((256, 256), bf16)] * ring,
        compiler_params=pltpu.CompilerParams(
            collective_id=0, has_side_effects=True, vmem_limit_bytes=vmem_grant
        ),
        name="halo",
    )(leaving[0, 0], counts[0, 0], pairs[0, 0], mine)

    moved, own, sides = pl.pallas_call(
        pair_kernel,
        out_shape=(
            jax.ShapeDtypeStruct((8 * blocks, 128), f32),
            jax.ShapeDtypeStruct((4 * blocks, 128), f32),
            jax.ShapeDtypeStruct((12 * blocks, 128), f32),
        ),
        in_specs=[anywhere()] * 4,
        out_specs=(anywhere(), vmem(), vmem()),
        scratch_shapes=[
            pltpu.SMEM((4096,), i32),
            pltpu.VMEM((32 * blocks, 128), f32),
            pltpu.VMEM((16, 128), f32),
            pltpu.VMEM((3 * blocks, 128, 128), bf16),
            pltpu.VMEM((4 * blocks, 32, 256), bf16),
            pltpu.VMEM((4 * blocks, 16, 128), bf16),
            pltpu.VMEM((3 * blocks // 8, 128, 128), f32),
            pltpu.VMEM((32 * blocks, 128), f32),
            pltpu.VMEM((32 * blocks, 128), f32),
            pltpu.VMEM((3, 256, 128), bf16),
            pltpu.VMEM((32 * blocks + 8, 128), f32),
            pltpu.VMEM((16 * early_turn * blocks // 8, 128), f32),
            pltpu.SemaphoreType.DMA((5,)),
        ]
        + [pltpu.VMEM((128, 256), f32)] * ring
        + [pltpu.VMEM((256, 256), bf16)] * ring,
        compiler_params=pltpu.CompilerParams(vmem_limit_bytes=vmem_grant),
        name="contact",
    )(lists.reshape(4096), cols.reshape(32 * blocks, 128), wide, ahead_of)

    mix, fluid = pl.pallas_call(
        finish_kernel,
        out_shape=(
            jax.ShapeDtypeStruct((14 * blocks, 128), f32),
            jax.ShapeDtypeStruct((2, 256), f32),
        ),
        in_specs=[anywhere()] * 5,
        out_specs=(vmem(), vmem()),
        scratch_shapes=[
            pltpu.VMEM((8 * blocks, 128), f32),
            pltpu.VMEM((blocks, 128), i32),
            pltpu.VMEM((blocks, 128), i32),
            pltpu.VMEM((1, 256), f32),
            pltpu.SemaphoreType.DMA((4,)),
            pltpu.VMEM((16, 96), f32),
            pltpu.SemaphoreType.DMA((3,)),
            pltpu.SemaphoreType.DMA((3,)),
        ],
        compiler_params=pltpu.CompilerParams(
            collective_id=1, has_side_effects=True, vmem_limit_bytes=vmem_grant
        ),
        name="finish",
    )(moved, sides, wall_flags[0, 0], cell_index[0, 0], fluid_temp.reshape(1, 256))

    rates, fluid = pl.pallas_call(
        rates_kernel,
        out_shape=(
            jax.ShapeDtypeStruct((4 * blocks, 128), f32),
            jax.ShapeDtypeStruct((2, 256), f32),
        ),
        in_specs=[anywhere()] * 3,
        out_specs=(vmem(), vmem()),
        scratch_shapes=[
            pltpu.VMEM((4 * blocks, 128), f32),
            pltpu.VMEM((14 * blocks, 128), f32),
            pltpu.VMEM((2, 256), f32),
            pltpu.SemaphoreType.DMA((3,)),
        ],
        compiler_params=pltpu.CompilerParams(vmem_limit_bytes=vmem_grant),
        name="rates",
    )(own, mix, fluid)
    return (
        moved.reshape(1, 1, blocks, 8, 128),
        rates.reshape(1, 1, blocks, 4, 128),
        fluid[None, None],
    )


def solution(mesh):
    in_specs = (
        P("gx", "gy", None, None, None),
        P("gx", "gy", None),
        P("gx", "gy", None, None),
        P("gx", "gy", None),
        P("gx", "gy", None, None),
        P("gx", "gy", None, None),
        P("gx", "gy", None),
    )
    out_specs = (
        P("gx", "gy", None, None, None),
        P("gx", "gy", None, None, None),
        P("gx", "gy", None, None),
    )
    return jax.shard_map(shards, mesh=mesh, in_specs=in_specs, out_specs=out_specs, check_vma=False)
```

```python
import functools
import math

import jax
import jax.numpy as jnp
from jax import lax
from jax.experimental import pallas as pl
from jax.experimental.pallas import tpu as pltpu
from jax.sharding import PartitionSpec as P

soften = 0.01
stiffness = 0.2
damping = 0.05
conductance = 0.05
film_gain = 0.5
wall_gain = 2.0
wall_temp = 1.0
gravity = 1.0
cell_volume = 32.0

f32 = jnp.float32
bf16 = jnp.bfloat16
i32 = jnp.int32

tiny = 1e-30
group = 16
lag_a = 2
lag_b = 2
ring = lag_a + lag_b
reach = 4
lateness = (50.0, 28.0, 22.0, 125.0, 20.0, 0.0, 0.0, 0.0, 0.0, 0.0, 0.0, 0.0, 30.0, 0.0, 0.0, 25.0)
early = 80
early_turn = 7
raw_first = 8
vmem_grant = 56 * 2**20
MESH = pl.DeviceIdType.MESH


def iota(shape, dim):
    return lax.broadcasted_iota(i32, shape, dim)


def split2(value):
    hi = value.astype(bf16).astype(f32)
    return hi, (value - hi).astype(bf16).astype(f32)


def split3(value):
    hi = value.astype(bf16).astype(f32)
    rest = value - hi
    mid = rest.astype(bf16).astype(f32)
    return hi, mid, rest - mid


def dot_tt(left, right):
    return lax.dot_general(left, right, (((1,), (1,)), ((), ())), preferred_element_type=f32)


def neighbours():
    a = lax.axis_index("gx")
    b = lax.axis_index("gy")
    na = lax.axis_size("gx")
    nb = lax.axis_size("gy")
    return (
        {"gx": lax.rem(a + 1, na)},
        {"gx": lax.rem(a + na - 1, na)},
        {"gy": lax.rem(b + 1, nb)},
        {"gy": lax.rem(b + nb - 1, nb)},
    )


def greet(everyone):
    barrier = pltpu.get_barrier_semaphore()
    for device in everyone:
        pl.semaphore_signal(barrier, inc=1, device_id=device, device_id_type=MESH)


def await_all(everyone):
    pl.semaphore_wait(pltpu.get_barrier_semaphore(), len(everyone))


def sort_pairs(lanes, pad, total):
    own = pad[0:1, :]
    code = pad[1:2, :]
    region = jnp.zeros_like(code)
    for step in range(1, 9):
        region = region + (code >= 96 * step).astype(i32)
    far = code - 96 * region
    live = iota((1, lanes), 1) < total

    def among(*names):
        hit = region == names[0]
        for name in names[1:]:
            hit = hit | (region == name)
        return hit

    kind = jnp.where(
        among(4),
        0,
        jnp.where(among(1, 5), 1, jnp.where(among(0, 3), 2, jnp.where(among(2), 3, 4))),
    )
    kind = jnp.where(live, kind, 5)
    u_far = among(0, 1, 2, 3)
    u = jnp.where(u_far, far, own) + jnp.where(among(4, 5, 3), 0, 96)
    v_slot = jnp.where(u_far, own, far)
    v_side = jnp.where(among(4, 1, 7), 0, jnp.where(among(5, 3, 0, 8), 1, 2))
    ranks = iota((8, lanes), 0)
    marks = (ranks == kind).astype(f32)
    before = (iota((lanes, lanes), 0) < iota((lanes, lanes), 1)).astype(bf16)
    seen = jnp.dot(marks.astype(bf16), before, preferred_element_type=f32)
    starts = jnp.sum((kind < ranks).astype(f32), axis=1, keepdims=True)
    place = jnp.sum(marks * (seen + starts), axis=0, keepdims=True)
    target = (iota((lanes, lanes), 0).astype(f32) == place).astype(bf16)
    rows = iota((8, lanes), 0)
    values = jnp.where(
        rows == 0, u, jnp.where(rows == 1, v_slot, jnp.where(rows == 2, v_side, 0))
    )
    moved = dot_tt(values.astype(bf16), target)
    packed = moved[0:1] + 512.0 * (moved[1:2] + 96.0 * moved[2:3])
    diag = iota((8, 128), 0) == iota((8, 128), 1)
    begin = jnp.sum(jnp.where(diag, starts, 0.0), axis=0, keepdims=True)
    return packed.astype(i32), begin.astype(i32)


def own_pairs(list_smem, refs, rings, early_ref):
    cols_ref, U, V, L, RT = refs[0:5]
    AB = rings[0:ring]
    M = rings[ring : 2 * ring]
    last = U.shape[0] - 1

    def entry(k):
        k = jnp.minimum(k, early - 1)
        code = list_smem[lax.shift_right_logical(k, 7), k & 127]
        u = jnp.minimum(code & 511, last)
        return u, jnp.minimum(lax.shift_right_logical(code, 9), last)

    def same(block):
        return block

    distances, weights, both = pair_machine(entry, same, same, cols_ref, U, V, L, RT, AB, M)
    for q in range(ring):
        distances(q, q)
    for q in range(lag_b):
        weights(q, q)

    def turn(t, carry):
        for q in range(group):
            k = t * group + q
            _, _, to_first, to_second = both(k, q % ring)
            early_ref[tile(2 * k), :] = to_first
            early_ref[tile(2 * k + 1), :] = to_second
            weights(k + lag_b, (q + lag_b) % ring)
            distances(k + ring, q % ring)
        return carry

    lax.fori_loop(0, early // group, turn, 0)


def halo_kernel(
    leaving_hbm,
    counts_hbm,
    pairs_hbm,
    state_hbm,
    cols_ref,
    lists_ref,
    wide_ref,
    early_ref,
    leaving_ref,
    counts_ref,
    pairs_ref,
    cat,
    dep,
    moved,
    pad,
    slot_vec,
    slot_smem,
    dep_send,
    dep_recv,
    list_send,
    list_recv,
    col_send,
    col_recv,
    local_sem,
    in_sem,
    near,
    near_send,
    near_recv,
    wide_send,
    wide_recv,
    list_vec,
    list_smem,
    U,
    V,
    L,
    RT,
    extra,
    pieces,
    natural,
    *rings,
):
    blocks = state_hbm.shape[0] // 8
    count = leaving_hbm.shape[0]
    ahead, behind, up, down = neighbours()
    a = lax.axis_index("gx")
    na = lax.axis_size("gx")
    along = {
        step: {"gx": lax.rem(a + step + na, na)} for step in range(-reach, reach + 1) if step
    }
    b = lax.axis_index("gy")
    nb = lax.axis_size("gy")
    across = {"gy": lax.rem(b + 2, nb)}
    everyone = (up, down, across, *along.values())
    state_ref = cat.at[8 * count : 8 * count + 8 * blocks]
    inputs = [
        pltpu.make_async_copy(source, target, in_sem.at[at])
        for at, (source, target) in enumerate(
            (
                (leaving_hbm, leaving_ref),
                (state_hbm, state_ref),
                (pairs_hbm, pairs_ref),
                (counts_hbm, counts_ref),
                (state_hbm, moved),
            )
        )
    ]
    for copy in inputs:
        copy.start()
    wide_ref[...] = jnp.zeros_like(wide_ref)
    greet(everyone)
    for copy in inputs:
        copy.wait()
    local = jnp.maximum(counts_ref[0] - early, 0).astype(f32)
    far = (counts_ref[1] - counts_ref[0]).astype(f32) * 0.125
    lane = iota((1, 128), 1)
    near[0:1, :] = jnp.where(lane < 64, far, local)
    for m in range(count):
        dep[8 * m : 8 * m + 8, :] = moved[pl.ds(leaving_ref[m] * 8, 8), :]
    await_all(everyone)
    asks = []
    for at, device in ((1, down), (2, up), (3, across)):
        copy = pltpu.make_async_remote_copy(
            src_ref=near.at[0:1],
            dst_ref=near.at[at : at + 1],
            send_sem=near_send.at[at - 1],
            recv_sem=near_recv.at[at - 1],
            device_id=device,
            device_id_type=MESH,
        )
        copy.start()
        asks.append(copy)
    depart = pltpu.make_async_remote_copy(
        src_ref=dep,
        dst_ref=cat.at[0 : 8 * count],
        send_sem=dep_send,
        recv_sem=dep_recv,
        device_id=ahead,
        device_id_type=MESH,
    )
    depart.start()
    place = iota((8, 128), 1)
    slot = place + count
    for m in range(count):
        slot = jnp.where(place == leaving_ref[m], m, slot)
    slot_vec[...] = slot
    to_smem = pltpu.make_async_copy(slot_vec, slot_smem, local_sem)
    to_smem.start()
    lanes = pad.shape[1]
    pad[...] = jnp.zeros_like(pad)
    pad[0:2, 0 : pairs_ref.shape[1]] = pairs_ref[...]
    packed, begin = sort_pairs(lanes, pad, counts_ref[1])
    lists_ref[0] = jnp.zeros((8, 128), i32)
    for row in range(lanes // 128):
        lists_ref[0, row : row + 1, :] = packed[:, 128 * row : 128 * row + 128]
    lists_ref[0, 6:7, :] = begin
    copies = []
    for copy in asks:
        copy.wait()
    turn = lane & 3
    row = near[0:1, :]
    for at, step in ((1, 1), (2, nb - 1), (3, 2)):
        row = jnp.where(turn == lax.rem(b + step, nb), near[at : at + 1, :], row)
    wide_ref[reach : reach + 1, :] = row
    for at, step in enumerate(along):
        copy = pltpu.make_async_remote_copy(
            src_ref=wide_ref.at[reach : reach + 1],
            dst_ref=wide_ref.at[reach - step : reach - step + 1],
            send_sem=wide_send.at[at],
            recv_sem=wide_recv.at[at],
            device_id=along[step],
            device_id_type=MESH,
        )
        copy.start()
        copies.append(copy)
    for at, device in ((1, down), (2, up), (3, ahead)):
        copy = pltpu.make_async_remote_copy(
            src_ref=lists_ref.at[0],
            dst_ref=lists_ref.at[at],
            send_sem=list_send.at[at - 1],
            recv_sem=list_recv.at[at - 1],
            device_id=device,
            device_id_type=MESH,
        )
        copy.start()
        copies.append(copy)
    to_smem.wait()
    codes = lists_ref[0]
    u = jnp.take_along_axis(slot, jnp.minimum(codes & 511, 95), axis=1)
    v = jnp.take_along_axis(
        slot, jnp.minimum(lax.shift_right_logical(codes, 9), 95), axis=1
    )
    list_vec[...] = u + 512 * v
    own_list = pltpu.make_async_copy(list_vec, list_smem, local_sem)
    own_list.start()
    own_list.wait()
    refs = (cat, U, V, L, RT, extra, pieces, natural)
    raw = count // 8
    build_groups(refs, raw, raw + raw_first, 2)
    depart.wait()

    def place_block(j, carry):
        moved[tile(j), :] = cat[pl.ds(slot_smem[0, j] * 8, 8), :]
        return carry

    lax.fori_loop(0, blocks, place_block, 0)
    keep = pltpu.make_async_copy(moved, cols_ref.at[0], local_sem)
    keep.start()
    for at, device in ((1, ahead), (2, down), (3, up)):
        copy = pltpu.make_async_remote_copy(
            src_ref=moved,
            dst_ref=cols_ref.at[at],
            send_sem=col_send.at[at - 1],
            recv_sem=col_recv.at[at - 1],
            device_id=device,
            device_id_type=MESH,
        )
        copy.start()
        copies.append(copy)
    keep.wait()
    build_groups(refs, raw + raw_first, raw + blocks // 8, 2)
    build_groups(refs, 0, raw, 3)
    own_pairs(list_smem, refs, rings, early_ref)
    for copy in copies:
        copy.wait()


def rows_of(base, c):
    return pl.ds(base * 8 + c, 8, 8)


def tile(i):
    return pl.ds(pl.multiple_of(i * 8, 8), 8)


def table_steps(cols_ref, U, V, L, RT, extra, pieces, natural, never):
    rows = iota((8, 128), 0)
    eye = (iota((128, 128), 0) == iota((128, 128), 1)).astype(bf16)
    eyes = jnp.concatenate([eye, eye, eye], axis=1)
    c6 = jnp.where(rows == 6, 1.0, 0.0)
    c7 = jnp.where(rows == 7, 0.25, 0.0)
    ca = jnp.where(rows < 3, -2.0, 0.0)
    cb = jnp.where(rows < 6, -0.25, 0.0)
    ones = jnp.where(rows < 6, 1.0, 0.0)

    def dense(base):
        x = [cols_ref[rows_of(base, c), :] for c in range(3)]
        v = [cols_ref[rows_of(base, c), :] for c in range(3, 6)]
        radius = cols_ref[rows_of(base, 7), :]
        root = jnp.sqrt(radius)
        square = x[0] * x[0] + x[1] * x[1] + x[2] * x[2] + 0.5 * soften
        dot = x[0] * v[0] + x[1] * v[1] + x[2] * v[2]
        extra[rows_of(base, 3), :] = jnp.ones((8, 128), f32)
        extra[rows_of(base, 4), :] = root * cols_ref[rows_of(base, 6), :]
        extra[rows_of(base, 5), :] = root
        extra[rows_of(base, 6), :] = square
        extra[rows_of(base, 7), :] = dot
        for c, piece in enumerate(split3(square) + split3(0.25 * dot)):
            pieces[rows_of(base, c), :] = piece

    def swap(value):
        return jnp.where(rows < 3, pltpu.roll(value, 5, 0), pltpu.roll(value, 3, 0))

    def eight(base, shift, at, held=None):
        for q in range(8):
            i = base + q
            S = cols_ref[tile(i), :]
            if held is not None:
                S = jnp.where(never, held, S)
            E = extra[tile(i), :]
            G = pieces[tile(i), :]
            hi, mid = split2(jnp.where(rows < 3, S, jnp.where(rows < 6, E, 0.0)))
            L[i] = jnp.concatenate([hi, mid], axis=0).astype(bf16)
            full = jnp.where(rows < 6, S, E)
            hi, mid = split2(full)
            if at is not None:
                low = jnp.where(rows < 6, hi, full - hi - mid)
                natural[at, 32 * q : 32 * q + 32, :] = jnp.concatenate(
                    [hi, low, mid, ones], axis=0
                ).astype(bf16)
            a0 = hi * ca + c6
            a1 = mid * ca + c6
            b0 = swap(hi) * cb + c7
            b1 = swap(mid) * cb + c7
            A = jnp.concatenate([a0, a1, a0, jnp.where(rows < 3, G, 0.0)], axis=0)
            B = jnp.concatenate(
                [b0, b1, b0, jnp.where((rows >= 3) & (rows < 6), G, 0.0)], axis=0
            )
            V[i + shift, :, 0:128] = A.astype(bf16)
            V[i + shift, :, 128:256] = B.astype(bf16)

    def turn(at, u_base):
        turned = dot_tt(eye, natural[at]).astype(bf16)
        for q in range(8):
            U[u_base + q, :, 0:32] = turned[:, 32 * q : 32 * q + 32]

    def column(base, u_base):
        radius = cols_ref[rows_of(base, 7), :]
        three = jnp.concatenate(split3(radius), axis=1).astype(bf16)
        RT[lax.shift_right_logical(u_base, 3), :, 0:8] = dot_tt(eyes, three)

    return dense, eight, turn, column


def build_tables(refs, first, start, step):
    dense, eight, turn, column = table_steps(*refs, first < 0)
    cols_ref, U = refs[0:2]

    def turns(t):
        turn(0, 8 * t)
        turn(1, 96 + 8 * t)
        turn(2, 192 + 8 * t)
        column(8 * t, 8 * t)
        column(96 + 8 * t, 96 + 8 * t)
        column(288 + 8 * t, 192 + 8 * t)

    def body(t, carry):
        turns(jnp.maximum(t - 1, 0))
        for col in range(4):
            dense(96 * col + 8 * t)
        eight(8 * t, 0, 0)
        eight(96 + 8 * t, 192, 1)
        eight(288 + 8 * t, -96, 2)
        held = U[first & 63, 0:16, :].astype(f32)[0:8]
        eight(192 + 8 * t, -96, None, held)
        return step(t, carry)

    count = cols_ref.shape[0] // 256
    carry = lax.fori_loop(0, count, body, start)
    turns(count - 1)
    return carry


def build_groups(refs, low, high, step):
    dense, eight, turn, column = table_steps(*refs, None)

    def body(t, carry):
        bases = [8 * (t * step + low + q) for q in range(step)]
        for base in bases:
            dense(base)
        for at, base in enumerate(bases):
            eight(base, 0, at)
        for at, base in enumerate(bases):
            turn(at, base)
        for base in bases:
            column(base, base)
        return carry

    lax.fori_loop(0, (high - low) // step, body, 0)


def shares(wide):
    rows = iota((8, 128), 0)
    lanes = iota((8, 128), 1)
    b = lax.axis_index("gy")
    nb = lax.axis_size("gy")
    own = wide[1:9, :]
    behind = wide[0:8, :]
    far = jnp.where(lanes < 64, own, pltpu.roll(behind, 64, 1))
    local = jnp.where(lanes < 64, pltpu.roll(own, 64, 1), behind)
    load = (
        local
        + 2.0 * far
        + 2.0 * pltpu.roll(far, 127, 1)
        + pltpu.roll(far, 1, 1)
        + 3.0 * jnp.where(rows == 0, far, pltpu.roll(far, 1, 0))
    )
    column = lax.axis_index("gx") + rows - (reach - 1) - jnp.where(lanes < 64, 0, 1)
    phase = (column + 32) & 15
    for at, late in enumerate(lateness):
        load = load + jnp.where(phase == at, late, 0.0)
    passing = jnp.where(rows < 7, local, 0.0)

    def step(given):
        ahead, up = given
        now = load - ahead - up + pltpu.roll(ahead, 1, 0) + pltpu.roll(up, 1, 1)
        ahead = ahead + 0.26 * (now - pltpu.roll(now, 7, 0))
        ahead = jnp.minimum(jnp.maximum(ahead, 0.0), jnp.maximum(passing - up, 0.0))
        up = up + 0.26 * (now - pltpu.roll(now, 127, 1))
        up = jnp.minimum(jnp.maximum(up, 0.0), jnp.maximum(local - ahead, 0.0))
        return ahead, up

    def value(given, shift, base):
        column = lax.rem(b + shift + nb, nb)
        picked = (rows == reach - 1) & (lanes == column + base)
        return jnp.sum(jnp.where(picked, given, 0.0)).astype(i32)

    start = jnp.zeros((8, 128), f32)
    return (start, start), step, value


def pair_machine(entry, spot, spot_u, cols_ref, U, V, L, RT, AB, M):
    def distances(k, at):
        u, v = entry(k)
        AB[at][...] = jnp.dot(U[u, :, 0:32], V[v], preferred_element_type=f32)

    def weights(k, at):
        u, v = entry(k)
        rt = cols_ref[pl.ds(spot(v) * 8 + 7, 1), :]
        lane = jnp.full((8, 128), u & 7, i32)
        eighth = lax.shift_right_logical(u, 3)

        def radius(r):
            return jnp.take_along_axis(RT[eighth, r : r + 8, :], lane, axis=1)

        for r in range(0, 128, 16):
            A = AB[at][r : r + 16, 0:128]
            B = AB[at][r : r + 16, 128:256]
            R = jnp.concatenate([radius(r), radius(r + 8)], axis=0) + rt
            inv = lax.rsqrt(A)
            gap = R - A * inv
            inter = jnp.maximum(gap, 0.0)
            root = inter * lax.rsqrt(jnp.maximum(gap, tiny))
            W = (root * inv) * (inter - B * inv)
            G = root * lax.rsqrt(R)
            wh = W.astype(bf16)
            gh = G.astype(bf16)
            M[at][r : r + 16, 0:128] = wh
            M[at][r : r + 16, 128:256] = gh
            M[at][128 + r : 144 + r, 0:128] = (W - wh.astype(f32)).astype(bf16)
            M[at][128 + r : 144 + r, 128:256] = (G - gh.astype(f32)).astype(bf16)

    rows = iota((8, 128), 0)

    def folded(out):
        both = out[0:8] + out[8:16]
        return jnp.where(rows < 4, both[:, 0:128], both[:, 128:256])

    def both(k, at):
        u, v = entry(k)
        w = spot(v)
        o = spot_u(u)
        first = jnp.concatenate([L[o], L[o]], axis=1)
        second = jnp.concatenate([L[w], L[w]], axis=1)
        m = M[at]
        crossed = jnp.concatenate(
            [
                jnp.concatenate([m[0:128, 0:128], m[128:256, 0:128]], axis=1),
                jnp.concatenate([m[0:128, 128:256], m[128:256, 128:256]], axis=1),
            ],
            axis=0,
        )
        to_second = folded(jnp.dot(first, m[...], preferred_element_type=f32))
        to_first = folded(dot_tt(second, crossed))
        return o, w, to_first, to_second

    return distances, weights, both


def pair_kernel(
    lists_hbm,
    cols_hbm,
    wide_hbm,
    early_hbm,
    moved_ref,
    own_ref,
    sides_ref,
    lists_ref,
    cols_ref,
    wide,
    U,
    V,
    L,
    RT,
    extra,
    pieces,
    natural,
    acc,
    before,
    sem,
    *rings,
):
    AB = rings[0:ring]
    M = rings[ring : 2 * ring]
    copies = [
        pltpu.make_async_copy(source, target, sem.at[at])
        for at, (source, target) in enumerate(
            (
                (cols_hbm, cols_ref),
                (lists_hbm, lists_ref),
                (wide_hbm, wide),
                (early_hbm, before.at[0 : 16 * early]),
            )
        )
    ]
    for copy in copies:
        copy.start()
    trash = acc.shape[0] // 8 - 1
    acc[...] = jnp.zeros_like(acc)
    for copy in copies:
        copy.wait()
    keep = pltpu.make_async_copy(cols_ref.at[0:768], moved_ref, sem.at[4])
    keep.start()
    given, step, value = shares(wide)
    first = lists_ref[0]
    done = jnp.minimum(lists_ref[6 * 128 + 1], early)

    def turn_in(t, carry):
        for q in range(early_turn):
            k = t * early_turn + q
            live = k < done
            code = lists_ref[k]
            o = jnp.where(live, code & 511, trash)
            w = jnp.where(live, lax.shift_right_logical(code, 9), trash)
            acc[tile(o), :] += before[tile(2 * k), :]
            acc[tile(w), :] += before[tile(2 * k + 1), :]
        return step(carry)

    refs = (cols_ref, U, V, L, RT, extra, pieces, natural)
    given = build_tables(refs, first, given, turn_in)
    ahead_out = value(given[0], 0, 32)
    up_out = value(given[1], 0, 32)
    ahead_in = value(given[0], 0, 96)
    ahead_down = value(given[0], -1, 32)
    up_in = value(given[1], -1, 32)

    def begin(at, name):
        return lists_ref[at * 1024 + 6 * 128 + name]

    def cut(at, first, second):
        end = begin(at, 1)
        low = jnp.minimum(end, early)
        first = jnp.minimum(low + first, end)
        return low, first, jnp.minimum(first + second, end)

    _, _, kept = cut(0, ahead_out, up_out)
    ahead_low, ahead_high, _ = cut(3, ahead_in, 0)
    _, up_low, up_high = cut(2, ahead_down, up_in)
    ends = []
    shifts = []
    so_far = 0
    for at, low, high in (
        (0, kept, begin(0, 1)),
        (0, begin(0, 1), begin(0, 2)),
        (1, begin(1, 2), begin(1, 3)),
        (2, begin(2, 3), begin(2, 4)),
        (3, begin(3, 4), begin(3, 5)),
        (3, ahead_low, ahead_high),
        (2, up_low, up_high),
    ):
        shifts.append(at * 1024 + low - so_far)
        so_far = so_far + (high - low)
        ends.append(so_far)
    n = so_far
    last = jnp.maximum(n - 1, 0)

    def entry(k):
        k = jnp.minimum(k, last)
        shift = shifts[6]
        for at in range(5, -1, -1):
            shift = jnp.where(k < ends[at], shifts[at], shift)
        code = lists_ref[k + shift]
        code = code + jnp.where(
            k < ends[4], 0, jnp.where(k < ends[5], 96 + 512 * 288, 192 + 512 * 192)
        )
        return code & 511, lax.shift_right_logical(code, 9)

    def spot_u(u):
        return jnp.where(u < 192, u, u + 96)

    def spot(v):
        return jnp.where(v < 96, v, jnp.where(v < 288, v + 96, v - 192))

    distances, weights, both = pair_machine(entry, spot, spot_u, cols_ref, U, V, L, RT, AB, M)

    def sums(k, at):
        o, w, to_first, to_second = both(k, at)
        live = k < n
        o = jnp.where(live, o, trash)
        w = jnp.where(live, w, trash)
        acc[tile(o), :] += to_first
        acc[tile(w), :] += to_second

    for q in range(ring):
        distances(q, q)
    for q in range(lag_b):
        weights(q, q)

    def turn(t, carry):
        for q in range(group):
            k = t * group + q
            sums(k, q % ring)
            weights(k + lag_b, (q + lag_b) % ring)
            distances(k + ring, q % ring)
        return carry

    lax.fori_loop(0, lax.div(n + group - 1, group), turn, 0)

    def close(base, out_ref, out_base):
        got = [acc[rows_of(base, c), :] for c in range(6)]
        terms = []
        for c in range(3):
            hi, mid = split2(cols_ref[rows_of(base, c), :])
            terms.append(stiffness * ((hi + mid) * got[3] - got[c]))
        root = conductance * extra[rows_of(base, 5), :]
        terms.append(root * (got[4] - cols_ref[rows_of(base, 6), :] * got[5]))
        for c in range(4):
            out_ref[pl.ds(out_base + c, 8, 4), :] = terms[c]

    def close_all(t, carry):
        close(8 * t, own_ref, 32 * t)
        for side in range(3):
            close(96 * (side + 1) + 8 * t, sides_ref, 384 * side + 32 * t)
        return carry

    lax.fori_loop(0, 12, close_all, 0)
    keep.wait()


def finish_kernel(
    moved_hbm,
    sides_ref,
    flags_hbm,
    cells_hbm,
    table_hbm,
    mix_ref,
    fluid_ref,
    moved_ref,
    flags_ref,
    cells_ref,
    table_ref,
    in_sem,
    sums,
    send,
    recv,
):
    ahead, behind, up, down = neighbours()
    inputs = [
        pltpu.make_async_copy(source, target, in_sem.at[at])
        for at, (source, target) in enumerate(
            (
                (moved_hbm, moved_ref),
                (flags_hbm, flags_ref),
                (cells_hbm, cells_ref),
                (table_hbm, table_ref),
            )
        )
    ]
    for copy in inputs:
        copy.start()
    greet((ahead, behind, up, down))
    await_all((ahead, behind, up, down))
    copies = []
    span = sides_ref.shape[0] // 3
    blocks = span // 4
    for at, device in ((0, behind), (1, up), (2, down)):
        copy = pltpu.make_async_remote_copy(
            src_ref=sides_ref.at[span * at : span * at + span],
            dst_ref=mix_ref.at[span * at : span * at + span],
            send_sem=send.at[at],
            recv_sem=recv.at[at],
            device_id=device,
            device_id_type=MESH,
        )
        copy.start()
        copies.append(copy)

    for copy in inputs:
        copy.wait()
    square = jnp.concatenate([table_ref[:, 16 * a : 16 * a + 16] for a in range(16)], axis=0)
    table = jnp.concatenate(split3(square), axis=0).astype(bf16)
    sums[...] = jnp.zeros_like(sums)
    sub = iota((16, 128), 0)

    def cells_of(g, carry):
        at = pl.ds(pl.multiple_of(g * 8, 8), 8)
        temper = moved_ref[rows_of(g * 8, 6), :]
        radius = moved_ref[rows_of(g * 8, 7), :]
        volume = 4.0 / 3.0 * math.pi * radius * radius * radius
        cell = cells_ref[at, :]
        high = lax.shift_right_logical(cell, 4)
        low = cell & 15
        fluid = []
        hots = []
        for c in range(8):
            hot_high = (sub == high[c : c + 1]).astype(f32)
            hot_low = (sub == low[c : c + 1]).astype(f32)
            parts = jnp.dot(table, hot_low.astype(bf16), preferred_element_type=f32)
            value = parts[0:16] + parts[16:32] + parts[32:48]
            fluid.append(jnp.sum(value * hot_high, axis=0, keepdims=True))
            hots.append((hot_high, hot_low))
        flow = film_gain * radius * radius * (temper - jnp.concatenate(fluid, axis=0))
        pieces = split3(volume) + split3(flow)
        total = sums[...]
        for c in range(8):
            hot_high, hot_low = hots[c]
            spread = jnp.concatenate([hot_low * piece[c : c + 1] for piece in pieces], axis=0)
            total = total + dot_tt(hot_high.astype(bf16), spread.astype(bf16))
        sums[...] = total
        wall = wall_gain * flags_ref[at, :].astype(f32) * (wall_temp - temper) * radius
        mix_ref[pl.ds(pl.multiple_of(3 * span + g * 8, 8), 8), :] = wall - flow
        mix_ref[pl.ds(pl.multiple_of(3 * span + blocks + g * 8, 8), 8), :] = 1.0 / volume
        return carry

    lax.fori_loop(0, 12, cells_of, 0)
    total = sums[...]
    solid = (total[:, 0:16] + total[:, 16:32] + total[:, 32:48]) / cell_volume
    heat = total[:, 48:64] + total[:, 64:80] + total[:, 80:96]
    for a in range(16):
        fluid_ref[0:1, 16 * a : 16 * a + 16] = solid[a : a + 1]
        fluid_ref[1:2, 16 * a : 16 * a + 16] = heat[a : a + 1]
    for copy in copies:
        copy.wait()


def rates_kernel(
    own_hbm, mix_hbm, fluid_hbm, rates_ref, fluid_ref, own, mix, fluid, sem
):
    copies = [
        pltpu.make_async_copy(source, target, sem.at[at])
        for at, (source, target) in enumerate(
            ((mix_hbm, mix), (own_hbm, own), (fluid_hbm, fluid))
        )
    ]
    for copy in copies:
        copy.start()
    for copy in copies:
        copy.wait()
    fluid_ref[...] = fluid[...]
    span = own.shape[0]
    blocks = span // 4

    def combine(g, carry):
        at = pl.multiple_of(g * 8, 8)
        inverse = mix[pl.ds(3 * span + blocks + at, 8), :]
        for c in range(4):
            here = pl.ds(g * 32 + c, 8, 4)
            value = own[here, :]
            for side in range(3):
                value = value + mix[pl.ds(span * side + g * 32 + c, 8, 4), :]
            if c == 3:
                value = value + mix[pl.ds(3 * span + at, 8), :]
            value = value * inverse
            if c == 2:
                value = value - gravity
            rates_ref[here, :] = value
        return carry

    lax.fori_loop(0, blocks // 8, combine, 0, unroll=4)


def anywhere():
    return pl.BlockSpec(memory_space=pl.ANY)


def vmem():
    return pl.BlockSpec(memory_space=pltpu.VMEM)


def shards(state, leaving, pairs, counts, wall_flags, cell_index, fluid_temp):
    mine = state[0, 0]
    blocks = mine.shape[0]
    count = leaving.shape[2]
    lanes = -(-pairs.shape[3] // 128) * 128
    cols, lists, wide, ahead_of = pl.pallas_call(
        halo_kernel,
        out_shape=(
            jax.ShapeDtypeStruct((4, 8 * blocks, 128), f32),
            jax.ShapeDtypeStruct((4, 8, 128), i32),
            jax.ShapeDtypeStruct((16, 128), f32),
            jax.ShapeDtypeStruct((16 * early, 128), f32),
        ),
        in_specs=[anywhere()] * 4,
        out_specs=(anywhere(), vmem(), vmem(), vmem()),
        scratch_shapes=[
            pltpu.SMEM(leaving.shape[2:], i32),
            pltpu.SMEM(counts.shape[2:], i32),
            pltpu.VMEM(pairs.shape[2:], i32),
            pltpu.VMEM((8 * (count + blocks), 128), f32),
            pltpu.VMEM((8 * count, 128), f32),
            pltpu.VMEM((8 * blocks, 128), f32),
            pltpu.VMEM((8, lanes), i32),
            pltpu.VMEM((8, 128), i32),
            pltpu.SMEM((8, 128), i32),
            pltpu.SemaphoreType.DMA,
            pltpu.SemaphoreType.DMA,
            pltpu.SemaphoreType.DMA((3,)),
            pltpu.SemaphoreType.DMA((3,)),
            pltpu.SemaphoreType.DMA((3,)),
            pltpu.SemaphoreType.DMA((3,)),
            pltpu.SemaphoreType.DMA,
            pltpu.SemaphoreType.DMA((5,)),
            pltpu.VMEM((8, 128), f32),
            pltpu.SemaphoreType.DMA((3,)),
            pltpu.SemaphoreType.DMA((3,)),
            pltpu.SemaphoreType.DMA((2 * reach,)),
            pltpu.SemaphoreType.DMA((2 * reach,)),
            pltpu.VMEM((8, 128), i32),
            pltpu.SMEM((8, 128), i32),
            pltpu.VMEM((count + blocks, 128, 128), bf16),
            pltpu.VMEM((count + blocks, 32, 256), bf16),
            pltpu.VMEM((count + blocks, 16, 128), bf16),
            pltpu.VMEM(((count + blocks) // 8, 128, 128), f32),
            pltpu.VMEM((8 * (count + blocks), 128), f32),
            pltpu.VMEM((8 * (count + blocks), 128), f32),
            pltpu.VMEM((3, 256, 128), bf16),
        ]
        + [pltpu.VMEM((128, 256), f32)] * ring
        + [pltpu.VMEM((256, 256), bf16)] * ring,
        compiler_params=pltpu.CompilerParams(
            collective_id=0, has_side_effects=True, vmem_limit_bytes=vmem_grant
        ),
        name="halo",
    )(leaving[0, 0], counts[0, 0], pairs[0, 0], mine.reshape(8 * blocks, 128))

    moved, own, sides = pl.pallas_call(
        pair_kernel,
        out_shape=(
            jax.ShapeDtypeStruct((8 * blocks, 128), f32),
            jax.ShapeDtypeStruct((4 * blocks, 128), f32),
            jax.ShapeDtypeStruct((12 * blocks, 128), f32),
        ),
        in_specs=[anywhere()] * 4,
        out_specs=(anywhere(), vmem(), vmem()),
        scratch_shapes=[
            pltpu.SMEM((4096,), i32),
            pltpu.VMEM((32 * blocks, 128), f32),
            pltpu.VMEM((16, 128), f32),
            pltpu.VMEM((3 * blocks, 128, 128), bf16),
            pltpu.VMEM((4 * blocks, 32, 256), bf16),
            pltpu.VMEM((4 * blocks, 16, 128), bf16),
            pltpu.VMEM((3 * blocks // 8, 128, 128), f32),
            pltpu.VMEM((32 * blocks, 128), f32),
            pltpu.VMEM((32 * blocks, 128), f32),
            pltpu.VMEM((3, 256, 128), bf16),
            pltpu.VMEM((32 * blocks + 8, 128), f32),
            pltpu.VMEM((16 * early_turn * blocks // 8, 128), f32),
            pltpu.SemaphoreType.DMA((5,)),
        ]
        + [pltpu.VMEM((128, 256), f32)] * ring
        + [pltpu.VMEM((256, 256), bf16)] * ring,
        compiler_params=pltpu.CompilerParams(vmem_limit_bytes=vmem_grant),
        name="contact",
    )(lists.reshape(4096), cols.reshape(32 * blocks, 128), wide, ahead_of)

    mix, fluid = pl.pallas_call(
        finish_kernel,
        out_shape=(
            jax.ShapeDtypeStruct((14 * blocks, 128), f32),
            jax.ShapeDtypeStruct((2, 256), f32),
        ),
        in_specs=[anywhere()] * 5,
        out_specs=(vmem(), vmem()),
        scratch_shapes=[
            pltpu.VMEM((8 * blocks, 128), f32),
            pltpu.VMEM((blocks, 128), i32),
            pltpu.VMEM((blocks, 128), i32),
            pltpu.VMEM((1, 256), f32),
            pltpu.SemaphoreType.DMA((4,)),
            pltpu.VMEM((16, 96), f32),
            pltpu.SemaphoreType.DMA((3,)),
            pltpu.SemaphoreType.DMA((3,)),
        ],
        compiler_params=pltpu.CompilerParams(
            collective_id=1, has_side_effects=True, vmem_limit_bytes=vmem_grant
        ),
        name="finish",
    )(moved, sides, wall_flags[0, 0], cell_index[0, 0], fluid_temp.reshape(1, 256))

    rates, fluid = pl.pallas_call(
        rates_kernel,
        out_shape=(
            jax.ShapeDtypeStruct((4 * blocks, 128), f32),
            jax.ShapeDtypeStruct((2, 256), f32),
        ),
        in_specs=[anywhere()] * 3,
        out_specs=(vmem(), vmem()),
        scratch_shapes=[
            pltpu.VMEM((4 * blocks, 128), f32),
            pltpu.VMEM((14 * blocks, 128), f32),
            pltpu.VMEM((2, 256), f32),
            pltpu.SemaphoreType.DMA((3,)),
        ],
        compiler_params=pltpu.CompilerParams(vmem_limit_bytes=vmem_grant),
        name="rates",
    )(own, mix, fluid)
    return (
        moved.reshape(1, 1, blocks, 8, 128),
        rates.reshape(1, 1, blocks, 4, 128),
        fluid[None, None],
    )


def solution(mesh):
    in_specs = (
        P("gx", "gy", None, None, None),
        P("gx", "gy", None),
        P("gx", "gy", None, None),
        P("gx", "gy", None),
        P("gx", "gy", None, None),
        P("gx", "gy", None, None),
        P("gx", "gy", None),
    )
    out_specs = (
        P("gx", "gy", None, None, None),
        P("gx", "gy", None, None, None),
        P("gx", "gy", None, None),
    )
    return jax.shard_map(shards, mesh=mesh, in_specs=in_specs, out_specs=out_specs, check_vma=False)
```

```python
import functools
import math

import jax
import jax.numpy as jnp
from jax import lax
from jax.experimental import pallas as pl
from jax.experimental.pallas import tpu as pltpu
from jax.sharding import PartitionSpec as P

soften = 0.01
stiffness = 0.2
damping = 0.05
conductance = 0.05
film_gain = 0.5
wall_gain = 2.0
wall_temp = 1.0
gravity = 1.0
cell_volume = 32.0

f32 = jnp.float32
bf16 = jnp.bfloat16
i32 = jnp.int32

tiny = 1e-30
group = 16
lag_a = 2
lag_b = 2
ring = lag_a + lag_b
reach = 4
lateness = (50.0, 28.0, 22.0, 125.0, 20.0, 0.0, 0.0, 0.0, 0.0, 0.0, 0.0, 0.0, 70.0, 0.0, 0.0, 35.0)
early = 64
early_turn = 6
vmem_grant = 56 * 2**20
MESH = pl.DeviceIdType.MESH


def iota(shape, dim):
    return lax.broadcasted_iota(i32, shape, dim)


def split2(value):
    hi = value.astype(bf16).astype(f32)
    return hi, (value - hi).astype(bf16).astype(f32)


def split3(value):
    hi = value.astype(bf16).astype(f32)
    rest = value - hi
    mid = rest.astype(bf16).astype(f32)
    return hi, mid, rest - mid


def dot_tt(left, right):
    return lax.dot_general(left, right, (((1,), (1,)), ((), ())), preferred_element_type=f32)


def neighbours():
    a = lax.axis_index("gx")
    b = lax.axis_index("gy")
    na = lax.axis_size("gx")
    nb = lax.axis_size("gy")
    return (
        {"gx": lax.rem(a + 1, na)},
        {"gx": lax.rem(a + na - 1, na)},
        {"gy": lax.rem(b + 1, nb)},
        {"gy": lax.rem(b + nb - 1, nb)},
    )


def greet(everyone):
    barrier = pltpu.get_barrier_semaphore()
    for device in everyone:
        pl.semaphore_signal(barrier, inc=1, device_id=device, device_id_type=MESH)


def await_all(everyone):
    pl.semaphore_wait(pltpu.get_barrier_semaphore(), len(everyone))


def sort_pairs(lanes, pad, total):
    own = pad[0:1, :]
    code = pad[1:2, :]
    region = jnp.zeros_like(code)
    for step in range(1, 9):
        region = region + (code >= 96 * step).astype(i32)
    far = code - 96 * region
    live = iota((1, lanes), 1) < total

    def among(*names):
        hit = region == names[0]
        for name in names[1:]:
            hit = hit | (region == name)
        return hit

    kind = jnp.where(
        among(4),
        0,
        jnp.where(among(1, 5), 1, jnp.where(among(0, 3), 2, jnp.where(among(2), 3, 4))),
    )
    kind = jnp.where(live, kind, 5)
    u_far = among(0, 1, 2, 3)
    u = jnp.where(u_far, far, own) + jnp.where(among(4, 5, 3), 0, 96)
    v_slot = jnp.where(u_far, own, far)
    v_side = jnp.where(among(4, 1, 7), 0, jnp.where(among(5, 3, 0, 8), 1, 2))
    ranks = iota((8, lanes), 0)
    marks = (ranks == kind).astype(f32)
    before = (iota((lanes, lanes), 0) < iota((lanes, lanes), 1)).astype(bf16)
    seen = jnp.dot(marks.astype(bf16), before, preferred_element_type=f32)
    starts = jnp.sum((kind < ranks).astype(f32), axis=1, keepdims=True)
    place = jnp.sum(marks * (seen + starts), axis=0, keepdims=True)
    target = (iota((lanes, lanes), 0).astype(f32) == place).astype(bf16)
    rows = iota((8, lanes), 0)
    values = jnp.where(
        rows == 0, u, jnp.where(rows == 1, v_slot, jnp.where(rows == 2, v_side, 0))
    )
    moved = dot_tt(values.astype(bf16), target)
    packed = moved[0:1] + 512.0 * (moved[1:2] + 96.0 * moved[2:3])
    diag = iota((8, 128), 0) == iota((8, 128), 1)
    begin = jnp.sum(jnp.where(diag, starts, 0.0), axis=0, keepdims=True)
    return packed.astype(i32), begin.astype(i32)


def own_pairs(list_smem, refs, rings, early_ref):
    cols_ref, U, V, L, RT = refs[0:5]
    AB = rings[0:ring]
    M = rings[ring : 2 * ring]
    last = U.shape[0] - 1

    def entry(k):
        k = jnp.minimum(k, early - 1)
        code = list_smem[lax.shift_right_logical(k, 7), k & 127]
        u = jnp.minimum(code & 511, last)
        return u, jnp.minimum(lax.shift_right_logical(code, 9), last)

    def same(block):
        return block

    distances, weights, both = pair_machine(entry, same, same, cols_ref, U, V, L, RT, AB, M)
    for q in range(ring):
        distances(q, q)
    for q in range(lag_b):
        weights(q, q)

    def turn(t, carry):
        for q in range(group):
            k = t * group + q
            _, _, to_first, to_second = both(k, q % ring)
            early_ref[tile(2 * k), :] = to_first
            early_ref[tile(2 * k + 1), :] = to_second
            weights(k + lag_b, (q + lag_b) % ring)
            distances(k + ring, q % ring)
        return carry

    lax.fori_loop(0, early // group, turn, 0)


def halo_kernel(
    leaving_hbm,
    counts_hbm,
    pairs_hbm,
    state_hbm,
    cols_ref,
    lists_ref,
    wide_ref,
    early_ref,
    leaving_ref,
    counts_ref,
    pairs_ref,
    cat,
    dep,
    moved,
    pad,
    slot_vec,
    slot_smem,
    dep_send,
    dep_recv,
    list_send,
    list_recv,
    col_send,
    col_recv,
    local_sem,
    in_sem,
    near,
    near_send,
    near_recv,
    wide_send,
    wide_recv,
    list_vec,
    list_smem,
    U,
    V,
    L,
    RT,
    extra,
    pieces,
    natural,
    *rings,
):
    blocks = state_hbm.shape[0] // 8
    count = leaving_hbm.shape[0]
    ahead, behind, up, down = neighbours()
    a = lax.axis_index("gx")
    na = lax.axis_size("gx")
    along = {
        step: {"gx": lax.rem(a + step + na, na)} for step in range(-reach, reach + 1) if step
    }
    b = lax.axis_index("gy")
    nb = lax.axis_size("gy")
    across = {"gy": lax.rem(b + 2, nb)}
    everyone = (up, down, across, *along.values())
    state_ref = cat.at[8 * count : 8 * count + 8 * blocks]
    inputs = [
        pltpu.make_async_copy(source, target, in_sem.at[at])
        for at, (source, target) in enumerate(
            (
                (leaving_hbm, leaving_ref),
                (state_hbm, state_ref),
                (pairs_hbm, pairs_ref),
                (counts_hbm, counts_ref),
                (state_hbm, moved),
            )
        )
    ]
    for copy in inputs:
        copy.start()
    wide_ref[...] = jnp.zeros_like(wide_ref)
    greet(everyone)
    for copy in inputs:
        copy.wait()
    local = jnp.maximum(counts_ref[0] - early, 0).astype(f32)
    far = (counts_ref[1] - counts_ref[0]).astype(f32) * 0.125
    lane = iota((1, 128), 1)
    near[0:1, :] = jnp.where(lane < 64, far, local)
    for m in range(count):
        dep[8 * m : 8 * m + 8, :] = moved[pl.ds(leaving_ref[m] * 8, 8), :]
    await_all(everyone)
    asks = []
    for at, device in ((1, down), (2, up), (3, across)):
        copy = pltpu.make_async_remote_copy(
            src_ref=near.at[0:1],
            dst_ref=near.at[at : at + 1],
            send_sem=near_send.at[at - 1],
            recv_sem=near_recv.at[at - 1],
            device_id=device,
            device_id_type=MESH,
        )
        copy.start()
        asks.append(copy)
    depart = pltpu.make_async_remote_copy(
        src_ref=dep,
        dst_ref=cat.at[0 : 8 * count],
        send_sem=dep_send,
        recv_sem=dep_recv,
        device_id=ahead,
        device_id_type=MESH,
    )
    depart.start()
    place = iota((8, 128), 1)
    slot = place + count
    for m in range(count):
        slot = jnp.where(place == leaving_ref[m], m, slot)
    slot_vec[...] = slot
    to_smem = pltpu.make_async_copy(slot_vec, slot_smem, local_sem)
    to_smem.start()
    lanes = pad.shape[1]
    pad[...] = jnp.zeros_like(pad)
    pad[0:2, 0 : pairs_ref.shape[1]] = pairs_ref[...]
    packed, begin = sort_pairs(lanes, pad, counts_ref[1])
    lists_ref[0] = jnp.zeros((8, 128), i32)
    for row in range(lanes // 128):
        lists_ref[0, row : row + 1, :] = packed[:, 128 * row : 128 * row + 128]
    lists_ref[0, 6:7, :] = begin
    copies = []
    for copy in asks:
        copy.wait()
    turn = lane & 3
    row = near[0:1, :]
    for at, step in ((1, 1), (2, nb - 1), (3, 2)):
        row = jnp.where(turn == lax.rem(b + step, nb), near[at : at + 1, :], row)
    wide_ref[reach : reach + 1, :] = row
    for at, step in enumerate(along):
        copy = pltpu.make_async_remote_copy(
            src_ref=wide_ref.at[reach : reach + 1],
            dst_ref=wide_ref.at[reach - step : reach - step + 1],
            send_sem=wide_send.at[at],
            recv_sem=wide_recv.at[at],
            device_id=along[step],
            device_id_type=MESH,
        )
        copy.start()
        copies.append(copy)
    for at, device in ((1, down), (2, up), (3, ahead)):
        copy = pltpu.make_async_remote_copy(
            src_ref=lists_ref.at[0],
            dst_ref=lists_ref.at[at],
            send_sem=list_send.at[at - 1],
            recv_sem=list_recv.at[at - 1],
            device_id=device,
            device_id_type=MESH,
        )
        copy.start()
        copies.append(copy)
    to_smem.wait()
    codes = lists_ref[0]
    u = jnp.take_along_axis(slot, jnp.minimum(codes & 511, 95), axis=1)
    v = jnp.take_along_axis(
        slot, jnp.minimum(lax.shift_right_logical(codes, 9), 95), axis=1
    )
    list_vec[...] = u + 512 * v
    own_list = pltpu.make_async_copy(list_vec, list_smem, local_sem)
    own_list.start()
    own_list.wait()
    refs = (cat, U, V, L, RT, extra, pieces, natural)
    raw = count // 8
    depart.wait()

    def place_block(j, carry):
        moved[tile(j), :] = cat[pl.ds(slot_smem[0, j] * 8, 8), :]
        return carry

    lax.fori_loop(0, blocks, place_block, 0)
    keep = pltpu.make_async_copy(moved, cols_ref.at[0], local_sem)
    keep.start()
    for at, device in ((1, ahead), (2, down), (3, up)):
        copy = pltpu.make_async_remote_copy(
            src_ref=moved,
            dst_ref=cols_ref.at[at],
            send_sem=col_send.at[at - 1],
            recv_sem=col_recv.at[at - 1],
            device_id=device,
            device_id_type=MESH,
        )
        copy.start()
        copies.append(copy)
    keep.wait()
    build_groups(refs, raw, raw + blocks // 8, 2)
    build_groups(refs, 0, raw, 3)
    own_pairs(list_smem, refs, rings, early_ref)
    for copy in copies:
        copy.wait()


def rows_of(base, c):
    return pl.ds(base * 8 + c, 8, 8)


def tile(i):
    return pl.ds(pl.multiple_of(i * 8, 8), 8)


def table_steps(cols_ref, U, V, L, RT, extra, pieces, natural, never):
    rows = iota((8, 128), 0)
    eye = (iota((128, 128), 0) == iota((128, 128), 1)).astype(bf16)
    eyes = jnp.concatenate([eye, eye, eye], axis=1)
    c6 = jnp.where(rows == 6, 1.0, 0.0)
    c7 = jnp.where(rows == 7, 0.25, 0.0)
    ca = jnp.where(rows < 3, -2.0, 0.0)
    cb = jnp.where(rows < 6, -0.25, 0.0)
    ones = jnp.where(rows < 6, 1.0, 0.0)

    def dense(base):
        x = [cols_ref[rows_of(base, c), :] for c in range(3)]
        v = [cols_ref[rows_of(base, c), :] for c in range(3, 6)]
        radius = cols_ref[rows_of(base, 7), :]
        root = jnp.sqrt(radius)
        square = x[0] * x[0] + x[1] * x[1] + x[2] * x[2] + 0.5 * soften
        dot = x[0] * v[0] + x[1] * v[1] + x[2] * v[2]
        extra[rows_of(base, 3), :] = jnp.ones((8, 128), f32)
        extra[rows_of(base, 4), :] = root * cols_ref[rows_of(base, 6), :]
        extra[rows_of(base, 5), :] = root
        extra[rows_of(base, 6), :] = square
        extra[rows_of(base, 7), :] = dot
        for c, piece in enumerate(split3(square) + split3(0.25 * dot)):
            pieces[rows_of(base, c), :] = piece

    def swap(value):
        return jnp.where(rows < 3, pltpu.roll(value, 5, 0), pltpu.roll(value, 3, 0))

    def eight(base, shift, at, held=None):
        for q in range(8):
            i = base + q
            S = cols_ref[tile(i), :]
            if held is not None:
                S = jnp.where(never, held, S)
            E = extra[tile(i), :]
            G = pieces[tile(i), :]
            hi, mid = split2(jnp.where(rows < 3, S, jnp.where(rows < 6, E, 0.0)))
            L[i] = jnp.concatenate([hi, mid], axis=0).astype(bf16)
            full = jnp.where(rows < 6, S, E)
            hi, mid = split2(full)
            if at is not None:
                low = jnp.where(rows < 6, hi, full - hi - mid)
                natural[at, 32 * q : 32 * q + 32, :] = jnp.concatenate(
                    [hi, low, mid, ones], axis=0
                ).astype(bf16)
            a0 = hi * ca + c6
            a1 = mid * ca + c6
            b0 = swap(hi) * cb + c7
            b1 = swap(mid) * cb + c7
            A = jnp.concatenate([a0, a1, a0, jnp.where(rows < 3, G, 0.0)], axis=0)
            B = jnp.concatenate(
                [b0, b1, b0, jnp.where((rows >= 3) & (rows < 6), G, 0.0)], axis=0
            )
            V[i + shift, :, 0:128] = A.astype(bf16)
            V[i + shift, :, 128:256] = B.astype(bf16)

    def turn(at, u_base):
        turned = dot_tt(eye, natural[at]).astype(bf16)
        for q in range(8):
            U[u_base + q, :, 0:32] = turned[:, 32 * q : 32 * q + 32]

    def column(base, u_base):
        radius = cols_ref[rows_of(base, 7), :]
        three = jnp.concatenate(split3(radius), axis=1).astype(bf16)
        RT[lax.shift_right_logical(u_base, 3), :, 0:8] = dot_tt(eyes, three)

    return dense, eight, turn, column


def build_tables(refs, first, start, step):
    dense, eight, turn, column = table_steps(*refs, first < 0)
    cols_ref, U = refs[0:2]

    def turns(t):
        turn(0, 8 * t)
        turn(1, 96 + 8 * t)
        turn(2, 192 + 8 * t)
        column(8 * t, 8 * t)
        column(96 + 8 * t, 96 + 8 * t)
        column(288 + 8 * t, 192 + 8 * t)

    def body(t, carry):
        turns(jnp.maximum(t - 1, 0))
        for col in range(4):
            dense(96 * col + 8 * t)
        eight(8 * t, 0, 0)
        eight(96 + 8 * t, 192, 1)
        eight(288 + 8 * t, -96, 2)
        held = U[first & 63, 0:16, :].astype(f32)[0:8]
        eight(192 + 8 * t, -96, None, held)
        return step(t, carry)

    count = cols_ref.shape[0] // 256
    carry = lax.fori_loop(0, count, body, start)
    turns(count - 1)
    return carry


def build_groups(refs, low, high, step):
    dense, eight, turn, column = table_steps(*refs, None)

    def body(t, carry):
        bases = [8 * (t * step + low + q) for q in range(step)]
        for base in bases:
            dense(base)
        for at, base in enumerate(bases):
            eight(base, 0, at)
        for at, base in enumerate(bases):
            turn(at, base)
        for base in bases:
            column(base, base)
        return carry

    lax.fori_loop(0, (high - low) // step, body, 0)


def shares(wide):
    rows = iota((8, 128), 0)
    lanes = iota((8, 128), 1)
    b = lax.axis_index("gy")
    nb = lax.axis_size("gy")
    own = wide[1:9, :]
    behind = wide[0:8, :]
    far = jnp.where(lanes < 64, own, pltpu.roll(behind, 64, 1))
    local = jnp.where(lanes < 64, pltpu.roll(own, 64, 1), behind)
    load = (
        local
        + 2.0 * far
        + 2.0 * pltpu.roll(far, 127, 1)
        + pltpu.roll(far, 1, 1)
        + 3.0 * jnp.where(rows == 0, far, pltpu.roll(far, 1, 0))
    )
    column = lax.axis_index("gx") + rows - (reach - 1) - jnp.where(lanes < 64, 0, 1)
    phase = (column + 32) & 15
    for at, late in enumerate(lateness):
        load = load + jnp.where(phase == at, late, 0.0)
    passing = jnp.where(rows < 7, local, 0.0)

    def step(given):
        ahead, up = given
        now = load - ahead - up + pltpu.roll(ahead, 1, 0) + pltpu.roll(up, 1, 1)
        ahead = ahead + 0.26 * (now - pltpu.roll(now, 7, 0))
        ahead = jnp.minimum(jnp.maximum(ahead, 0.0), jnp.maximum(passing - up, 0.0))
        up = up + 0.26 * (now - pltpu.roll(now, 127, 1))
        up = jnp.minimum(jnp.maximum(up, 0.0), jnp.maximum(local - ahead, 0.0))
        return ahead, up

    def value(given, shift, base):
        column = lax.rem(b + shift + nb, nb)
        picked = (rows == reach - 1) & (lanes == column + base)
        return jnp.sum(jnp.where(picked, given, 0.0)).astype(i32)

    start = jnp.zeros((8, 128), f32)
    return (start, start), step, value


def pair_machine(entry, spot, spot_u, cols_ref, U, V, L, RT, AB, M):
    def distances(k, at):
        u, v = entry(k)
        AB[at][...] = jnp.dot(U[u, :, 0:32], V[v], preferred_element_type=f32)

    def weights(k, at):
        u, v = entry(k)
        rt = cols_ref[pl.ds(spot(v) * 8 + 7, 1), :]
        lane = jnp.full((8, 128), u & 7, i32)
        eighth = lax.shift_right_logical(u, 3)

        def radius(r):
            return jnp.take_along_axis(RT[eighth, r : r + 8, :], lane, axis=1)

        for r in range(0, 128, 16):
            A = AB[at][r : r + 16, 0:128]
            B = AB[at][r : r + 16, 128:256]
            R = jnp.concatenate([radius(r), radius(r + 8)], axis=0) + rt
            inv = lax.rsqrt(A)
            gap = R - A * inv
            inter = jnp.maximum(gap, 0.0)
            root = inter * lax.rsqrt(jnp.maximum(gap, tiny))
            W = (root * inv) * (inter - B * inv)
            G = root * lax.rsqrt(R)
            wh = W.astype(bf16)
            gh = G.astype(bf16)
            M[at][r : r + 16, 0:128] = wh
            M[at][r : r + 16, 128:256] = gh
            M[at][128 + r : 144 + r, 0:128] = (W - wh.astype(f32)).astype(bf16)
            M[at][128 + r : 144 + r, 128:256] = (G - gh.astype(f32)).astype(bf16)

    rows = iota((8, 128), 0)

    def folded(out):
        both = out[0:8] + out[8:16]
        return jnp.where(rows < 4, both[:, 0:128], both[:, 128:256])

    def both(k, at):
        u, v = entry(k)
        w = spot(v)
        o = spot_u(u)
        first = jnp.concatenate([L[o], L[o]], axis=1)
        second = jnp.concatenate([L[w], L[w]], axis=1)
        m = M[at]
        crossed = jnp.concatenate(
            [
                jnp.concatenate([m[0:128, 0:128], m[128:256, 0:128]], axis=1),
                jnp.concatenate([m[0:128, 128:256], m[128:256, 128:256]], axis=1),
            ],
            axis=0,
        )
        to_second = folded(jnp.dot(first, m[...], preferred_element_type=f32))
        to_first = folded(dot_tt(second, crossed))
        return o, w, to_first, to_second

    return distances, weights, both


def pair_kernel(
    lists_hbm,
    cols_hbm,
    wide_hbm,
    early_hbm,
    moved_ref,
    own_ref,
    sides_ref,
    lists_ref,
    cols_ref,
    wide,
    U,
    V,
    L,
    RT,
    extra,
    pieces,
    natural,
    acc,
    before,
    sem,
    *rings,
):
    AB = rings[0:ring]
    M = rings[ring : 2 * ring]
    copies = [
        pltpu.make_async_copy(source, target, sem.at[at])
        for at, (source, target) in enumerate(
            (
                (cols_hbm, cols_ref),
                (lists_hbm, lists_ref),
                (wide_hbm, wide),
                (early_hbm, before.at[0 : 16 * early]),
            )
        )
    ]
    for copy in copies:
        copy.start()
    trash = acc.shape[0] // 8 - 1
    acc[...] = jnp.zeros_like(acc)
    for copy in copies:
        copy.wait()
    keep = pltpu.make_async_copy(cols_ref.at[0:768], moved_ref, sem.at[4])
    keep.start()
    given, step, value = shares(wide)
    first = lists_ref[0]
    done = jnp.minimum(lists_ref[6 * 128 + 1], early)

    def turn_in(t, carry):
        for q in range(early_turn):
            k = t * early_turn + q
            live = k < done
            code = lists_ref[k]
            o = jnp.where(live, code & 511, trash)
            w = jnp.where(live, lax.shift_right_logical(code, 9), trash)
            acc[tile(o), :] += before[tile(2 * k), :]
            acc[tile(w), :] += before[tile(2 * k + 1), :]
        return step(carry)

    refs = (cols_ref, U, V, L, RT, extra, pieces, natural)
    given = build_tables(refs, first, given, turn_in)
    ahead_out = value(given[0], 0, 32)
    up_out = value(given[1], 0, 32)
    ahead_in = value(given[0], 0, 96)
    ahead_down = value(given[0], -1, 32)
    up_in = value(given[1], -1, 32)

    def begin(at, name):
        return lists_ref[at * 1024 + 6 * 128 + name]

    def cut(at, first, second):
        end = begin(at, 1)
        low = jnp.minimum(end, early)
        first = jnp.minimum(low + first, end)
        return low, first, jnp.minimum(first + second, end)

    _, _, kept = cut(0, ahead_out, up_out)
    ahead_low, ahead_high, _ = cut(3, ahead_in, 0)
    _, up_low, up_high = cut(2, ahead_down, up_in)
    ends = []
    shifts = []
    so_far = 0
    for at, low, high in (
        (0, kept, begin(0, 1)),
        (0, begin(0, 1), begin(0, 2)),
        (1, begin(1, 2), begin(1, 3)),
        (2, begin(2, 3), begin(2, 4)),
        (3, begin(3, 4), begin(3, 5)),
        (3, ahead_low, ahead_high),
        (2, up_low, up_high),
    ):
        shifts.append(at * 1024 + low - so_far)
        so_far = so_far + (high - low)
        ends.append(so_far)
    n = so_far
    last = jnp.maximum(n - 1, 0)

    def entry(k):
        k = jnp.minimum(k, last)
        shift = shifts[6]
        for at in range(5, -1, -1):
            shift = jnp.where(k < ends[at], shifts[at], shift)
        code = lists_ref[k + shift]
        code = code + jnp.where(
            k < ends[4], 0, jnp.where(k < ends[5], 96 + 512 * 288, 192 + 512 * 192)
        )
        return code & 511, lax.shift_right_logical(code, 9)

    def spot_u(u):
        return jnp.where(u < 192, u, u + 96)

    def spot(v):
        return jnp.where(v < 96, v, jnp.where(v < 288, v + 96, v - 192))

    distances, weights, both = pair_machine(entry, spot, spot_u, cols_ref, U, V, L, RT, AB, M)

    def sums(k, at):
        o, w, to_first, to_second = both(k, at)
        live = k < n
        o = jnp.where(live, o, trash)
        w = jnp.where(live, w, trash)
        acc[tile(o), :] += to_first
        acc[tile(w), :] += to_second

    for q in range(ring):
        distances(q, q)
    for q in range(lag_b):
        weights(q, q)

    def turn(t, carry):
        for q in range(group):
            k = t * group + q
            sums(k, q % ring)
            weights(k + lag_b, (q + lag_b) % ring)
            distances(k + ring, q % ring)
        return carry

    lax.fori_loop(0, lax.div(n + group - 1, group), turn, 0)

    def close(base, out_ref, out_base):
        got = [acc[rows_of(base, c), :] for c in range(6)]
        terms = []
        for c in range(3):
            hi, mid = split2(cols_ref[rows_of(base, c), :])
            terms.append(stiffness * ((hi + mid) * got[3] - got[c]))
        root = conductance * extra[rows_of(base, 5), :]
        terms.append(root * (got[4] - cols_ref[rows_of(base, 6), :] * got[5]))
        for c in range(4):
            out_ref[pl.ds(out_base + c, 8, 4), :] = terms[c]

    def close_all(t, carry):
        close(8 * t, own_ref, 32 * t)
        for side in range(3):
            close(96 * (side + 1) + 8 * t, sides_ref, 384 * side + 32 * t)
        return carry

    lax.fori_loop(0, 12, close_all, 0)
    keep.wait()


def finish_kernel(
    moved_hbm,
    sides_ref,
    flags_hbm,
    cells_hbm,
    table_hbm,
    mix_ref,
    fluid_ref,
    moved_ref,
    flags_ref,
    cells_ref,
    table_ref,
    in_sem,
    sums,
    send,
    recv,
):
    ahead, behind, up, down = neighbours()
    inputs = [
        pltpu.make_async_copy(source, target, in_sem.at[at])
        for at, (source, target) in enumerate(
            (
                (moved_hbm, moved_ref),
                (flags_hbm, flags_ref),
                (cells_hbm, cells_ref),
                (table_hbm, table_ref),
            )
        )
    ]
    for copy in inputs:
        copy.start()
    greet((ahead, behind, up, down))
    await_all((ahead, behind, up, down))
    copies = []
    span = sides_ref.shape[0] // 3
    blocks = span // 4
    for at, device in ((0, behind), (1, up), (2, down)):
        copy = pltpu.make_async_remote_copy(
            src_ref=sides_ref.at[span * at : span * at + span],
            dst_ref=mix_ref.at[span * at : span * at + span],
            send_sem=send.at[at],
            recv_sem=recv.at[at],
            device_id=device,
            device_id_type=MESH,
        )
        copy.start()
        copies.append(copy)

    for copy in inputs:
        copy.wait()
    square = jnp.concatenate([table_ref[:, 16 * a : 16 * a + 16] for a in range(16)], axis=0)
    table = jnp.concatenate(split3(square), axis=0).astype(bf16)
    sums[...] = jnp.zeros_like(sums)
    sub = iota((16, 128), 0)

    def cells_of(g, carry):
        at = pl.ds(pl.multiple_of(g * 8, 8), 8)
        temper = moved_ref[rows_of(g * 8, 6), :]
        radius = moved_ref[rows_of(g * 8, 7), :]
        volume = 4.0 / 3.0 * math.pi * radius * radius * radius
        cell = cells_ref[at, :]
        high = lax.shift_right_logical(cell, 4)
        low = cell & 15
        fluid = []
        hots = []
        for c in range(8):
            hot_high = (sub == high[c : c + 1]).astype(f32)
            hot_low = (sub == low[c : c + 1]).astype(f32)
            parts = jnp.dot(table, hot_low.astype(bf16), preferred_element_type=f32)
            value = parts[0:16] + parts[16:32] + parts[32:48]
            fluid.append(jnp.sum(value * hot_high, axis=0, keepdims=True))
            hots.append((hot_high, hot_low))
        flow = film_gain * radius * radius * (temper - jnp.concatenate(fluid, axis=0))
        pieces = split3(volume) + split3(flow)
        total = sums[...]
        for c in range(8):
            hot_high, hot_low = hots[c]
            spread = jnp.concatenate([hot_low * piece[c : c + 1] for piece in pieces], axis=0)
            total = total + dot_tt(hot_high.astype(bf16), spread.astype(bf16))
        sums[...] = total
        wall = wall_gain * flags_ref[at, :].astype(f32) * (wall_temp - temper) * radius
        mix_ref[pl.ds(pl.multiple_of(3 * span + g * 8, 8), 8), :] = wall - flow
        mix_ref[pl.ds(pl.multiple_of(3 * span + blocks + g * 8, 8), 8), :] = 1.0 / volume
        return carry

    lax.fori_loop(0, 12, cells_of, 0)
    total = sums[...]
    solid = (total[:, 0:16] + total[:, 16:32] + total[:, 32:48]) / cell_volume
    heat = total[:, 48:64] + total[:, 64:80] + total[:, 80:96]
    for a in range(16):
        fluid_ref[0:1, 16 * a : 16 * a + 16] = solid[a : a + 1]
        fluid_ref[1:2, 16 * a : 16 * a + 16] = heat[a : a + 1]
    for copy in copies:
        copy.wait()


def rates_kernel(
    own_hbm, mix_hbm, fluid_hbm, rates_ref, fluid_ref, own, mix, fluid, sem
):
    copies = [
        pltpu.make_async_copy(source, target, sem.at[at])
        for at, (source, target) in enumerate(
            ((mix_hbm, mix), (own_hbm, own), (fluid_hbm, fluid))
        )
    ]
    for copy in copies:
        copy.start()
    for copy in copies:
        copy.wait()
    fluid_ref[...] = fluid[...]
    span = own.shape[0]
    blocks = span // 4

    def combine(g, carry):
        at = pl.multiple_of(g * 8, 8)
        inverse = mix[pl.ds(3 * span + blocks + at, 8), :]
        for c in range(4):
            here = pl.ds(g * 32 + c, 8, 4)
            value = own[here, :]
            for side in range(3):
                value = value + mix[pl.ds(span * side + g * 32 + c, 8, 4), :]
            if c == 3:
                value = value + mix[pl.ds(3 * span + at, 8), :]
            value = value * inverse
            if c == 2:
                value = value - gravity
            rates_ref[here, :] = value
        return carry

    lax.fori_loop(0, blocks // 8, combine, 0, unroll=4)


def anywhere():
    return pl.BlockSpec(memory_space=pl.ANY)


def vmem():
    return pl.BlockSpec(memory_space=pltpu.VMEM)


def shards(state, leaving, pairs, counts, wall_flags, cell_index, fluid_temp):
    mine = state[0, 0]
    blocks = mine.shape[0]
    count = leaving.shape[2]
    lanes = -(-pairs.shape[3] // 128) * 128
    cols, lists, wide, ahead_of = pl.pallas_call(
        halo_kernel,
        out_shape=(
            jax.ShapeDtypeStruct((4, 8 * blocks, 128), f32),
            jax.ShapeDtypeStruct((4, 8, 128), i32),
            jax.ShapeDtypeStruct((16, 128), f32),
            jax.ShapeDtypeStruct((16 * early, 128), f32),
        ),
        in_specs=[anywhere()] * 4,
        out_specs=(anywhere(), vmem(), vmem(), vmem()),
        scratch_shapes=[
            pltpu.SMEM(leaving.shape[2:], i32),
            pltpu.SMEM(counts.shape[2:], i32),
            pltpu.VMEM(pairs.shape[2:], i32),
            pltpu.VMEM((8 * (count + blocks), 128), f32),
            pltpu.VMEM((8 * count, 128), f32),
            pltpu.VMEM((8 * blocks, 128), f32),
            pltpu.VMEM((8, lanes), i32),
            pltpu.VMEM((8, 128), i32),
            pltpu.SMEM((8, 128), i32),
            pltpu.SemaphoreType.DMA,
            pltpu.SemaphoreType.DMA,
            pltpu.SemaphoreType.DMA((3,)),
            pltpu.SemaphoreType.DMA((3,)),
            pltpu.SemaphoreType.DMA((3,)),
            pltpu.SemaphoreType.DMA((3,)),
            pltpu.SemaphoreType.DMA,
            pltpu.SemaphoreType.DMA((5,)),
            pltpu.VMEM((8, 128), f32),
            pltpu.SemaphoreType.DMA((3,)),
            pltpu.SemaphoreType.DMA((3,)),
            pltpu.SemaphoreType.DMA((2 * reach,)),
            pltpu.SemaphoreType.DMA((2 * reach,)),
            pltpu.VMEM((8, 128), i32),
            pltpu.SMEM((8, 128), i32),
            pltpu.VMEM((count + blocks, 128, 128), bf16),
            pltpu.VMEM((count + blocks, 32, 256), bf16),
            pltpu.VMEM((count + blocks, 16, 128), bf16),
            pltpu.VMEM(((count + blocks) // 8, 128, 128), f32),
            pltpu.VMEM((8 * (count + blocks), 128), f32),
            pltpu.VMEM((8 * (count + blocks), 128), f32),
            pltpu.VMEM((3, 256, 128), bf16),
        ]
        + [pltpu.VMEM((128, 256), f32)] * ring
        + [pltpu.VMEM((256, 256), bf16)] * ring,
        compiler_params=pltpu.CompilerParams(
            collective_id=0, has_side_effects=True, vmem_limit_bytes=vmem_grant
        ),
        name="halo",
    )(leaving[0, 0], counts[0, 0], pairs[0, 0], mine.reshape(8 * blocks, 128))

    moved, own, sides = pl.pallas_call(
        pair_kernel,
        out_shape=(
            jax.ShapeDtypeStruct((8 * blocks, 128), f32),
            jax.ShapeDtypeStruct((4 * blocks, 128), f32),
            jax.ShapeDtypeStruct((12 * blocks, 128), f32),
        ),
        in_specs=[anywhere()] * 4,
        out_specs=(anywhere(), vmem(), vmem()),
        scratch_shapes=[
            pltpu.SMEM((4096,), i32),
            pltpu.VMEM((32 * blocks, 128), f32),
            pltpu.VMEM((16, 128), f32),
            pltpu.VMEM((3 * blocks, 128, 128), bf16),
            pltpu.VMEM((4 * blocks, 32, 256), bf16),
            pltpu.VMEM((4 * blocks, 16, 128), bf16),
            pltpu.VMEM((3 * blocks // 8, 128, 128), f32),
            pltpu.VMEM((32 * blocks, 128), f32),
            pltpu.VMEM((32 * blocks, 128), f32),
            pltpu.VMEM((3, 256, 128), bf16),
            pltpu.VMEM((32 * blocks + 8, 128), f32),
            pltpu.VMEM((16 * early_turn * blocks // 8, 128), f32),
            pltpu.SemaphoreType.DMA((5,)),
        ]
        + [pltpu.VMEM((128, 256), f32)] * ring
        + [pltpu.VMEM((256, 256), bf16)] * ring,
        compiler_params=pltpu.CompilerParams(vmem_limit_bytes=vmem_grant),
        name="contact",
    )(lists.reshape(4096), cols.reshape(32 * blocks, 128), wide, ahead_of)

    mix, fluid = pl.pallas_call(
        finish_kernel,
        out_shape=(
            jax.ShapeDtypeStruct((14 * blocks, 128), f32),
            jax.ShapeDtypeStruct((2, 256), f32),
        ),
        in_specs=[anywhere()] * 5,
        out_specs=(vmem(), vmem()),
        scratch_shapes=[
            pltpu.VMEM((8 * blocks, 128), f32),
            pltpu.VMEM((blocks, 128), i32),
            pltpu.VMEM((blocks, 128), i32),
            pltpu.VMEM((1, 256), f32),
            pltpu.SemaphoreType.DMA((4,)),
            pltpu.VMEM((16, 96), f32),
            pltpu.SemaphoreType.DMA((3,)),
            pltpu.SemaphoreType.DMA((3,)),
        ],
        compiler_params=pltpu.CompilerParams(
            collective_id=1, has_side_effects=True, vmem_limit_bytes=vmem_grant
        ),
        name="finish",
    )(moved, sides, wall_flags[0, 0], cell_index[0, 0], fluid_temp.reshape(1, 256))

    rates, fluid = pl.pallas_call(
        rates_kernel,
        out_shape=(
            jax.ShapeDtypeStruct((4 * blocks, 128), f32),
            jax.ShapeDtypeStruct((2, 256), f32),
        ),
        in_specs=[anywhere()] * 3,
        out_specs=(vmem(), vmem()),
        scratch_shapes=[
            pltpu.VMEM((4 * blocks, 128), f32),
            pltpu.VMEM((14 * blocks, 128), f32),
            pltpu.VMEM((2, 256), f32),
            pltpu.SemaphoreType.DMA((3,)),
        ],
        compiler_params=pltpu.CompilerParams(vmem_limit_bytes=vmem_grant),
        name="rates",
    )(own, mix, fluid)
    return (
        moved.reshape(1, 1, blocks, 8, 128),
        rates.reshape(1, 1, blocks, 4, 128),
        fluid[None, None],
    )


def solution(mesh):
    in_specs = (
        P("gx", "gy", None, None, None),
        P("gx", "gy", None),
        P("gx", "gy", None, None),
        P("gx", "gy", None),
        P("gx", "gy", None, None),
        P("gx", "gy", None, None),
        P("gx", "gy", None),
    )
    out_specs = (
        P("gx", "gy", None, None, None),
        P("gx", "gy", None, None, None),
        P("gx", "gy", None, None),
    )
    return jax.shard_map(shards, mesh=mesh, in_specs=in_specs, out_specs=out_specs, check_vma=False)
```

```python
import functools
import math

import jax
import jax.numpy as jnp
from jax import lax
from jax.experimental import pallas as pl
from jax.experimental.pallas import tpu as pltpu
from jax.sharding import PartitionSpec as P

soften = 0.01
stiffness = 0.2
damping = 0.05
conductance = 0.05
film_gain = 0.5
wall_gain = 2.0
wall_temp = 1.0
gravity = 1.0
cell_volume = 32.0

f32 = jnp.float32
bf16 = jnp.bfloat16
i32 = jnp.int32

tiny = 1e-30
group = 16
lag_a = 2
lag_b = 2
ring = lag_a + lag_b
reach = 4
lateness = (50.0, 28.0, 22.0, 125.0, 20.0, 0.0, 0.0, 0.0, 0.0, 0.0, 0.0, 0.0, 85.0, 0.0, 0.0, 35.0)
early = 64
early_turn = 6
vmem_grant = 56 * 2**20
MESH = pl.DeviceIdType.MESH


def iota(shape, dim):
    return lax.broadcasted_iota(i32, shape, dim)


def split2(value):
    hi = value.astype(bf16).astype(f32)
    return hi, (value - hi).astype(bf16).astype(f32)


def split3(value):
    hi = value.astype(bf16).astype(f32)
    rest = value - hi
    mid = rest.astype(bf16).astype(f32)
    return hi, mid, rest - mid


def dot_tt(left, right):
    return lax.dot_general(left, right, (((1,), (1,)), ((), ())), preferred_element_type=f32)


def neighbours():
    a = lax.axis_index("gx")
    b = lax.axis_index("gy")
    na = lax.axis_size("gx")
    nb = lax.axis_size("gy")
    return (
        {"gx": lax.rem(a + 1, na)},
        {"gx": lax.rem(a + na - 1, na)},
        {"gy": lax.rem(b + 1, nb)},
        {"gy": lax.rem(b + nb - 1, nb)},
    )


def greet(everyone):
    barrier = pltpu.get_barrier_semaphore()
    for device in everyone:
        pl.semaphore_signal(barrier, inc=1, device_id=device, device_id_type=MESH)


def await_all(everyone):
    pl.semaphore_wait(pltpu.get_barrier_semaphore(), len(everyone))


def sort_pairs(lanes, pad, total):
    own = pad[0:1, :]
    code = pad[1:2, :]
    region = jnp.zeros_like(code)
    for step in range(1, 9):
        region = region + (code >= 96 * step).astype(i32)
    far = code - 96 * region
    live = iota((1, lanes), 1) < total

    def among(*names):
        hit = region == names[0]
        for name in names[1:]:
            hit = hit | (region == name)
        return hit

    kind = jnp.where(
        among(4),
        0,
        jnp.where(among(1, 5), 1, jnp.where(among(0, 3), 2, jnp.where(among(2), 3, 4))),
    )
    kind = jnp.where(live, kind, 5)
    u_far = among(0, 1, 2, 3)
    u = jnp.where(u_far, far, own) + jnp.where(among(4, 5, 3), 0, 96)
    v_slot = jnp.where(u_far, own, far)
    v_side = jnp.where(among(4, 1, 7), 0, jnp.where(among(5, 3, 0, 8), 1, 2))
    ranks = iota((8, lanes), 0)
    marks = (ranks == kind).astype(f32)
    before = (iota((lanes, lanes), 0) < iota((lanes, lanes), 1)).astype(bf16)
    seen = jnp.dot(marks.astype(bf16), before, preferred_element_type=f32)
    starts = jnp.sum((kind < ranks).astype(f32), axis=1, keepdims=True)
    place = jnp.sum(marks * (seen + starts), axis=0, keepdims=True)
    target = (iota((lanes, lanes), 0).astype(f32) == place).astype(bf16)
    rows = iota((8, lanes), 0)
    values = jnp.where(
        rows == 0, u, jnp.where(rows == 1, v_slot, jnp.where(rows == 2, v_side, 0))
    )
    moved = dot_tt(values.astype(bf16), target)
    packed = moved[0:1] + 512.0 * (moved[1:2] + 96.0 * moved[2:3])
    diag = iota((8, 128), 0) == iota((8, 128), 1)
    begin = jnp.sum(jnp.where(diag, starts, 0.0), axis=0, keepdims=True)
    return packed.astype(i32), begin.astype(i32)


def own_pairs(list_smem, refs, rings, early_ref):
    cols_ref, U, V, L, RT = refs[0:5]
    AB = rings[0:ring]
    M = rings[ring : 2 * ring]
    last = U.shape[0] - 1

    def entry(k):
        k = jnp.minimum(k, early - 1)
        code = list_smem[lax.shift_right_logical(k, 7), k & 127]
        u = jnp.minimum(code & 511, last)
        return u, jnp.minimum(lax.shift_right_logical(code, 9), last)

    def same(block):
        return block

    distances, weights, both = pair_machine(entry, same, same, cols_ref, U, V, L, RT, AB, M)
    for q in range(ring):
        distances(q, q)
    for q in range(lag_b):
        weights(q, q)

    def turn(t, carry):
        for q in range(group):
            k = t * group + q
            _, _, to_first, to_second = both(k, q % ring)
            early_ref[tile(2 * k), :] = to_first
            early_ref[tile(2 * k + 1), :] = to_second
            weights(k + lag_b, (q + lag_b) % ring)
            distances(k + ring, q % ring)
        return carry

    lax.fori_loop(0, early // group, turn, 0)


def halo_kernel(
    leaving_hbm,
    counts_hbm,
    pairs_hbm,
    state_hbm,
    cols_ref,
    lists_ref,
    wide_ref,
    early_ref,
    leaving_ref,
    counts_ref,
    pairs_ref,
    cat,
    dep,
    moved,
    pad,
    slot_vec,
    slot_smem,
    dep_send,
    dep_recv,
    list_send,
    list_recv,
    col_send,
    col_recv,
    local_sem,
    in_sem,
    near,
    near_send,
    near_recv,
    wide_send,
    wide_recv,
    list_vec,
    list_smem,
    U,
    V,
    L,
    RT,
    extra,
    pieces,
    natural,
    *rings,
):
    blocks = state_hbm.shape[0] // 8
    count = leaving_hbm.shape[0]
    ahead, behind, up, down = neighbours()
    a = lax.axis_index("gx")
    na = lax.axis_size("gx")
    along = {
        step: {"gx": lax.rem(a + step + na, na)} for step in range(-reach, reach + 1) if step
    }
    b = lax.axis_index("gy")
    nb = lax.axis_size("gy")
    across = {"gy": lax.rem(b + 2, nb)}
    everyone = (up, down, across, *along.values())
    state_ref = cat.at[8 * count : 8 * count + 8 * blocks]
    inputs = [
        pltpu.make_async_copy(source, target, in_sem.at[at])
        for at, (source, target) in enumerate(
            (
                (leaving_hbm, leaving_ref),
                (state_hbm, state_ref),
                (pairs_hbm, pairs_ref),
                (counts_hbm, counts_ref),
                (state_hbm, moved),
            )
        )
    ]
    for copy in inputs:
        copy.start()
    wide_ref[...] = jnp.zeros_like(wide_ref)
    greet(everyone)
    for copy in inputs:
        copy.wait()
    local = jnp.maximum(counts_ref[0] - early, 0).astype(f32)
    far = (counts_ref[1] - counts_ref[0]).astype(f32) * 0.125
    lane = iota((1, 128), 1)
    near[0:1, :] = jnp.where(lane < 64, far, local)
    for m in range(count):
        dep[8 * m : 8 * m + 8, :] = moved[pl.ds(leaving_ref[m] * 8, 8), :]
    await_all(everyone)
    asks = []
    for at, device in ((1, down), (2, up), (3, across)):
        copy = pltpu.make_async_remote_copy(
            src_ref=near.at[0:1],
            dst_ref=near.at[at : at + 1],
            send_sem=near_send.at[at - 1],
            recv_sem=near_recv.at[at - 1],
            device_id=device,
            device_id_type=MESH,
        )
        copy.start()
        asks.append(copy)
    depart = pltpu.make_async_remote_copy(
        src_ref=dep,
        dst_ref=cat.at[0 : 8 * count],
        send_sem=dep_send,
        recv_sem=dep_recv,
        device_id=ahead,
        device_id_type=MESH,
    )
    depart.start()
    place = iota((8, 128), 1)
    slot = place + count
    for m in range(count):
        slot = jnp.where(place == leaving_ref[m], m, slot)
    slot_vec[...] = slot
    to_smem = pltpu.make_async_copy(slot_vec, slot_smem, local_sem)
    to_smem.start()
    lanes = pad.shape[1]
    pad[...] = jnp.zeros_like(pad)
    pad[0:2, 0 : pairs_ref.shape[1]] = pairs_ref[...]
    packed, begin = sort_pairs(lanes, pad, counts_ref[1])
    lists_ref[0] = jnp.zeros((8, 128), i32)
    for row in range(lanes // 128):
        lists_ref[0, row : row + 1, :] = packed[:, 128 * row : 128 * row + 128]
    lists_ref[0, 6:7, :] = begin
    copies = []
    for copy in asks:
        copy.wait()
    turn = lane & 3
    row = near[0:1, :]
    for at, step in ((1, 1), (2, nb - 1), (3, 2)):
        row = jnp.where(turn == lax.rem(b + step, nb), near[at : at + 1, :], row)
    wide_ref[reach : reach + 1, :] = row
    for at, step in enumerate(along):
        copy = pltpu.make_async_remote_copy(
            src_ref=wide_ref.at[reach : reach + 1],
            dst_ref=wide_ref.at[reach - step : reach - step + 1],
            send_sem=wide_send.at[at],
            recv_sem=wide_recv.at[at],
            device_id=along[step],
            device_id_type=MESH,
        )
        copy.start()
        copies.append(copy)
    for at, device in ((1, down), (2, up), (3, ahead)):
        copy = pltpu.make_async_remote_copy(
            src_ref=lists_ref.at[0],
            dst_ref=lists_ref.at[at],
            send_sem=list_send.at[at - 1],
            recv_sem=list_recv.at[at - 1],
            device_id=device,
            device_id_type=MESH,
        )
        copy.start()
        copies.append(copy)
    to_smem.wait()
    codes = lists_ref[0]
    u = jnp.take_along_axis(slot, jnp.minimum(codes & 511, 95), axis=1)
    v = jnp.take_along_axis(
        slot, jnp.minimum(lax.shift_right_logical(codes, 9), 95), axis=1
    )
    list_vec[...] = u + 512 * v
    own_list = pltpu.make_async_copy(list_vec, list_smem, local_sem)
    own_list.start()
    own_list.wait()
    refs = (cat, U, V, L, RT, extra, pieces, natural)
    raw = count // 8
    depart.wait()

    def place_block(j, carry):
        moved[tile(j), :] = cat[pl.ds(slot_smem[0, j] * 8, 8), :]
        return carry

    lax.fori_loop(0, blocks, place_block, 0)
    keep = pltpu.make_async_copy(moved, cols_ref.at[0], local_sem)
    keep.start()
    for at, device in ((1, ahead), (2, down), (3, up)):
        copy = pltpu.make_async_remote_copy(
            src_ref=moved,
            dst_ref=cols_ref.at[at],
            send_sem=col_send.at[at - 1],
            recv_sem=col_recv.at[at - 1],
            device_id=device,
            device_id_type=MESH,
        )
        copy.start()
        copies.append(copy)
    build_groups(refs, raw, raw + blocks // 8, 2)
    build_groups(refs, 0, raw, 3)
    own_pairs(list_smem, refs, rings, early_ref)
    keep.wait()
    for copy in copies:
        copy.wait()


def rows_of(base, c):
    return pl.ds(base * 8 + c, 8, 8)


def tile(i):
    return pl.ds(pl.multiple_of(i * 8, 8), 8)


def table_steps(cols_ref, U, V, L, RT, extra, pieces, natural, never):
    rows = iota((8, 128), 0)
    eye = (iota((128, 128), 0) == iota((128, 128), 1)).astype(bf16)
    eyes = jnp.concatenate([eye, eye, eye], axis=1)
    c6 = jnp.where(rows == 6, 1.0, 0.0)
    c7 = jnp.where(rows == 7, 0.25, 0.0)
    ca = jnp.where(rows < 3, -2.0, 0.0)
    cb = jnp.where(rows < 6, -0.25, 0.0)
    ones = jnp.where(rows < 6, 1.0, 0.0)

    def dense(base):
        x = [cols_ref[rows_of(base, c), :] for c in range(3)]
        v = [cols_ref[rows_of(base, c), :] for c in range(3, 6)]
        radius = cols_ref[rows_of(base, 7), :]
        root = jnp.sqrt(radius)
        square = x[0] * x[0] + x[1] * x[1] + x[2] * x[2] + 0.5 * soften
        dot = x[0] * v[0] + x[1] * v[1] + x[2] * v[2]
        extra[rows_of(base, 3), :] = jnp.ones((8, 128), f32)
        extra[rows_of(base, 4), :] = root * cols_ref[rows_of(base, 6), :]
        extra[rows_of(base, 5), :] = root
        extra[rows_of(base, 6), :] = square
        extra[rows_of(base, 7), :] = dot
        for c, piece in enumerate(split3(square) + split3(0.25 * dot)):
            pieces[rows_of(base, c), :] = piece

    def swap(value):
        return jnp.where(rows < 3, pltpu.roll(value, 5, 0), pltpu.roll(value, 3, 0))

    def eight(base, shift, at, held=None):
        for q in range(8):
            i = base + q
            S = cols_ref[tile(i), :]
            if held is not None:
                S = jnp.where(never, held, S)
            E = extra[tile(i), :]
            G = pieces[tile(i), :]
            hi, mid = split2(jnp.where(rows < 3, S, jnp.where(rows < 6, E, 0.0)))
            L[i] = jnp.concatenate([hi, mid], axis=0).astype(bf16)
            full = jnp.where(rows < 6, S, E)
            hi, mid = split2(full)
            if at is not None:
                low = jnp.where(rows < 6, hi, full - hi - mid)
                natural[at, 32 * q : 32 * q + 32, :] = jnp.concatenate(
                    [hi, low, mid, ones], axis=0
                ).astype(bf16)
            a0 = hi * ca + c6
            a1 = mid * ca + c6
            b0 = swap(hi) * cb + c7
            b1 = swap(mid) * cb + c7
            A = jnp.concatenate([a0, a1, a0, jnp.where(rows < 3, G, 0.0)], axis=0)
            B = jnp.concatenate(
                [b0, b1, b0, jnp.where((rows >= 3) & (rows < 6), G, 0.0)], axis=0
            )
            V[i + shift, :, 0:128] = A.astype(bf16)
            V[i + shift, :, 128:256] = B.astype(bf16)

    def turn(at, u_base):
        turned = dot_tt(eye, natural[at]).astype(bf16)
        for q in range(8):
            U[u_base + q, :, 0:32] = turned[:, 32 * q : 32 * q + 32]

    def column(base, u_base):
        radius = cols_ref[rows_of(base, 7), :]
        three = jnp.concatenate(split3(radius), axis=1).astype(bf16)
        RT[lax.shift_right_logical(u_base, 3), :, 0:8] = dot_tt(eyes, three)

    return dense, eight, turn, column


def build_tables(refs, first, start, step):
    dense, eight, turn, column = table_steps(*refs, first < 0)
    cols_ref, U = refs[0:2]

    def turns(t):
        turn(0, 8 * t)
        turn(1, 96 + 8 * t)
        turn(2, 192 + 8 * t)
        column(8 * t, 8 * t)
        column(96 + 8 * t, 96 + 8 * t)
        column(288 + 8 * t, 192 + 8 * t)

    def body(t, carry):
        turns(jnp.maximum(t - 1, 0))
        for col in range(4):
            dense(96 * col + 8 * t)
        eight(8 * t, 0, 0)
        eight(96 + 8 * t, 192, 1)
        eight(288 + 8 * t, -96, 2)
        held = U[first & 63, 0:16, :].astype(f32)[0:8]
        eight(192 + 8 * t, -96, None, held)
        return step(t, carry)

    count = cols_ref.shape[0] // 256
    carry = lax.fori_loop(0, count, body, start)
    turns(count - 1)
    return carry


def build_groups(refs, low, high, step):
    dense, eight, turn, column = table_steps(*refs, None)

    def body(t, carry):
        bases = [8 * (t * step + low + q) for q in range(step)]
        for base in bases:
            dense(base)
        for at, base in enumerate(bases):
            eight(base, 0, at)
        for at, base in enumerate(bases):
            turn(at, base)
        for base in bases:
            column(base, base)
        return carry

    lax.fori_loop(0, (high - low) // step, body, 0)


def shares(wide):
    rows = iota((8, 128), 0)
    lanes = iota((8, 128), 1)
    b = lax.axis_index("gy")
    nb = lax.axis_size("gy")
    own = wide[1:9, :]
    behind = wide[0:8, :]
    far = jnp.where(lanes < 64, own, pltpu.roll(behind, 64, 1))
    local = jnp.where(lanes < 64, pltpu.roll(own, 64, 1), behind)
    load = (
        local
        + 2.0 * far
        + 2.0 * pltpu.roll(far, 127, 1)
        + pltpu.roll(far, 1, 1)
        + 3.0 * jnp.where(rows == 0, far, pltpu.roll(far, 1, 0))
    )
    column = lax.axis_index("gx") + rows - (reach - 1) - jnp.where(lanes < 64, 0, 1)
    phase = (column + 32) & 15
    for at, late in enumerate(lateness):
        load = load + jnp.where(phase == at, late, 0.0)
    passing = jnp.where(rows < 7, local, 0.0)

    def step(given):
        ahead, up = given
        now = load - ahead - up + pltpu.roll(ahead, 1, 0) + pltpu.roll(up, 1, 1)
        ahead = ahead + 0.26 * (now - pltpu.roll(now, 7, 0))
        ahead = jnp.minimum(jnp.maximum(ahead, 0.0), jnp.maximum(passing - up, 0.0))
        up = up + 0.26 * (now - pltpu.roll(now, 127, 1))
        up = jnp.minimum(jnp.maximum(up, 0.0), jnp.maximum(local - ahead, 0.0))
        return ahead, up

    def value(given, shift, base):
        column = lax.rem(b + shift + nb, nb)
        picked = (rows == reach - 1) & (lanes == column + base)
        return jnp.sum(jnp.where(picked, given, 0.0)).astype(i32)

    start = jnp.zeros((8, 128), f32)
    return (start, start), step, value


def pair_machine(entry, spot, spot_u, cols_ref, U, V, L, RT, AB, M):
    def distances(k, at):
        u, v = entry(k)
        AB[at][...] = jnp.dot(U[u, :, 0:32], V[v], preferred_element_type=f32)

    def weights(k, at):
        u, v = entry(k)
        rt = cols_ref[pl.ds(spot(v) * 8 + 7, 1), :]
        lane = jnp.full((8, 128), u & 7, i32)
        eighth = lax.shift_right_logical(u, 3)

        def radius(r):
            return jnp.take_along_axis(RT[eighth, r : r + 8, :], lane, axis=1)

        for r in range(0, 128, 16):
            A = AB[at][r : r + 16, 0:128]
            B = AB[at][r : r + 16, 128:256]
            R = jnp.concatenate([radius(r), radius(r + 8)], axis=0) + rt
            inv = lax.rsqrt(A)
            gap = R - A * inv
            inter = jnp.maximum(gap, 0.0)
            root = inter * lax.rsqrt(jnp.maximum(gap, tiny))
            W = (root * inv) * (inter - B * inv)
            G = root * lax.rsqrt(R)
            wh = W.astype(bf16)
            gh = G.astype(bf16)
            M[at][r : r + 16, 0:128] = wh
            M[at][r : r + 16, 128:256] = gh
            M[at][128 + r : 144 + r, 0:128] = (W - wh.astype(f32)).astype(bf16)
            M[at][128 + r : 144 + r, 128:256] = (G - gh.astype(f32)).astype(bf16)

    rows = iota((8, 128), 0)

    def folded(out):
        both = out[0:8] + out[8:16]
        return jnp.where(rows < 4, both[:, 0:128], both[:, 128:256])

    def both(k, at):
        u, v = entry(k)
        w = spot(v)
        o = spot_u(u)
        first = jnp.concatenate([L[o], L[o]], axis=1)
        second = jnp.concatenate([L[w], L[w]], axis=1)
        m = M[at]
        crossed = jnp.concatenate(
            [
                jnp.concatenate([m[0:128, 0:128], m[128:256, 0:128]], axis=1),
                jnp.concatenate([m[0:128, 128:256], m[128:256, 128:256]], axis=1),
            ],
            axis=0,
        )
        to_second = folded(jnp.dot(first, m[...], preferred_element_type=f32))
        to_first = folded(dot_tt(second, crossed))
        return o, w, to_first, to_second

    return distances, weights, both


def pair_kernel(
    lists_hbm,
    cols_hbm,
    wide_hbm,
    early_hbm,
    moved_ref,
    own_ref,
    sides_ref,
    lists_ref,
    cols_ref,
    wide,
    U,
    V,
    L,
    RT,
    extra,
    pieces,
    natural,
    acc,
    before,
    sem,
    *rings,
):
    AB = rings[0:ring]
    M = rings[ring : 2 * ring]
    copies = [
        pltpu.make_async_copy(source, target, sem.at[at])
        for at, (source, target) in enumerate(
            (
                (cols_hbm, cols_ref),
                (lists_hbm, lists_ref),
                (wide_hbm, wide),
                (early_hbm, before.at[0 : 16 * early]),
            )
        )
    ]
    for copy in copies:
        copy.start()
    trash = acc.shape[0] // 8 - 1
    acc[...] = jnp.zeros_like(acc)
    for copy in copies:
        copy.wait()
    keep = pltpu.make_async_copy(cols_ref.at[0:768], moved_ref, sem.at[4])
    keep.start()
    given, step, value = shares(wide)
    first = lists_ref[0]
    done = jnp.minimum(lists_ref[6 * 128 + 1], early)

    def turn_in(t, carry):
        for q in range(early_turn):
            k = t * early_turn + q
            live = k < done
            code = lists_ref[k]
            o = jnp.where(live, code & 511, trash)
            w = jnp.where(live, lax.shift_right_logical(code, 9), trash)
            acc[tile(o), :] += before[tile(2 * k), :]
            acc[tile(w), :] += before[tile(2 * k + 1), :]
        return step(carry)

    refs = (cols_ref, U, V, L, RT, extra, pieces, natural)
    given = build_tables(refs, first, given, turn_in)
    ahead_out = value(given[0], 0, 32)
    up_out = value(given[1], 0, 32)
    ahead_in = value(given[0], 0, 96)
    ahead_down = value(given[0], -1, 32)
    up_in = value(given[1], -1, 32)

    def begin(at, name):
        return lists_ref[at * 1024 + 6 * 128 + name]

    def cut(at, first, second):
        end = begin(at, 1)
        low = jnp.minimum(end, early)
        first = jnp.minimum(low + first, end)
        return low, first, jnp.minimum(first + second, end)

    _, _, kept = cut(0, ahead_out, up_out)
    ahead_low, ahead_high, _ = cut(3, ahead_in, 0)
    _, up_low, up_high = cut(2, ahead_down, up_in)
    ends = []
    shifts = []
    so_far = 0
    for at, low, high in (
        (0, kept, begin(0, 1)),
        (0, begin(0, 1), begin(0, 2)),
        (1, begin(1, 2), begin(1, 3)),
        (2, begin(2, 3), begin(2, 4)),
        (3, begin(3, 4), begin(3, 5)),
        (3, ahead_low, ahead_high),
        (2, up_low, up_high),
    ):
        shifts.append(at * 1024 + low - so_far)
        so_far = so_far + (high - low)
        ends.append(so_far)
    n = so_far
    last = jnp.maximum(n - 1, 0)

    def entry(k):
        k = jnp.minimum(k, last)
        shift = shifts[6]
        for at in range(5, -1, -1):
            shift = jnp.where(k < ends[at], shifts[at], shift)
        code = lists_ref[k + shift]
        code = code + jnp.where(
            k < ends[4], 0, jnp.where(k < ends[5], 96 + 512 * 288, 192 + 512 * 192)
        )
        return code & 511, lax.shift_right_logical(code, 9)

    def spot_u(u):
        return jnp.where(u < 192, u, u + 96)

    def spot(v):
        return jnp.where(v < 96, v, jnp.where(v < 288, v + 96, v - 192))

    distances, weights, both = pair_machine(entry, spot, spot_u, cols_ref, U, V, L, RT, AB, M)

    def sums(k, at):
        o, w, to_first, to_second = both(k, at)
        live = k < n
        o = jnp.where(live, o, trash)
        w = jnp.where(live, w, trash)
        acc[tile(o), :] += to_first
        acc[tile(w), :] += to_second

    for q in range(ring):
        distances(q, q)
    for q in range(lag_b):
        weights(q, q)

    def turn(t, carry):
        for q in range(group):
            k = t * group + q
            sums(k, q % ring)
            weights(k + lag_b, (q + lag_b) % ring)
            distances(k + ring, q % ring)
        return carry

    lax.fori_loop(0, lax.div(n + group - 1, group), turn, 0)

    def close(base, out_ref, out_base):
        got = [acc[rows_of(base, c), :] for c in range(6)]
        terms = []
        for c in range(3):
            hi, mid = split2(cols_ref[rows_of(base, c), :])
            terms.append(stiffness * ((hi + mid) * got[3] - got[c]))
        root = conductance * extra[rows_of(base, 5), :]
        terms.append(root * (got[4] - cols_ref[rows_of(base, 6), :] * got[5]))
        for c in range(4):
            out_ref[pl.ds(out_base + c, 8, 4), :] = terms[c]

    def close_all(t, carry):
        close(8 * t, own_ref, 32 * t)
        for side in range(3):
            close(96 * (side + 1) + 8 * t, sides_ref, 384 * side + 32 * t)
        return carry

    lax.fori_loop(0, 12, close_all, 0)
    keep.wait()


def finish_kernel(
    moved_hbm,
    sides_ref,
    flags_hbm,
    cells_hbm,
    table_hbm,
    mix_ref,
    fluid_ref,
    moved_ref,
    flags_ref,
    cells_ref,
    table_ref,
    in_sem,
    sums,
    send,
    recv,
):
    ahead, behind, up, down = neighbours()
    inputs = [
        pltpu.make_async_copy(source, target, in_sem.at[at])
        for at, (source, target) in enumerate(
            (
                (moved_hbm, moved_ref),
                (flags_hbm, flags_ref),
                (cells_hbm, cells_ref),
                (table_hbm, table_ref),
            )
        )
    ]
    for copy in inputs:
        copy.start()
    greet((ahead, behind, up, down))
    await_all((ahead, behind, up, down))
    copies = []
    span = sides_ref.shape[0] // 3
    blocks = span // 4
    for at, device in ((0, behind), (1, up), (2, down)):
        copy = pltpu.make_async_remote_copy(
            src_ref=sides_ref.at[span * at : span * at + span],
            dst_ref=mix_ref.at[span * at : span * at + span],
            send_sem=send.at[at],
            recv_sem=recv.at[at],
            device_id=device,
            device_id_type=MESH,
        )
        copy.start()
        copies.append(copy)

    for copy in inputs:
        copy.wait()
    square = jnp.concatenate([table_ref[:, 16 * a : 16 * a + 16] for a in range(16)], axis=0)
    table = jnp.concatenate(split3(square), axis=0).astype(bf16)
    sums[...] = jnp.zeros_like(sums)
    sub = iota((16, 128), 0)

    def cells_of(g, carry):
        at = pl.ds(pl.multiple_of(g * 8, 8), 8)
        temper = moved_ref[rows_of(g * 8, 6), :]
        radius = moved_ref[rows_of(g * 8, 7), :]
        volume = 4.0 / 3.0 * math.pi * radius * radius * radius
        cell = cells_ref[at, :]
        high = lax.shift_right_logical(cell, 4)
        low = cell & 15
        fluid = []
        hots = []
        for c in range(8):
            hot_high = (sub == high[c : c + 1]).astype(f32)
            hot_low = (sub == low[c : c + 1]).astype(f32)
            parts = jnp.dot(table, hot_low.astype(bf16), preferred_element_type=f32)
            value = parts[0:16] + parts[16:32] + parts[32:48]
            fluid.append(jnp.sum(value * hot_high, axis=0, keepdims=True))
            hots.append((hot_high, hot_low))
        flow = film_gain * radius * radius * (temper - jnp.concatenate(fluid, axis=0))
        pieces = split3(volume) + split3(flow)
        total = sums[...]
        for c in range(8):
            hot_high, hot_low = hots[c]
            spread = jnp.concatenate([hot_low * piece[c : c + 1] for piece in pieces], axis=0)
            total = total + dot_tt(hot_high.astype(bf16), spread.astype(bf16))
        sums[...] = total
        wall = wall_gain * flags_ref[at, :].astype(f32) * (wall_temp - temper) * radius
        mix_ref[pl.ds(pl.multiple_of(3 * span + g * 8, 8), 8), :] = wall - flow
        mix_ref[pl.ds(pl.multiple_of(3 * span + blocks + g * 8, 8), 8), :] = 1.0 / volume
        return carry

    lax.fori_loop(0, 12, cells_of, 0)
    total = sums[...]
    solid = (total[:, 0:16] + total[:, 16:32] + total[:, 32:48]) / cell_volume
    heat = total[:, 48:64] + total[:, 64:80] + total[:, 80:96]
    for a in range(16):
        fluid_ref[0:1, 16 * a : 16 * a + 16] = solid[a : a + 1]
        fluid_ref[1:2, 16 * a : 16 * a + 16] = heat[a : a + 1]
    for copy in copies:
        copy.wait()


def rates_kernel(
    own_hbm, mix_hbm, fluid_hbm, rates_ref, fluid_ref, own, mix, fluid, sem
):
    copies = [
        pltpu.make_async_copy(source, target, sem.at[at])
        for at, (source, target) in enumerate(
            ((mix_hbm, mix), (own_hbm, own), (fluid_hbm, fluid))
        )
    ]
    for copy in copies:
        copy.start()
    for copy in copies:
        copy.wait()
    fluid_ref[...] = fluid[...]
    span = own.shape[0]
    blocks = span // 4

    def combine(g, carry):
        at = pl.multiple_of(g * 8, 8)
        inverse = mix[pl.ds(3 * span + blocks + at, 8), :]
        for c in range(4):
            here = pl.ds(g * 32 + c, 8, 4)
            value = own[here, :]
            for side in range(3):
                value = value + mix[pl.ds(span * side + g * 32 + c, 8, 4), :]
            if c == 3:
                value = value + mix[pl.ds(3 * span + at, 8), :]
            value = value * inverse
            if c == 2:
                value = value - gravity
            rates_ref[here, :] = value
        return carry

    lax.fori_loop(0, blocks // 8, combine, 0, unroll=4)


def anywhere():
    return pl.BlockSpec(memory_space=pl.ANY)


def vmem():
    return pl.BlockSpec(memory_space=pltpu.VMEM)


def shards(state, leaving, pairs, counts, wall_flags, cell_index, fluid_temp):
    mine = state[0, 0]
    blocks = mine.shape[0]
    count = leaving.shape[2]
    lanes = -(-pairs.shape[3] // 128) * 128
    cols, lists, wide, ahead_of = pl.pallas_call(
        halo_kernel,
        out_shape=(
            jax.ShapeDtypeStruct((4, 8 * blocks, 128), f32),
            jax.ShapeDtypeStruct((4, 8, 128), i32),
            jax.ShapeDtypeStruct((16, 128), f32),
            jax.ShapeDtypeStruct((16 * early, 128), f32),
        ),
        in_specs=[anywhere()] * 4,
        out_specs=(anywhere(), vmem(), vmem(), vmem()),
        scratch_shapes=[
            pltpu.SMEM(leaving.shape[2:], i32),
            pltpu.SMEM(counts.shape[2:], i32),
            pltpu.VMEM(pairs.shape[2:], i32),
            pltpu.VMEM((8 * (count + blocks), 128), f32),
            pltpu.VMEM((8 * count, 128), f32),
            pltpu.VMEM((8 * blocks, 128), f32),
            pltpu.VMEM((8, lanes), i32),
            pltpu.VMEM((8, 128), i32),
            pltpu.SMEM((8, 128), i32),
            pltpu.SemaphoreType.DMA,
            pltpu.SemaphoreType.DMA,
            pltpu.SemaphoreType.DMA((3,)),
            pltpu.SemaphoreType.DMA((3,)),
            pltpu.SemaphoreType.DMA((3,)),
            pltpu.SemaphoreType.DMA((3,)),
            pltpu.SemaphoreType.DMA,
            pltpu.SemaphoreType.DMA((5,)),
            pltpu.VMEM((8, 128), f32),
            pltpu.SemaphoreType.DMA((3,)),
            pltpu.SemaphoreType.DMA((3,)),
            pltpu.SemaphoreType.DMA((2 * reach,)),
            pltpu.SemaphoreType.DMA((2 * reach,)),
            pltpu.VMEM((8, 128), i32),
            pltpu.SMEM((8, 128), i32),
            pltpu.VMEM((count + blocks, 128, 128), bf16),
            pltpu.VMEM((count + blocks, 32, 256), bf16),
            pltpu.VMEM((count + blocks, 16, 128), bf16),
            pltpu.VMEM(((count + blocks) // 8, 128, 128), f32),
            pltpu.VMEM((8 * (count + blocks), 128), f32),
            pltpu.VMEM((8 * (count + blocks), 128), f32),
            pltpu.VMEM((3, 256, 128), bf16),
        ]
        + [pltpu.VMEM((128, 256), f32)] * ring
        + [pltpu.VMEM((256, 256), bf16)] * ring,
        compiler_params=pltpu.CompilerParams(
            collective_id=0, has_side_effects=True, vmem_limit_bytes=vmem_grant
        ),
        name="halo",
    )(leaving[0, 0], counts[0, 0], pairs[0, 0], mine.reshape(8 * blocks, 128))

    moved, own, sides = pl.pallas_call(
        pair_kernel,
        out_shape=(
            jax.ShapeDtypeStruct((8 * blocks, 128), f32),
            jax.ShapeDtypeStruct((4 * blocks, 128), f32),
            jax.ShapeDtypeStruct((12 * blocks, 128), f32),
        ),
        in_specs=[anywhere()] * 4,
        out_specs=(anywhere(), vmem(), vmem()),
        scratch_shapes=[
            pltpu.SMEM((4096,), i32),
            pltpu.VMEM((32 * blocks, 128), f32),
            pltpu.VMEM((16, 128), f32),
            pltpu.VMEM((3 * blocks, 128, 128), bf16),
            pltpu.VMEM((4 * blocks, 32, 256), bf16),
            pltpu.VMEM((4 * blocks, 16, 128), bf16),
            pltpu.VMEM((3 * blocks // 8, 128, 128), f32),
            pltpu.VMEM((32 * blocks, 128), f32),
            pltpu.VMEM((32 * blocks, 128), f32),
            pltpu.VMEM((3, 256, 128), bf16),
            pltpu.VMEM((32 * blocks + 8, 128), f32),
            pltpu.VMEM((16 * early_turn * blocks // 8, 128), f32),
            pltpu.SemaphoreType.DMA((5,)),
        ]
        + [pltpu.VMEM((128, 256), f32)] * ring
        + [pltpu.VMEM((256, 256), bf16)] * ring,
        compiler_params=pltpu.CompilerParams(vmem_limit_bytes=vmem_grant),
        name="contact",
    )(lists.reshape(4096), cols.reshape(32 * blocks, 128), wide, ahead_of)

    mix, fluid = pl.pallas_call(
        finish_kernel,
        out_shape=(
            jax.ShapeDtypeStruct((14 * blocks, 128), f32),
            jax.ShapeDtypeStruct((2, 256), f32),
        ),
        in_specs=[anywhere()] * 5,
        out_specs=(vmem(), vmem()),
        scratch_shapes=[
            pltpu.VMEM((8 * blocks, 128), f32),
            pltpu.VMEM((blocks, 128), i32),
            pltpu.VMEM((blocks, 128), i32),
            pltpu.VMEM((1, 256), f32),
            pltpu.SemaphoreType.DMA((4,)),
            pltpu.VMEM((16, 96), f32),
            pltpu.SemaphoreType.DMA((3,)),
            pltpu.SemaphoreType.DMA((3,)),
        ],
        compiler_params=pltpu.CompilerParams(
            collective_id=1, has_side_effects=True, vmem_limit_bytes=vmem_grant
        ),
        name="finish",
    )(moved, sides, wall_flags[0, 0], cell_index[0, 0], fluid_temp.reshape(1, 256))

    rates, fluid = pl.pallas_call(
        rates_kernel,
        out_shape=(
            jax.ShapeDtypeStruct((4 * blocks, 128), f32),
            jax.ShapeDtypeStruct((2, 256), f32),
        ),
        in_specs=[anywhere()] * 3,
        out_specs=(vmem(), vmem()),
        scratch_shapes=[
            pltpu.VMEM((4 * blocks, 128), f32),
            pltpu.VMEM((14 * blocks, 128), f32),
            pltpu.VMEM((2, 256), f32),
            pltpu.SemaphoreType.DMA((3,)),
        ],
        compiler_params=pltpu.CompilerParams(vmem_limit_bytes=vmem_grant),
        name="rates",
    )(own, mix, fluid)
    return (
        moved.reshape(1, 1, blocks, 8, 128),
        rates.reshape(1, 1, blocks, 4, 128),
        fluid[None, None],
    )


def solution(mesh):
    in_specs = (
        P("gx", "gy", None, None, None),
        P("gx", "gy", None),
        P("gx", "gy", None, None),
        P("gx", "gy", None),
        P("gx", "gy", None, None),
        P("gx", "gy", None, None),
        P("gx", "gy", None),
    )
    out_specs = (
        P("gx", "gy", None, None, None),
        P("gx", "gy", None, None, None),
        P("gx", "gy", None, None),
    )
    return jax.shard_map(shards, mesh=mesh, in_specs=in_specs, out_specs=out_specs, check_vma=False)
```

```python
import functools
import math

import jax
import jax.numpy as jnp
from jax import lax
from jax.experimental import pallas as pl
from jax.experimental.pallas import tpu as pltpu
from jax.sharding import PartitionSpec as P

soften = 0.01
stiffness = 0.2
damping = 0.05
conductance = 0.05
film_gain = 0.5
wall_gain = 2.0
wall_temp = 1.0
gravity = 1.0
cell_volume = 32.0

f32 = jnp.float32
bf16 = jnp.bfloat16
i32 = jnp.int32

tiny = 1e-30
group = 16
lag_a = 2
lag_b = 2
ring = lag_a + lag_b
reach = 4
lateness = (50.0, 28.0, 22.0, 125.0, 20.0, 0.0, 0.0, 0.0, 0.0, 0.0, 0.0, 0.0, 85.0, 0.0, 0.0, 35.0)
early = 64
early_turn = 6
vmem_grant = 56 * 2**20
MESH = pl.DeviceIdType.MESH


def iota(shape, dim):
    return lax.broadcasted_iota(i32, shape, dim)


def split2(value):
    hi = value.astype(bf16).astype(f32)
    return hi, (value - hi).astype(bf16).astype(f32)


def split3(value):
    hi = value.astype(bf16).astype(f32)
    rest = value - hi
    mid = rest.astype(bf16).astype(f32)
    return hi, mid, rest - mid


def dot_tt(left, right):
    return lax.dot_general(left, right, (((1,), (1,)), ((), ())), preferred_element_type=f32)


def neighbours():
    a = lax.axis_index("gx")
    b = lax.axis_index("gy")
    na = lax.axis_size("gx")
    nb = lax.axis_size("gy")
    return (
        {"gx": lax.rem(a + 1, na)},
        {"gx": lax.rem(a + na - 1, na)},
        {"gy": lax.rem(b + 1, nb)},
        {"gy": lax.rem(b + nb - 1, nb)},
    )


def greet(everyone):
    barrier = pltpu.get_barrier_semaphore()
    for device in everyone:
        pl.semaphore_signal(barrier, inc=1, device_id=device, device_id_type=MESH)


def await_all(everyone):
    pl.semaphore_wait(pltpu.get_barrier_semaphore(), len(everyone))


def sort_pairs(lanes, pad, total):
    own = pad[0:1, :]
    code = pad[1:2, :]
    region = jnp.zeros_like(code)
    for step in range(1, 9):
        region = region + (code >= 96 * step).astype(i32)
    far = code - 96 * region
    live = iota((1, lanes), 1) < total

    def among(*names):
        hit = region == names[0]
        for name in names[1:]:
            hit = hit | (region == name)
        return hit

    kind = jnp.where(
        among(4),
        0,
        jnp.where(among(1, 5), 1, jnp.where(among(0, 3), 2, jnp.where(among(2), 3, 4))),
    )
    kind = jnp.where(live, kind, 5)
    u_far = among(0, 1, 2, 3)
    u = jnp.where(u_far, far, own) + jnp.where(among(4, 5, 3), 0, 96)
    v_slot = jnp.where(u_far, own, far)
    v_side = jnp.where(among(4, 1, 7), 0, jnp.where(among(5, 3, 0, 8), 1, 2))
    ranks = iota((8, lanes), 0)
    marks = (ranks == kind).astype(f32)
    before = (iota((lanes, lanes), 0) < iota((lanes, lanes), 1)).astype(bf16)
    seen = jnp.dot(marks.astype(bf16), before, preferred_element_type=f32)
    starts = jnp.sum((kind < ranks).astype(f32), axis=1, keepdims=True)
    place = jnp.sum(marks * (seen + starts), axis=0, keepdims=True)
    target = (iota((lanes, lanes), 0).astype(f32) == place).astype(bf16)
    rows = iota((8, lanes), 0)
    values = jnp.where(
        rows == 0, u, jnp.where(rows == 1, v_slot, jnp.where(rows == 2, v_side, 0))
    )
    moved = dot_tt(values.astype(bf16), target)
    packed = moved[0:1] + 512.0 * (moved[1:2] + 96.0 * moved[2:3])
    diag = iota((8, 128), 0) == iota((8, 128), 1)
    begin = jnp.sum(jnp.where(diag, starts, 0.0), axis=0, keepdims=True)
    return packed.astype(i32), begin.astype(i32)


def own_pairs(list_smem, refs, rings, early_ref):
    cols_ref, U, V, L, RT = refs[0:5]
    AB = rings[0:ring]
    M = rings[ring : 2 * ring]
    last = U.shape[0] - 1

    def entry(k):
        k = jnp.minimum(k, early - 1)
        code = list_smem[lax.shift_right_logical(k, 7), k & 127]
        u = jnp.minimum(code & 511, last)
        return u, jnp.minimum(lax.shift_right_logical(code, 9), last)

    def same(block):
        return block

    distances, weights, both = pair_machine(entry, same, same, cols_ref, U, V, L, RT, AB, M)
    for q in range(ring):
        distances(q, q)
    for q in range(lag_b):
        weights(q, q)

    def turn(t, carry):
        for q in range(group):
            k = t * group + q
            _, _, to_first, to_second = both(k, q % ring)
            early_ref[tile(2 * k), :] = to_first
            early_ref[tile(2 * k + 1), :] = to_second
            weights(k + lag_b, (q + lag_b) % ring)
            distances(k + ring, q % ring)
        return carry

    lax.fori_loop(0, early // group, turn, 0)


def halo_kernel(
    leaving_hbm,
    counts_hbm,
    pairs_hbm,
    state_hbm,
    cols_ref,
    lists_ref,
    wide_ref,
    early_ref,
    leaving_ref,
    counts_ref,
    pairs_ref,
    cat,
    dep,
    moved,
    pad,
    slot_vec,
    slot_smem,
    dep_send,
    dep_recv,
    list_send,
    list_recv,
    col_send,
    col_recv,
    local_sem,
    in_sem,
    near,
    near_send,
    near_recv,
    wide_send,
    wide_recv,
    list_vec,
    list_smem,
    U,
    V,
    L,
    RT,
    extra,
    pieces,
    natural,
    *rings,
):
    blocks = state_hbm.shape[0] // 8
    count = leaving_hbm.shape[0]
    ahead, behind, up, down = neighbours()
    a = lax.axis_index("gx")
    na = lax.axis_size("gx")
    along = {
        step: {"gx": lax.rem(a + step + na, na)} for step in range(-reach, reach + 1) if step
    }
    b = lax.axis_index("gy")
    nb = lax.axis_size("gy")
    across = {"gy": lax.rem(b + 2, nb)}
    everyone = (up, down, across, *along.values())
    state_ref = cat.at[8 * count : 8 * count + 8 * blocks]
    inputs = [
        pltpu.make_async_copy(source, target, in_sem.at[at])
        for at, (source, target) in enumerate(
            (
                (leaving_hbm, leaving_ref),
                (state_hbm, state_ref),
                (pairs_hbm, pairs_ref),
                (counts_hbm, counts_ref),
                (state_hbm, moved),
            )
        )
    ]
    for copy in inputs:
        copy.start()
    wide_ref[...] = jnp.zeros_like(wide_ref)
    greet(everyone)
    for at in (0, 3, 4):
        inputs[at].wait()
    local = jnp.maximum(counts_ref[0] - early, 0).astype(f32)
    far = (counts_ref[1] - counts_ref[0]).astype(f32) * 0.125
    lane = iota((1, 128), 1)
    near[0:1, :] = jnp.where(lane < 64, far, local)
    for m in range(count):
        dep[8 * m : 8 * m + 8, :] = moved[pl.ds(leaving_ref[m] * 8, 8), :]
    await_all(everyone)
    asks = []
    for at, device in ((1, down), (2, up), (3, across)):
        copy = pltpu.make_async_remote_copy(
            src_ref=near.at[0:1],
            dst_ref=near.at[at : at + 1],
            send_sem=near_send.at[at - 1],
            recv_sem=near_recv.at[at - 1],
            device_id=device,
            device_id_type=MESH,
        )
        copy.start()
        asks.append(copy)
    depart = pltpu.make_async_remote_copy(
        src_ref=dep,
        dst_ref=cat.at[0 : 8 * count],
        send_sem=dep_send,
        recv_sem=dep_recv,
        device_id=ahead,
        device_id_type=MESH,
    )
    depart.start()
    inputs[1].wait()
    inputs[2].wait()
    place = iota((8, 128), 1)
    slot = place + count
    for m in range(count):
        slot = jnp.where(place == leaving_ref[m], m, slot)
    slot_vec[...] = slot
    to_smem = pltpu.make_async_copy(slot_vec, slot_smem, local_sem)
    to_smem.start()
    lanes = pad.shape[1]
    pad[...] = jnp.zeros_like(pad)
    pad[0:2, 0 : pairs_ref.shape[1]] = pairs_ref[...]
    packed, begin = sort_pairs(lanes, pad, counts_ref[1])
    lists_ref[0] = jnp.zeros((8, 128), i32)
    for row in range(lanes // 128):
        lists_ref[0, row : row + 1, :] = packed[:, 128 * row : 128 * row + 128]
    lists_ref[0, 6:7, :] = begin
    copies = []
    for copy in asks:
        copy.wait()
    turn = lane & 3
    row = near[0:1, :]
    for at, step in ((1, 1), (2, nb - 1), (3, 2)):
        row = jnp.where(turn == lax.rem(b + step, nb), near[at : at + 1, :], row)
    wide_ref[reach : reach + 1, :] = row
    for at, step in enumerate(along):
        copy = pltpu.make_async_remote_copy(
            src_ref=wide_ref.at[reach : reach + 1],
            dst_ref=wide_ref.at[reach - step : reach - step + 1],
            send_sem=wide_send.at[at],
            recv_sem=wide_recv.at[at],
            device_id=along[step],
            device_id_type=MESH,
        )
        copy.start()
        copies.append(copy)
    for at, device in ((1, down), (2, up), (3, ahead)):
        copy = pltpu.make_async_remote_copy(
            src_ref=lists_ref.at[0],
            dst_ref=lists_ref.at[at],
            send_sem=list_send.at[at - 1],
            recv_sem=list_recv.at[at - 1],
            device_id=device,
            device_id_type=MESH,
        )
        copy.start()
        copies.append(copy)
    to_smem.wait()
    refs = (cat, U, V, L, RT, extra, pieces, natural)
    raw = count // 8
    depart.wait()

    def place_block(j, carry):
        moved[tile(j), :] = cat[pl.ds(slot_smem[0, j] * 8, 8), :]
        return carry

    lax.fori_loop(0, blocks, place_block, 0)
    keep = pltpu.make_async_copy(moved, cols_ref.at[0], local_sem)
    keep.start()
    for at, device in ((1, ahead), (2, down), (3, up)):
        copy = pltpu.make_async_remote_copy(
            src_ref=moved,
            dst_ref=cols_ref.at[at],
            send_sem=col_send.at[at - 1],
            recv_sem=col_recv.at[at - 1],
            device_id=device,
            device_id_type=MESH,
        )
        copy.start()
        copies.append(copy)
    codes = lists_ref[0]
    u = jnp.take_along_axis(slot, jnp.minimum(codes & 511, 95), axis=1)
    v = jnp.take_along_axis(
        slot, jnp.minimum(lax.shift_right_logical(codes, 9), 95), axis=1
    )
    list_vec[...] = u + 512 * v
    own_list = pltpu.make_async_copy(list_vec, list_smem, in_sem.at[0])
    own_list.start()
    build_groups(refs, raw, raw + blocks // 8, 2)
    build_groups(refs, 0, raw, 3)
    own_list.wait()
    own_pairs(list_smem, refs, rings, early_ref)
    keep.wait()
    for copy in copies:
        copy.wait()


def rows_of(base, c):
    return pl.ds(base * 8 + c, 8, 8)


def tile(i):
    return pl.ds(pl.multiple_of(i * 8, 8), 8)


def table_steps(cols_ref, U, V, L, RT, extra, pieces, natural, never):
    rows = iota((8, 128), 0)
    eye = (iota((128, 128), 0) == iota((128, 128), 1)).astype(bf16)
    eyes = jnp.concatenate([eye, eye, eye], axis=1)
    c6 = jnp.where(rows == 6, 1.0, 0.0)
    c7 = jnp.where(rows == 7, 0.25, 0.0)
    ca = jnp.where(rows < 3, -2.0, 0.0)
    cb = jnp.where(rows < 6, -0.25, 0.0)
    ones = jnp.where(rows < 6, 1.0, 0.0)

    def dense(base):
        x = [cols_ref[rows_of(base, c), :] for c in range(3)]
        v = [cols_ref[rows_of(base, c), :] for c in range(3, 6)]
        radius = cols_ref[rows_of(base, 7), :]
        root = jnp.sqrt(radius)
        square = x[0] * x[0] + x[1] * x[1] + x[2] * x[2] + 0.5 * soften
        dot = x[0] * v[0] + x[1] * v[1] + x[2] * v[2]
        extra[rows_of(base, 3), :] = jnp.ones((8, 128), f32)
        extra[rows_of(base, 4), :] = root * cols_ref[rows_of(base, 6), :]
        extra[rows_of(base, 5), :] = root
        extra[rows_of(base, 6), :] = square
        extra[rows_of(base, 7), :] = dot
        for c, piece in enumerate(split3(square) + split3(0.25 * dot)):
            pieces[rows_of(base, c), :] = piece

    def swap(value):
        return jnp.where(rows < 3, pltpu.roll(value, 5, 0), pltpu.roll(value, 3, 0))

    def eight(base, shift, at, held=None):
        for q in range(8):
            i = base + q
            S = cols_ref[tile(i), :]
            if held is not None:
                S = jnp.where(never, held, S)
            E = extra[tile(i), :]
            G = pieces[tile(i), :]
            hi, mid = split2(jnp.where(rows < 3, S, jnp.where(rows < 6, E, 0.0)))
            L[i] = jnp.concatenate([hi, mid], axis=0).astype(bf16)
            full = jnp.where(rows < 6, S, E)
            hi, mid = split2(full)
            if at is not None:
                low = jnp.where(rows < 6, hi, full - hi - mid)
                natural[at, 32 * q : 32 * q + 32, :] = jnp.concatenate(
                    [hi, low, mid, ones], axis=0
                ).astype(bf16)
            a0 = hi * ca + c6
            a1 = mid * ca + c6
            b0 = swap(hi) * cb + c7
            b1 = swap(mid) * cb + c7
            A = jnp.concatenate([a0, a1, a0, jnp.where(rows < 3, G, 0.0)], axis=0)
            B = jnp.concatenate(
                [b0, b1, b0, jnp.where((rows >= 3) & (rows < 6), G, 0.0)], axis=0
            )
            V[i + shift, :, 0:128] = A.astype(bf16)
            V[i + shift, :, 128:256] = B.astype(bf16)

    def turn(at, u_base):
        turned = dot_tt(eye, natural[at]).astype(bf16)
        for q in range(8):
            U[u_base + q, :, 0:32] = turned[:, 32 * q : 32 * q + 32]

    def column(base, u_base):
        radius = cols_ref[rows_of(base, 7), :]
        three = jnp.concatenate(split3(radius), axis=1).astype(bf16)
        RT[lax.shift_right_logical(u_base, 3), :, 0:8] = dot_tt(eyes, three)

    return dense, eight, turn, column


def build_tables(refs, first, start, step):
    dense, eight, turn, column = table_steps(*refs, first < 0)
    cols_ref, U = refs[0:2]

    def turns(t):
        turn(0, 8 * t)
        turn(1, 96 + 8 * t)
        turn(2, 192 + 8 * t)
        column(8 * t, 8 * t)
        column(96 + 8 * t, 96 + 8 * t)
        column(288 + 8 * t, 192 + 8 * t)

    def body(t, carry):
        turns(jnp.maximum(t - 1, 0))
        for col in range(4):
            dense(96 * col + 8 * t)
        eight(8 * t, 0, 0)
        eight(96 + 8 * t, 192, 1)
        eight(288 + 8 * t, -96, 2)
        held = U[first & 63, 0:16, :].astype(f32)[0:8]
        eight(192 + 8 * t, -96, None, held)
        return step(t, carry)

    count = cols_ref.shape[0] // 256
    carry = lax.fori_loop(0, count, body, start)
    turns(count - 1)
    return carry


def build_groups(refs, low, high, step):
    dense, eight, turn, column = table_steps(*refs, None)

    def body(t, carry):
        bases = [8 * (t * step + low + q) for q in range(step)]
        for base in bases:
            dense(base)
        for at, base in enumerate(bases):
            eight(base, 0, at)
        for at, base in enumerate(bases):
            turn(at, base)
        for base in bases:
            column(base, base)
        return carry

    lax.fori_loop(0, (high - low) // step, body, 0)


def shares(wide):
    rows = iota((8, 128), 0)
    lanes = iota((8, 128), 1)
    b = lax.axis_index("gy")
    nb = lax.axis_size("gy")
    own = wide[1:9, :]
    behind = wide[0:8, :]
    far = jnp.where(lanes < 64, own, pltpu.roll(behind, 64, 1))
    local = jnp.where(lanes < 64, pltpu.roll(own, 64, 1), behind)
    load = (
        local
        + 2.0 * far
        + 2.0 * pltpu.roll(far, 127, 1)
        + pltpu.roll(far, 1, 1)
        + 3.0 * jnp.where(rows == 0, far, pltpu.roll(far, 1, 0))
    )
    column = lax.axis_index("gx") + rows - (reach - 1) - jnp.where(lanes < 64, 0, 1)
    phase = (column + 32) & 15
    for at, late in enumerate(lateness):
        load = load + jnp.where(phase == at, late, 0.0)
    passing = jnp.where(rows < 7, local, 0.0)

    def step(given):
        ahead, up = given
        now = load - ahead - up + pltpu.roll(ahead, 1, 0) + pltpu.roll(up, 1, 1)
        ahead = ahead + 0.26 * (now - pltpu.roll(now, 7, 0))
        ahead = jnp.minimum(jnp.maximum(ahead, 0.0), jnp.maximum(passing - up, 0.0))
        up = up + 0.26 * (now - pltpu.roll(now, 127, 1))
        up = jnp.minimum(jnp.maximum(up, 0.0), jnp.maximum(local - ahead, 0.0))
        return ahead, up

    def value(given, shift, base):
        column = lax.rem(b + shift + nb, nb)
        picked = (rows == reach - 1) & (lanes == column + base)
        return jnp.sum(jnp.where(picked, given, 0.0)).astype(i32)

    start = jnp.zeros((8, 128), f32)
    return (start, start), step, value


def pair_machine(entry, spot, spot_u, cols_ref, U, V, L, RT, AB, M):
    def distances(k, at):
        u, v = entry(k)
        AB[at][...] = jnp.dot(U[u, :, 0:32], V[v], preferred_element_type=f32)

    def weights(k, at):
        u, v = entry(k)
        rt = cols_ref[pl.ds(spot(v) * 8 + 7, 1), :]
        lane = jnp.full((8, 128), u & 7, i32)
        eighth = lax.shift_right_logical(u, 3)

        def radius(r):
            return jnp.take_along_axis(RT[eighth, r : r + 8, :], lane, axis=1)

        for r in range(0, 128, 16):
            A = AB[at][r : r + 16, 0:128]
            B = AB[at][r : r + 16, 128:256]
            R = jnp.concatenate([radius(r), radius(r + 8)], axis=0) + rt
            inv = lax.rsqrt(A)
            gap = R - A * inv
            inter = jnp.maximum(gap, 0.0)
            root = inter * lax.rsqrt(jnp.maximum(gap, tiny))
            W = (root * inv) * (inter - B * inv)
            G = root * lax.rsqrt(R)
            wh = W.astype(bf16)
            gh = G.astype(bf16)
            M[at][r : r + 16, 0:128] = wh
            M[at][r : r + 16, 128:256] = gh
            M[at][128 + r : 144 + r, 0:128] = (W - wh.astype(f32)).astype(bf16)
            M[at][128 + r : 144 + r, 128:256] = (G - gh.astype(f32)).astype(bf16)

    rows = iota((8, 128), 0)

    def folded(out):
        both = out[0:8] + out[8:16]
        return jnp.where(rows < 4, both[:, 0:128], both[:, 128:256])

    def both(k, at):
        u, v = entry(k)
        w = spot(v)
        o = spot_u(u)
        first = jnp.concatenate([L[o], L[o]], axis=1)
        second = jnp.concatenate([L[w], L[w]], axis=1)
        m = M[at]
        crossed = jnp.concatenate(
            [
                jnp.concatenate([m[0:128, 0:128], m[128:256, 0:128]], axis=1),
                jnp.concatenate([m[0:128, 128:256], m[128:256, 128:256]], axis=1),
            ],
            axis=0,
        )
        to_second = folded(jnp.dot(first, m[...], preferred_element_type=f32))
        to_first = folded(dot_tt(second, crossed))
        return o, w, to_first, to_second

    return distances, weights, both


def pair_kernel(
    lists_hbm,
    cols_hbm,
    wide_hbm,
    early_hbm,
    moved_ref,
    own_ref,
    sides_ref,
    lists_ref,
    cols_ref,
    wide,
    U,
    V,
    L,
    RT,
    extra,
    pieces,
    natural,
    acc,
    before,
    sem,
    *rings,
):
    AB = rings[0:ring]
    M = rings[ring : 2 * ring]
    copies = [
        pltpu.make_async_copy(source, target, sem.at[at])
        for at, (source, target) in enumerate(
            (
                (cols_hbm, cols_ref),
                (lists_hbm, lists_ref),
                (wide_hbm, wide),
                (early_hbm, before.at[0 : 16 * early]),
            )
        )
    ]
    for copy in copies:
        copy.start()
    trash = acc.shape[0] // 8 - 1
    acc[...] = jnp.zeros_like(acc)
    for copy in copies:
        copy.wait()
    keep = pltpu.make_async_copy(cols_ref.at[0:768], moved_ref, sem.at[4])
    keep.start()
    given, step, value = shares(wide)
    first = lists_ref[0]
    done = jnp.minimum(lists_ref[6 * 128 + 1], early)

    def turn_in(t, carry):
        for q in range(early_turn):
            k = t * early_turn + q
            live = k < done
            code = lists_ref[k]
            o = jnp.where(live, code & 511, trash)
            w = jnp.where(live, lax.shift_right_logical(code, 9), trash)
            acc[tile(o), :] += before[tile(2 * k), :]
            acc[tile(w), :] += before[tile(2 * k + 1), :]
        return step(carry)

    refs = (cols_ref, U, V, L, RT, extra, pieces, natural)
    given = build_tables(refs, first, given, turn_in)
    ahead_out = value(given[0], 0, 32)
    up_out = value(given[1], 0, 32)
    ahead_in = value(given[0], 0, 96)
    ahead_down = value(given[0], -1, 32)
    up_in = value(given[1], -1, 32)

    def begin(at, name):
        return lists_ref[at * 1024 + 6 * 128 + name]

    def cut(at, first, second):
        end = begin(at, 1)
        low = jnp.minimum(end, early)
        first = jnp.minimum(low + first, end)
        return low, first, jnp.minimum(first + second, end)

    _, _, kept = cut(0, ahead_out, up_out)
    ahead_low, ahead_high, _ = cut(3, ahead_in, 0)
    _, up_low, up_high = cut(2, ahead_down, up_in)
    ends = []
    shifts = []
    so_far = 0
    for at, low, high in (
        (0, kept, begin(0, 1)),
        (0, begin(0, 1), begin(0, 2)),
        (1, begin(1, 2), begin(1, 3)),
        (2, begin(2, 3), begin(2, 4)),
        (3, begin(3, 4), begin(3, 5)),
        (3, ahead_low, ahead_high),
        (2, up_low, up_high),
    ):
        shifts.append(at * 1024 + low - so_far)
        so_far = so_far + (high - low)
        ends.append(so_far)
    n = so_far
    last = jnp.maximum(n - 1, 0)

    def entry(k):
        k = jnp.minimum(k, last)
        shift = shifts[6]
        for at in range(5, -1, -1):
            shift = jnp.where(k < ends[at], shifts[at], shift)
        code = lists_ref[k + shift]
        code = code + jnp.where(
            k < ends[4], 0, jnp.where(k < ends[5], 96 + 512 * 288, 192 + 512 * 192)
        )
        return code & 511, lax.shift_right_logical(code, 9)

    def spot_u(u):
        return jnp.where(u < 192, u, u + 96)

    def spot(v):
        return jnp.where(v < 96, v, jnp.where(v < 288, v + 96, v - 192))

    distances, weights, both = pair_machine(entry, spot, spot_u, cols_ref, U, V, L, RT, AB, M)

    def sums(k, at):
        o, w, to_first, to_second = both(k, at)
        live = k < n
        o = jnp.where(live, o, trash)
        w = jnp.where(live, w, trash)
        acc[tile(o), :] += to_first
        acc[tile(w), :] += to_second

    for q in range(ring):
        distances(q, q)
    for q in range(lag_b):
        weights(q, q)

    def turn(t, carry):
        for q in range(group):
            k = t * group + q
            sums(k, q % ring)
            weights(k + lag_b, (q + lag_b) % ring)
            distances(k + ring, q % ring)
        return carry

    lax.fori_loop(0, lax.div(n + group - 1, group), turn, 0)

    def close(base, out_ref, out_base):
        got = [acc[rows_of(base, c), :] for c in range(6)]
        terms = []
        for c in range(3):
            hi, mid = split2(cols_ref[rows_of(base, c), :])
            terms.append(stiffness * ((hi + mid) * got[3] - got[c]))
        root = conductance * extra[rows_of(base, 5), :]
        terms.append(root * (got[4] - cols_ref[rows_of(base, 6), :] * got[5]))
        for c in range(4):
            out_ref[pl.ds(out_base + c, 8, 4), :] = terms[c]

    def close_all(t, carry):
        close(8 * t, own_ref, 32 * t)
        for side in range(3):
            close(96 * (side + 1) + 8 * t, sides_ref, 384 * side + 32 * t)
        return carry

    lax.fori_loop(0, 12, close_all, 0)
    keep.wait()


def finish_kernel(
    moved_hbm,
    sides_ref,
    flags_hbm,
    cells_hbm,
    table_hbm,
    mix_ref,
    fluid_ref,
    moved_ref,
    flags_ref,
    cells_ref,
    table_ref,
    in_sem,
    sums,
    send,
    recv,
):
    ahead, behind, up, down = neighbours()
    inputs = [
        pltpu.make_async_copy(source, target, in_sem.at[at])
        for at, (source, target) in enumerate(
            (
                (moved_hbm, moved_ref),
                (flags_hbm, flags_ref),
                (cells_hbm, cells_ref),
                (table_hbm, table_ref),
            )
        )
    ]
    for copy in inputs:
        copy.start()
    greet((ahead, behind, up, down))
    await_all((ahead, behind, up, down))
    copies = []
    span = sides_ref.shape[0] // 3
    blocks = span // 4
    for at, device in ((0, behind), (1, up), (2, down)):
        copy = pltpu.make_async_remote_copy(
            src_ref=sides_ref.at[span * at : span * at + span],
            dst_ref=mix_ref.at[span * at : span * at + span],
            send_sem=send.at[at],
            recv_sem=recv.at[at],
            device_id=device,
            device_id_type=MESH,
        )
        copy.start()
        copies.append(copy)

    for copy in inputs:
        copy.wait()
    square = jnp.concatenate([table_ref[:, 16 * a : 16 * a + 16] for a in range(16)], axis=0)
    table = jnp.concatenate(split3(square), axis=0).astype(bf16)
    sums[...] = jnp.zeros_like(sums)
    sub = iota((16, 128), 0)

    def cells_of(g, carry):
        at = pl.ds(pl.multiple_of(g * 8, 8), 8)
        temper = moved_ref[rows_of(g * 8, 6), :]
        radius = moved_ref[rows_of(g * 8, 7), :]
        volume = 4.0 / 3.0 * math.pi * radius * radius * radius
        cell = cells_ref[at, :]
        high = lax.shift_right_logical(cell, 4)
        low = cell & 15
        fluid = []
        hots = []
        for c in range(8):
            hot_high = (sub == high[c : c + 1]).astype(f32)
            hot_low = (sub == low[c : c + 1]).astype(f32)
            parts = jnp.dot(table, hot_low.astype(bf16), preferred_element_type=f32)
            value = parts[0:16] + parts[16:32] + parts[32:48]
            fluid.append(jnp.sum(value * hot_high, axis=0, keepdims=True))
            hots.append((hot_high, hot_low))
        flow = film_gain * radius * radius * (temper - jnp.concatenate(fluid, axis=0))
        pieces = split3(volume) + split3(flow)
        total = sums[...]
        for c in range(8):
            hot_high, hot_low = hots[c]
            spread = jnp.concatenate([hot_low * piece[c : c + 1] for piece in pieces], axis=0)
            total = total + dot_tt(hot_high.astype(bf16), spread.astype(bf16))
        sums[...] = total
        wall = wall_gain * flags_ref[at, :].astype(f32) * (wall_temp - temper) * radius
        mix_ref[pl.ds(pl.multiple_of(3 * span + g * 8, 8), 8), :] = wall - flow
        mix_ref[pl.ds(pl.multiple_of(3 * span + blocks + g * 8, 8), 8), :] = 1.0 / volume
        return carry

    lax.fori_loop(0, 12, cells_of, 0)
    total = sums[...]
    solid = (total[:, 0:16] + total[:, 16:32] + total[:, 32:48]) / cell_volume
    heat = total[:, 48:64] + total[:, 64:80] + total[:, 80:96]
    for a in range(16):
        fluid_ref[0:1, 16 * a : 16 * a + 16] = solid[a : a + 1]
        fluid_ref[1:2, 16 * a : 16 * a + 16] = heat[a : a + 1]
    for copy in copies:
        copy.wait()


def rates_kernel(
    own_hbm, mix_hbm, fluid_hbm, rates_ref, fluid_ref, own, mix, fluid, sem
):
    copies = [
        pltpu.make_async_copy(source, target, sem.at[at])
        for at, (source, target) in enumerate(
            ((mix_hbm, mix), (own_hbm, own), (fluid_hbm, fluid))
        )
    ]
    for copy in copies:
        copy.start()
    for copy in copies:
        copy.wait()
    fluid_ref[...] = fluid[...]
    span = own.shape[0]
    blocks = span // 4

    def combine(g, carry):
        at = pl.multiple_of(g * 8, 8)
        inverse = mix[pl.ds(3 * span + blocks + at, 8), :]
        for c in range(4):
            here = pl.ds(g * 32 + c, 8, 4)
            value = own[here, :]
            for side in range(3):
                value = value + mix[pl.ds(span * side + g * 32 + c, 8, 4), :]
            if c == 3:
                value = value + mix[pl.ds(3 * span + at, 8), :]
            value = value * inverse
            if c == 2:
                value = value - gravity
            rates_ref[here, :] = value
        return carry

    lax.fori_loop(0, blocks // 8, combine, 0, unroll=4)


def anywhere():
    return pl.BlockSpec(memory_space=pl.ANY)


def vmem():
    return pl.BlockSpec(memory_space=pltpu.VMEM)


def shards(state, leaving, pairs, counts, wall_flags, cell_index, fluid_temp):
    mine = state[0, 0]
    blocks = mine.shape[0]
    count = leaving.shape[2]
    lanes = -(-pairs.shape[3] // 128) * 128
    cols, lists, wide, ahead_of = pl.pallas_call(
        halo_kernel,
        out_shape=(
            jax.ShapeDtypeStruct((4, 8 * blocks, 128), f32),
            jax.ShapeDtypeStruct((4, 8, 128), i32),
            jax.ShapeDtypeStruct((16, 128), f32),
            jax.ShapeDtypeStruct((16 * early, 128), f32),
        ),
        in_specs=[anywhere()] * 4,
        out_specs=(anywhere(), vmem(), vmem(), vmem()),
        scratch_shapes=[
            pltpu.SMEM(leaving.shape[2:], i32),
            pltpu.SMEM(counts.shape[2:], i32),
            pltpu.VMEM(pairs.shape[2:], i32),
            pltpu.VMEM((8 * (count + blocks), 128), f32),
            pltpu.VMEM((8 * count, 128), f32),
            pltpu.VMEM((8 * blocks, 128), f32),
            pltpu.VMEM((8, lanes), i32),
            pltpu.VMEM((8, 128), i32),
            pltpu.SMEM((8, 128), i32),
            pltpu.SemaphoreType.DMA,
            pltpu.SemaphoreType.DMA,
            pltpu.SemaphoreType.DMA((3,)),
            pltpu.SemaphoreType.DMA((3,)),
            pltpu.SemaphoreType.DMA((3,)),
            pltpu.SemaphoreType.DMA((3,)),
            pltpu.SemaphoreType.DMA,
            pltpu.SemaphoreType.DMA((5,)),
            pltpu.VMEM((8, 128), f32),
            pltpu.SemaphoreType.DMA((3,)),
            pltpu.SemaphoreType.DMA((3,)),
            pltpu.SemaphoreType.DMA((2 * reach,)),
            pltpu.SemaphoreType.DMA((2 * reach,)),
            pltpu.VMEM((8, 128), i32),
            pltpu.SMEM((8, 128), i32),
            pltpu.VMEM((count + blocks, 128, 128), bf16),
            pltpu.VMEM((count + blocks, 32, 256), bf16),
            pltpu.VMEM((count + blocks, 16, 128), bf16),
            pltpu.VMEM(((count + blocks) // 8, 128, 128), f32),
            pltpu.VMEM((8 * (count + blocks), 128), f32),
            pltpu.VMEM((8 * (count + blocks), 128), f32),
            pltpu.VMEM((3, 256, 128), bf16),
        ]
        + [pltpu.VMEM((128, 256), f32)] * ring
        + [pltpu.VMEM((256, 256), bf16)] * ring,
        compiler_params=pltpu.CompilerParams(
            collective_id=0, has_side_effects=True, vmem_limit_bytes=vmem_grant
        ),
        name="halo",
    )(leaving[0, 0], counts[0, 0], pairs[0, 0], mine.reshape(8 * blocks, 128))

    moved, own, sides = pl.pallas_call(
        pair_kernel,
        out_shape=(
            jax.ShapeDtypeStruct((8 * blocks, 128), f32),
            jax.ShapeDtypeStruct((4 * blocks, 128), f32),
            jax.ShapeDtypeStruct((12 * blocks, 128), f32),
        ),
        in_specs=[anywhere()] * 4,
        out_specs=(anywhere(), vmem(), vmem()),
        scratch_shapes=[
            pltpu.SMEM((4096,), i32),
            pltpu.VMEM((32 * blocks, 128), f32),
            pltpu.VMEM((16, 128), f32),
            pltpu.VMEM((3 * blocks, 128, 128), bf16),
            pltpu.VMEM((4 * blocks, 32, 256), bf16),
            pltpu.VMEM((4 * blocks, 16, 128), bf16),
            pltpu.VMEM((3 * blocks // 8, 128, 128), f32),
            pltpu.VMEM((32 * blocks, 128), f32),
            pltpu.VMEM((32 * blocks, 128), f32),
            pltpu.VMEM((3, 256, 128), bf16),
            pltpu.VMEM((32 * blocks + 8, 128), f32),
            pltpu.VMEM((16 * early_turn * blocks // 8, 128), f32),
            pltpu.SemaphoreType.DMA((5,)),
        ]
        + [pltpu.VMEM((128, 256), f32)] * ring
        + [pltpu.VMEM((256, 256), bf16)] * ring,
        compiler_params=pltpu.CompilerParams(vmem_limit_bytes=vmem_grant),
        name="contact",
    )(lists.reshape(4096), cols.reshape(32 * blocks, 128), wide, ahead_of)

    mix, fluid = pl.pallas_call(
        finish_kernel,
        out_shape=(
            jax.ShapeDtypeStruct((14 * blocks, 128), f32),
            jax.ShapeDtypeStruct((2, 256), f32),
        ),
        in_specs=[anywhere()] * 5,
        out_specs=(vmem(), vmem()),
        scratch_shapes=[
            pltpu.VMEM((8 * blocks, 128), f32),
            pltpu.VMEM((blocks, 128), i32),
            pltpu.VMEM((blocks, 128), i32),
            pltpu.VMEM((1, 256), f32),
            pltpu.SemaphoreType.DMA((4,)),
            pltpu.VMEM((16, 96), f32),
            pltpu.SemaphoreType.DMA((3,)),
            pltpu.SemaphoreType.DMA((3,)),
        ],
        compiler_params=pltpu.CompilerParams(
            collective_id=1, has_side_effects=True, vmem_limit_bytes=vmem_grant
        ),
        name="finish",
    )(moved, sides, wall_flags[0, 0], cell_index[0, 0], fluid_temp.reshape(1, 256))

    rates, fluid = pl.pallas_call(
        rates_kernel,
        out_shape=(
            jax.ShapeDtypeStruct((4 * blocks, 128), f32),
            jax.ShapeDtypeStruct((2, 256), f32),
        ),
        in_specs=[anywhere()] * 3,
        out_specs=(vmem(), vmem()),
        scratch_shapes=[
            pltpu.VMEM((4 * blocks, 128), f32),
            pltpu.VMEM((14 * blocks, 128), f32),
            pltpu.VMEM((2, 256), f32),
            pltpu.SemaphoreType.DMA((3,)),
        ],
        compiler_params=pltpu.CompilerParams(vmem_limit_bytes=vmem_grant),
        name="rates",
    )(own, mix, fluid)
    return (
        moved.reshape(1, 1, blocks, 8, 128),
        rates.reshape(1, 1, blocks, 4, 128),
        fluid[None, None],
    )


def solution(mesh):
    in_specs = (
        P("gx", "gy", None, None, None),
        P("gx", "gy", None),
        P("gx", "gy", None, None),
        P("gx", "gy", None),
        P("gx", "gy", None, None),
        P("gx", "gy", None, None),
        P("gx", "gy", None),
    )
    out_specs = (
        P("gx", "gy", None, None, None),
        P("gx", "gy", None, None, None),
        P("gx", "gy", None, None),
    )
    return jax.shard_map(shards, mesh=mesh, in_specs=in_specs, out_specs=out_specs, check_vma=False)
```
